32 devices in a mesh: smp: 4 (over y, core), gx: 4 (over z), gz: 2 (over x).
Axes of the slice: x: 2, y: 2, z: 4, core: 2. Of those that a mesh axis runs over, the one named last changes fastest.
Arguments:
- features: bfloat16 [4, 32, 20, 8, 256], P('smp', None, 'gx', None, 'gz'), may hold values from -6 to 6
- first_weight: bfloat16 [32, 3, 3, 3, 32], replicated, may hold values from -0.21875 to 0.21875
- first_bias: float32 [32], replicated, may hold values from -1 to 1
- second_weight: bfloat16 [32, 3, 3, 3, 32], replicated, may hold values from -0.21875 to 0.21875
- second_bias: float32 [32], replicated, may hold values from -1 to 1
- cotangent: bfloat16 [4, 32, 20, 8, 256], P('smp', None, 'gx', None, 'gz'), may hold values from -6 to 6
Outputs:
- output: bfloat16 [4, 32, 20, 8, 256], P('smp', None, 'gx', None, 'gz')
- first_grad: float32 [32, 3, 3, 3, 32], replicated
- first_bias_grad: float32 [32], replicated
- second_grad: float32 [32, 3, 3, 3, 32], replicated
- second_bias_grad: float32 [32], replicated
The draws below stay inside these ranges and needn't reach their ends.
All inputs are finite; a program needn't handle non-finite values.
Results may differ from the reference program's by a relative error of at most 0.011.
Values may be sent and summed in bfloat16 or wider, within the bound.
No kernel may reach another device: no remote copies, remote signals or barrier semaphores. Data moves between devices by JAX's collectives and lax.ppermute only.
A program may use at most 128 MiB of HBM per device.

```python
import math
import jax
import jax.numpy as jnp
from jax import lax

C = 32
NY = 8
SAMPLES = 4
NX = 20
NZ = 256
CELLS = 163840


def levels(key, extent, pieces, least, largest):
    def one(position, blocks):
        heights = jax.random.uniform(jax.random.fold_in(jax.random.fold_in(key, 6), position), (blocks,), jnp.float32, least / len(pieces), largest / len(pieces))
        return jnp.repeat(jnp.exp(heights), extent[position] // blocks).reshape((-1,) + (1,) * (len(extent) - position - 1))

    loudness = one(*pieces[0])
    for cut in pieces[1:]:
        loudness = loudness * one(*cut)
    return loudness


def bell_draw(own_key, dims, scale, most, cuts=(), held_as=jnp.bfloat16):
    drawn = jax.random.normal(own_key, dims, jnp.float32) * scale
    if len(cuts) > 0:
        drawn = levels(own_key, dims, cuts, -0.22, 0.18) * drawn
    return jnp.clip(drawn, min=-most, max=most).astype(held_as)


def setup_inputs(seed: int = 0) -> dict:
    seeds = jax.random.split(jax.random.key(seed), 7)
    features = bell_draw(seeds[0], (SAMPLES, C, NX, NY, NZ), 1.0, 6.0, ((0, 4), (2, 4), (4, 2)))
    first_weight = bell_draw(seeds[1], (C, 3, 3, 3, C), (27 * C) ** -0.5, 0.21875)
    first_bias = jnp.clip(jax.random.uniform(seeds[2], (C,), jnp.float32, -1.0, 1.0), -1.0, 1.0)
    second_weight = bell_draw(seeds[3], (C, 3, 3, 3, C), (27 * C) ** -0.5, 0.21875)
    second_bias = jnp.clip(jax.random.uniform(seeds[4], (C,), jnp.float32, -1.0, 1.0), -1.0, 1.0)
    cotangent = bell_draw(seeds[5], (SAMPLES, C, NX, NY, NZ), 1.0, 6.0, ((0, 4), (2, 4), (4, 2)))
    return {"features": features, "first_weight": first_weight, "first_bias": first_bias, "second_weight": second_weight, "second_bias": second_bias, "cotangent": cotangent}


def pad_field(field_in):
    wrapped = jnp.pad(field_in, ((0, 0), (0, 0), (1, 1), (0, 0), (1, 1)), mode='wrap')
    return jnp.pad(wrapped, ((0, 0), (0, 0), (0, 0), (1, 1), (0, 0))).astype(jnp.float32)

def window(padded, offset_x, offset_y, offset_z, shape):
    return padded[:, :, offset_x:offset_x + shape[2], offset_y:offset_y + shape[3], offset_z:offset_z + shape[4]]

def convolve(padded, weight, shape):
    weight_f = weight.astype(jnp.float32)
    summed = jnp.zeros((shape[0], weight.shape[0], shape[2], shape[3], shape[4]), jnp.float32)
    for offset_x in range(3):
        for offset_y in range(3):
            for offset_z in range(3):
                summed = summed + jnp.einsum('oi,sixyz->soxyz', weight_f[:, offset_x, offset_y, offset_z], window(padded, offset_x, offset_y, offset_z, shape), precision=lax.Precision.HIGHEST)
    return summed

def correlate(upstream, padded):
    shape = upstream.shape
    upstream_f = upstream.astype(jnp.float32)
    tap_terms = []
    for offset_x in range(3):
        for offset_y in range(3):
            for offset_z in range(3):
                tap_terms.append(jnp.einsum('soxyz,sixyz->oi', upstream_f, window(padded, offset_x, offset_y, offset_z, shape), precision=lax.Precision.HIGHEST))
    stacked = jnp.stack(tap_terms, axis=1)
    return stacked.reshape(shape[1], 3, 3, 3, padded.shape[1])

def reference(features, first_weight, first_bias, second_weight, second_bias, cotangent):
    grad_scale = 1.0 / math.sqrt(CELLS)
    flipped = jnp.transpose(jnp.flip(second_weight, (1, 2, 3)), (4, 1, 2, 3, 0))
    outputs = []
    first_grad = jnp.zeros(first_weight.shape, jnp.float32)
    second_grad = jnp.zeros(second_weight.shape, jnp.float32)
    first_bgrad = jnp.zeros(first_bias.shape, jnp.float32)
    second_bgrad = jnp.zeros(second_bias.shape, jnp.float32)
    for sample in range(SAMPLES):
        field_in = features[sample:sample + 1]
        shape = field_in.shape
        input_pad = pad_field(field_in)
        preact = convolve(input_pad, first_weight, shape) + first_bias[None, :, None, None, None]
        hidden = jax.nn.silu(preact).astype(jnp.bfloat16)
        hidden_pad = pad_field(hidden)
        residual_term = convolve(hidden_pad, second_weight, shape) + second_bias[None, :, None, None, None]
        outputs.append((field_in.astype(jnp.float32) + residual_term).astype(jnp.bfloat16))
        upstream = cotangent[sample:sample + 1]
        second_grad = second_grad + correlate(upstream, hidden_pad)
        second_bgrad = second_bgrad + lax.optimization_barrier(jnp.sum(upstream.astype(jnp.float32), axis=(0, 2, 3, 4)))
        hidden_grad = convolve(pad_field(upstream), flipped, shape)
        logistic = jax.nn.sigmoid(preact)
        preact_grad = (hidden_grad * logistic * (1.0 + preact * (1.0 - logistic))).astype(jnp.bfloat16)
        first_grad = first_grad + correlate(preact_grad, input_pad)
        first_bgrad = first_bgrad + lax.optimization_barrier(jnp.sum(preact_grad.astype(jnp.float32), axis=(0, 2, 3, 4)))
    return (jnp.concatenate(outputs, 0), first_grad * grad_scale, first_bgrad * grad_scale, second_grad * grad_scale, second_bgrad * grad_scale)
```

```python
import functools

import jax
import jax.numpy as jnp
from jax import lax
from jax.experimental import pallas as pl
from jax.experimental.pallas import tpu as pltpu
from jax.sharding import PartitionSpec as P

AXES = ("smp", "gx", "gz")
BF = jnp.bfloat16
F32 = jnp.float32
LANES = 128
TERMS = 896


def mm(a, b):
    return lax.dot_general(a, b, (((1,), (0,)), ((), ())), preferred_element_type=F32)


def mm_nt(a, b):
    return lax.dot_general(a, b, (((1,), (1,)), ((), ())), preferred_element_type=F32)


def iota(shape, dim):
    return lax.broadcasted_iota(jnp.int32, shape, dim)


def one_hot(hit):
    return jnp.where(hit, 1.0, 0.0).astype(BF)


def params():
    return pltpu.CompilerParams(vmem_limit_bytes=50 * 2**20)


def pack_kernel(nx, ch, ny, f_ref, g_ref, fo_ref, go_ref, up_ref, dn_ref, edge_ref, raw):
    rows = ch * ny
    r, k = iota((rows, rows), 0), iota((rows, rows), 1)
    perm = one_hot(k == (r % ch) * ny + r // ch)
    for src, dst in ((f_ref, fo_ref), (g_ref, go_ref)):
        for x in range(nx):
            block = src[0, :, x].astype(F32).reshape(rows, LANES)
            raw[:, x * LANES : (x + 1) * LANES] = block.astype(BF)
        dst[...] = mm(perm, raw[...]).astype(BF)
    last = (nx - 1) * LANES
    up_ref[0:rows] = fo_ref[:, last - LANES : last]
    up_ref[rows : 2 * rows] = fo_ref[:, last:]
    up_ref[2 * rows :] = go_ref[:, last:]
    dn_ref[0:rows] = fo_ref[:, 0:LANES]
    dn_ref[rows : 2 * rows] = fo_ref[:, LANES : 2 * LANES]
    dn_ref[2 * rows :] = go_ref[:, 0:LANES]
    n = edge_ref.shape[0]
    j, m = iota((n, nx * LANES), 0), iota((n, nx * LANES), 1)
    c, x = j // nx, j % nx
    zf = jnp.where(c < 2, c, LANES - 4 + c)
    pick_f = one_hot((c < 4) & (m == x * LANES + zf))
    zg = jnp.where(c == 4, 0, LANES - 1)
    pick_g = one_hot((c >= 4) & (c < 6) & (m == x * LANES + zg))
    edge_ref[...] = (mm_nt(pick_f, fo_ref[...]) + mm_nt(pick_g, go_ref[...])).astype(BF)


def pack(features, cotangent):
    _, ch, nx, ny, _ = features.shape
    rows = ch * ny
    edge_rows = -(-6 * nx // 32) * 32
    sds = jax.ShapeDtypeStruct
    return pl.pallas_call(
        functools.partial(pack_kernel, nx, ch, ny),
        out_shape=(
            sds((rows, nx * LANES), BF),
            sds((rows, nx * LANES), BF),
            sds((3 * rows, LANES), BF),
            sds((3 * rows, LANES), BF),
            sds((edge_rows, rows), BF),
        ),
        scratch_shapes=[pltpu.VMEM((rows, nx * LANES), BF)],
        compiler_params=params(),
        name="pack",
    )(features, cotangent)


def bands_kernel(ny, w_ref, t_ref):
    ch = w_ref.shape[2]
    rows = ny * ch
    lane = iota((ch, rows), 1)
    for kind in range(w_ref.shape[0]):
        for tap in range(9):
            a, c = tap // 3, tap % 3
            wide = jnp.concatenate([w_ref[kind, tap], jnp.zeros((ch, rows - LANES), F32)], axis=1)
            for y in range(ny):
                block = wide if y == 1 else pltpu.roll(wide, (ch * (y - 1)) % rows, 1)
                if y == 0:
                    block = jnp.where(lane >= rows - ch, 0.0, block)
                if y == ny - 1:
                    block = jnp.where(lane < ch, 0.0, block)
                t_ref[kind, a, y * ch : (y + 1) * ch, c * rows : (c + 1) * rows] = block.astype(BF)


def bands(first_weight, second_weight, ny):
    ch = first_weight.shape[0]
    rows = ch * ny
    flipped = jnp.transpose(jnp.flip(second_weight, (1, 2, 3)), (4, 1, 2, 3, 0))
    stacked = jnp.stack([first_weight, flipped, second_weight])
    laid = jnp.transpose(stacked, (0, 2, 4, 1, 3, 5)).reshape(3, 9, ch, 3 * ch).astype(F32)
    laid = jnp.pad(laid, ((0, 0), (0, 0), (0, 0), (0, LANES - 3 * ch)))
    return pl.pallas_call(
        functools.partial(bands_kernel, ny),
        out_shape=jax.ShapeDtypeStruct((3, 3, rows, 3 * rows), BF),
        compiler_params=params(),
        cost_estimate=pl.CostEstimate(flops=2_000_000_000, bytes_accessed=4_000_000, transcendentals=0),
        name="bands",
    )(laid)


def shifted_rows(out, row, block, before, after, rows):
    lane = iota(block.shape, 1)
    at = slice(row * LANES, (row + 1) * LANES)
    wide = block.astype(F32)
    out[0:rows, at] = jnp.where(lane == 0, before, pltpu.roll(wide, 1, 1)).astype(BF)
    out[rows : 2 * rows, at] = block
    out[2 * rows :, at] = jnp.where(lane == LANES - 1, after, pltpu.roll(wide, LANES - 1, 1)).astype(BF)


def lane_to(edges, source, target):
    shift = (target - source) % LANES
    return edges if shift == 0 else pltpu.roll(edges, shift, 1)


def fold_taps(product, ch, ny):
    rows = ch * ny
    lane = iota((ch, rows), 1)
    total = None
    for y in range(ny):
        block = product[y * ch : (y + 1) * ch]
        if y == 0:
            block = jnp.where(lane >= rows - ch, 0.0, block)
        if y == ny - 1:
            block = jnp.where(lane < ch, 0.0, block)
        if y != 1:
            block = pltpu.roll(block, (ch * (1 - y)) % rows, 1)
        total = block if total is None else total + block
    return total[:, :LANES]


def place_taps(columns, folded, a, c, ch):
    lane = iota(folded.shape, 1)
    for b in range(3):
        target = ch * ((a * 3 + b) * 3 + c)
        col, offset = target // LANES, target % LANES
        moved = lane_to(folded, b * ch, offset)
        columns[col] = jnp.where((lane >= offset) & (lane < offset + ch), moved, columns[col])


def bias_terms(field, ch, ny):
    nx = field.shape[1] // LANES
    wide = field.astype(F32)
    total = wide[:, 0:LANES]
    for x in range(1, nx):
        total = total + wide[:, x * LANES : (x + 1) * LANES]
    folded = total[0:ch]
    for y in range(1, ny):
        folded = folded + total[y * ch : (y + 1) * ch]
    return jnp.sum(folded, axis=1, keepdims=True)


def main_kernel(
    nx, ch, ny, right, scale,
    t_ref, f_ref, g_ref, above_ref, below_ref, edge_ref, bias_ref,
    hid_ref, hid_edge_ref, second_ref, first_ref,
    fs, gs, es, pre,
):
    rows = ch * ny
    per = edge_ref.shape[0] // (6 if right else 3)
    n_src = edge_ref.shape[0]
    j, k = iota((LANES, n_src), 0), iota((LANES, n_src), 1)
    s, xx = j // 16, j % 16
    column = jnp.where(s == 0, 2, jnp.where(s == 1, 3, jnp.where(s == 5, 0, jnp.where(s == 6, 1, jnp.where(s == 3, 5, jnp.where(s == 7, 4, -1))))))
    base = jnp.where(s >= 4, right, 0)
    row = jnp.where(xx < 2, per + nx - 2 + xx, jnp.where(xx < nx + 2, xx - 2, 2 * per + xx - nx - 2))
    place = one_hot((column >= 0) & (xx < nx + 4) & (k == base + column * nx + row))
    edges_t = mm(place, edge_ref[...])
    field = jnp.concatenate([above_ref[0:rows], above_ref[rows : 2 * rows], f_ref[...], below_ref[0:rows], below_ref[rows : 2 * rows]], axis=1)
    wide_n = (nx + 4) * LANES
    j, k = iota((LANES, wide_n), 0), iota((LANES, wide_n), 1)
    s, xx = j // 16, j % 16
    target = jnp.where(s == 2, xx * LANES, jnp.where(s == 4, xx * LANES + LANES - 1, -1))
    own = one_hot((xx < nx + 4) & (k == target))
    edges = (edges_t + mm_nt(own, field)).T

    for x in range(nx + 4):
        block = field[:, x * LANES : (x + 1) * LANES]
        shifted_rows(fs, x, block, lane_to(edges, 16 + x, 0), lane_to(edges, 80 + x, LANES - 1), rows)
    for x in range(nx + 2):
        if x == 0:
            block = above_ref[2 * rows :]
        elif x == nx + 1:
            block = below_ref[2 * rows :]
        else:
            block = g_ref[:, (x - 1) * LANES : x * LANES]
        shifted_rows(gs, x, block, lane_to(edges, 48 + x + 1, 0), lane_to(edges, 112 + x + 1, LANES - 1), rows)
    for a in range(3):
        for c in range(3):
            es[a, c * rows : (c + 1) * rows] = lane_to(edges, 16 * c + a, 0).astype(BF)

    bias = bias_ref[...]
    n7 = (nx + 2) * LANES
    acc = mm(t_ref[0, 0], fs[:, 0:n7])
    for a in range(1, 3):
        acc = acc + mm(t_ref[0, a], fs[:, a * LANES : a * LANES + n7])
    preact = acc + bias
    pre[...] = preact
    hid_ref[...] = (preact / (1.0 + jnp.exp(-preact))).astype(BF)
    acc = mm(t_ref[0, 0], es[0])
    for a in range(1, 3):
        acc = acc + mm(t_ref[0, a], es[a])
    preact = acc + bias
    hid_edge_ref[...] = (preact / (1.0 + jnp.exp(-preact))).astype(BF)

    n5 = nx * LANES
    hidden = hid_ref[:, LANES : LANES + n5]
    columns = [jnp.zeros((ch, LANES), F32) for _ in range(TERMS // LANES)]
    for a in range(3):
        for c in range(3):
            left = gs[(2 - c) * rows : (3 - c) * rows, (2 - a) * LANES : (2 - a) * LANES + n5]
            place_taps(columns, fold_taps(mm_nt(left, hidden), ch, ny), a, c, ch)
    lane = iota((ch, LANES), 1)
    spare = 27 * ch % LANES
    columns[-1] = jnp.where(lane == spare, bias_terms(g_ref[...], ch, ny), columns[-1])
    for i, part in enumerate(columns):
        second_ref[:, i * LANES : (i + 1) * LANES] = part * scale

    acc = mm(t_ref[1, 0], gs[:, 0:n5])
    for a in range(1, 3):
        acc = acc + mm(t_ref[1, a], gs[:, a * LANES : a * LANES + n5])
    preact = pre[:, LANES : LANES + n5]
    logistic = 1.0 / (1.0 + jnp.exp(-preact))
    preact_grad = (acc * logistic * (1.0 + preact * (1.0 - logistic))).astype(BF)

    columns = [jnp.zeros((ch, LANES), F32) for _ in range(TERMS // LANES)]
    for a in range(3):
        for c in range(3):
            taps = fs[c * rows : (c + 1) * rows, (a + 1) * LANES : (a + 1) * LANES + n5]
            place_taps(columns, fold_taps(mm_nt(preact_grad, taps), ch, ny), a, c, ch)
    columns[-1] = jnp.where(lane == spare, bias_terms(preact_grad, ch, ny), columns[-1])
    for i, part in enumerate(columns):
        first_ref[:, i * LANES : (i + 1) * LANES] = part * scale


def main(taps, field, cot, above, below, edge, right, bias, ch, ny, scale):
    rows = ch * ny
    nx = field.shape[1] // LANES
    sds = jax.ShapeDtypeStruct
    return pl.pallas_call(
        functools.partial(main_kernel, nx, ch, ny, right, scale),
        out_shape=(
            sds((rows, (nx + 2) * LANES), BF),
            sds((rows, LANES), BF),
            sds((ch, TERMS), F32),
            sds((ch, TERMS), F32),
        ),
        scratch_shapes=[
            pltpu.VMEM((3 * rows, (nx + 4) * LANES), BF),
            pltpu.VMEM((3 * rows, (nx + 2) * LANES), BF),
            pltpu.VMEM((3, 3 * rows, LANES), BF),
            pltpu.VMEM((rows, (nx + 2) * LANES), F32),
        ],
        compiler_params=params(),
        name="main",
    )(taps, field, cot, above, below, edge, bias)


def output_kernel(nx, ch, ny, t_ref, h_ref, e_ref, f_ref, bias_ref, o_ref, hs):
    rows = ch * ny
    edges = e_ref[...].astype(F32)
    for x in range(nx + 2):
        block = h_ref[:, x * LANES : (x + 1) * LANES]
        shifted_rows(hs, x, block, lane_to(edges, x, 0), lane_to(edges, 64 + x, LANES - 1), rows)
    n5 = nx * LANES
    acc = mm(t_ref[2, 0], hs[:, 0:n5])
    for a in range(1, 3):
        acc = acc + mm(t_ref[2, a], hs[:, a * LANES : a * LANES + n5])
    total = (f_ref[...].astype(F32) + (acc + bias_ref[...])).astype(BF)
    r, k = iota((rows, rows), 0), iota((rows, rows), 1)
    back = one_hot(k == (r % ny) * ch + r // ny)
    ordered = mm(back, total)
    for x in range(nx):
        o_ref[0, :, x] = ordered[:, x * LANES : (x + 1) * LANES].reshape(ch, ny, LANES).astype(BF)


def residual(taps, hidden, hidden_edge, field, bias, ch, ny):
    rows = ch * ny
    nx = field.shape[1] // LANES
    return pl.pallas_call(
        functools.partial(output_kernel, nx, ch, ny),
        out_shape=jax.ShapeDtypeStruct((1, ch, nx, ny, LANES), BF),
        scratch_shapes=[pltpu.VMEM((3 * rows, (nx + 2) * LANES), BF)],
        compiler_params=params(),
        cost_estimate=pl.CostEstimate(flops=3_000_000_000, bytes_accessed=3_000_000, transcendentals=0),
        name="residual",
    )(taps, hidden, hidden_edge, field, bias)


def moved(array, sizes, step):
    ns, nx, nz = sizes
    pairs = []
    for s in range(ns):
        for x in range(nx):
            for z in range(nz):
                t, u, v = step(s, x, z)
                pairs.append(((s * nx + x) * nz + z, (t * nx + u) * nz + v))
    return lax.ppermute(array, AXES, pairs)


def around(array, sizes, dx, dz):
    ns, nx, nz = sizes
    return moved(array, sizes, lambda s, x, z: (s, (x + dx) % nx, (z + dz) % nz))


def swapped(array, sizes, bits):
    return moved(array, sizes, lambda s, x, z: (s ^ bits[0], x ^ bits[1], z ^ bits[2]))


def pair_sums(terms):
    while len(terms) > 1:
        terms = [terms[i] + terms[i + 1] for i in range(0, len(terms), 2)]
    return terms[0]


def sum_over(array, sizes, pair):
    steps = [(0, 0, 0)]
    for bits in pair:
        steps = steps + [tuple(p ^ q for p, q in zip(bits, step)) for step in steps]
    sent = array.astype(BF)
    terms = [sent] + [swapped(sent, sizes, step) for step in steps[1:]]
    return pair_sums([term.astype(F32) for term in terms])


def sum_all(second, first, sizes):
    if any(n & (n - 1) for n in sizes) or sizes[0] == 1:
        return lax.psum((second, first), AXES)
    even = lax.axis_index("smp") % 2 == 0
    near = (1, 0, 0)
    mine = jnp.where(even, second, first) + swapped(jnp.where(even, first, second), sizes, near)
    bits = [(1 << i, 0, 0) for i in range(1, sizes[0].bit_length() - 1)]
    bits += [(0, 0, 1 << i) for i in range(sizes[2].bit_length() - 1)]
    bits += [(0, 1 << i, 0) for i in range(sizes[1].bit_length() - 1)]
    for i in range(0, len(bits), 2):
        mine = sum_over(mine, sizes, bits[i : i + 2])
    other = swapped(mine, sizes, near)
    return jnp.where(even, mine, other), jnp.where(even, other, mine)


def shards(sizes, features, first_weight, first_bias, second_weight, second_bias, cotangent):
    ns, ngx, ngz = sizes
    _, ch, nx, ny, nz = features.shape
    assert features.shape[0] == 1 and nz == LANES
    scale = float((ns * nx * ngx * ny * nz * ngz) ** -0.5)
    field, cot, up, down, edge = pack(features, cotangent)
    above = around(up, sizes, 1, 0)
    below = around(down, sizes, -1, 0)
    sides = [[around(edge, sizes, dx, 1) for dx in (0, 1, -1)]]
    if ngz != 2:
        sides.append([around(edge, sizes, dx, -1) for dx in (0, 1, -1)])
    taps = bands(first_weight, second_weight, ny)
    edges = jnp.concatenate([part for side in sides for part in side], axis=0)
    right = edges.shape[0] // 2 if ngz != 2 else 0
    column = lambda bias: jnp.tile(bias, ny)[:, None]
    hidden, hidden_edge, second, first = main(
        taps, field, cot, above, below, edges, right, column(first_bias), ch, ny, scale
    )
    output = residual(taps, hidden, hidden_edge, field, column(second_bias), ch, ny)
    second, first = sum_all(second, first, sizes)
    spread = lambda terms: (terms[:, : 27 * ch].reshape(ch, 3, 3, 3, ch), terms[:, 27 * ch])
    first_grad, first_bgrad = spread(first)
    second_grad, second_bgrad = spread(second)
    return output, first_grad, first_bgrad, second_grad, second_bgrad


def solution(mesh):
    sizes = tuple(mesh.shape[axis] for axis in AXES)
    split = P("smp", None, "gx", None, "gz")
    return jax.shard_map(
        functools.partial(shards, sizes),
        mesh=mesh,
        in_specs=(split, P(), P(), P(), P(), split),
        out_specs=(split, P(), P(), P(), P()),
        check_vma=False,
    )
```

```python
import functools

import jax
import jax.numpy as jnp
from jax import lax
from jax.experimental import pallas as pl
from jax.experimental.pallas import tpu as pltpu
from jax.sharding import PartitionSpec as P

AXES = ("smp", "gx", "gz")
BF = jnp.bfloat16
F32 = jnp.float32
LANES = 128
TERMS = 896


def mm(a, b):
    return lax.dot_general(a, b, (((1,), (0,)), ((), ())), preferred_element_type=F32)


def mm_nt(a, b):
    return lax.dot_general(a, b, (((1,), (1,)), ((), ())), preferred_element_type=F32)


def iota(shape, dim):
    return lax.broadcasted_iota(jnp.int32, shape, dim)


def one_hot(hit):
    return jnp.where(hit, 1.0, 0.0).astype(BF)


def params():
    return pltpu.CompilerParams(vmem_limit_bytes=20 * 2**20)


def is_even(axis):
    return lax.axis_index(axis) % 2 == 0


def pack_kernel(
    nx, ch, ny, f_any, g_any, fo_ref, go_ref, one_ref, two_ref, far_one_ref, far_two_ref, edge_ref, held, raw, sems
):
    rows = ch * ny
    part = ch // 4
    copies = []
    for i, src in enumerate((f_any, g_any)):
        for q in range(4):
            at = pl.ds(q * part, part)
            copies.append(pltpu.make_async_copy(src.at[0, at], held.at[i, at], sems.at[i * 4 + q]))
    for copy in copies:
        copy.start()
    r, k = iota((rows, rows), 0), iota((rows, rows), 1)
    perm = one_hot(k == (r % ch) * ny + r // ch)
    for i, dst in enumerate((fo_ref, go_ref)):
        for copy in copies[i * 4 : i * 4 + 4]:
            copy.wait()
        for x in range(nx):
            block = held[i, :, x].astype(F32).reshape(rows, LANES)
            raw[:, x * LANES : (x + 1) * LANES] = block.astype(BF)
        dst[...] = mm(perm, raw[...]).astype(BF)
    even = is_even("gx")
    last = (nx - 1) * LANES
    for i, src in enumerate((fo_ref, go_ref)):
        up, down = src[:, last:], src[:, 0:LANES]
        one_ref[i * rows : (i + 1) * rows] = jnp.where(even, up, down)
        two_ref[i * rows : (i + 1) * rows] = jnp.where(even, down, up)
    up, down = fo_ref[:, last - LANES : last], fo_ref[:, LANES : 2 * LANES]
    far_one_ref[...] = jnp.where(even, up, down)
    far_two_ref[...] = jnp.where(even, down, up)
    n = edge_ref.shape[0]
    j, m = iota((n, nx * LANES), 0), iota((n, nx * LANES), 1)
    c, x = j // nx, j % nx
    zf = jnp.where(c < 2, c, LANES - 4 + c)
    pick_f = one_hot((c < 4) & (m == x * LANES + zf))
    zg = jnp.where(c == 4, 0, LANES - 1)
    pick_g = one_hot((c >= 4) & (c < 6) & (m == x * LANES + zg))
    edge_ref[...] = (mm_nt(pick_f, fo_ref[...]) + mm_nt(pick_g, go_ref[...])).astype(BF)


def pack(features, cotangent):
    _, ch, nx, ny, _ = features.shape
    rows = ch * ny
    edge_rows = -(-6 * nx // 32) * 32
    sds = jax.ShapeDtypeStruct
    anywhere = pl.BlockSpec(memory_space=pl.ANY)
    return pl.pallas_call(
        functools.partial(pack_kernel, nx, ch, ny),
        out_shape=(
            sds((rows, nx * LANES), BF),
            sds((rows, nx * LANES), BF),
            sds((2 * rows, LANES), BF),
            sds((2 * rows, LANES), BF),
            sds((rows, LANES), BF),
            sds((rows, LANES), BF),
            sds((edge_rows, rows), BF),
        ),
        in_specs=[anywhere, anywhere],
        scratch_shapes=[
            pltpu.VMEM((2, ch, nx, ny, LANES), BF),
            pltpu.VMEM((rows, nx * LANES), BF),
            pltpu.SemaphoreType.DMA((8,)),
        ],
        compiler_params=params(),
        name="pack",
    )(features, cotangent)


def bands_kernel(ny, w1_ref, w2_ref, t1_ref, tv_ref, t2_ref):
    ch = w1_ref.shape[-1]
    rows = ny * ch
    lane = iota((ch, rows), 1)
    r, k = iota((ch, ch), 0), iota((ch, ch), 1)
    turned = mm_nt(one_hot(r == k), w2_ref[...].reshape(27 * ch, ch))
    rest = jnp.zeros((ch, rows - 3 * ch), F32)

    def flipped(a, b, c):
        at = ch * ((2 - a) * 9 + (2 - b) * 3 + (2 - c))
        return turned[:, at : at + ch]

    first = lambda a, b, c: w1_ref[a, b, c].astype(F32)
    second = lambda a, b, c: w2_ref[a, b, c].astype(F32)
    for tap, out in ((first, t1_ref), (flipped, tv_ref), (second, t2_ref)):
        for a in range(3):
            for c in range(3):
                wide = jnp.concatenate([tap(a, 0, c), tap(a, 1, c), tap(a, 2, c), rest], axis=1)
                for y in range(ny):
                    block = wide if y == 1 else pltpu.roll(wide, (ch * (y - 1)) % rows, 1)
                    if y == 0:
                        block = jnp.where(lane >= rows - ch, 0.0, block)
                    if y == ny - 1:
                        block = jnp.where(lane < ch, 0.0, block)
                    out[a, y * ch : (y + 1) * ch, c * rows : (c + 1) * rows] = block.astype(BF)


def bands(first_weight, second_weight, ny):
    ch = first_weight.shape[0]
    rows = ch * ny
    laid = lambda weight: jnp.transpose(weight, (1, 2, 3, 0, 4))
    return pl.pallas_call(
        functools.partial(bands_kernel, ny),
        out_shape=(jax.ShapeDtypeStruct((3, rows, 3 * rows), BF),) * 3,
        compiler_params=params(),
        cost_estimate=pl.CostEstimate(flops=1_000_000_000, bytes_accessed=4_000_000, transcendentals=0),
        name="bands",
    )(laid(first_weight), laid(second_weight))


def shifted_rows(out, row, block, before, after, rows):
    lane = iota(block.shape, 1)
    at = slice(row * LANES, (row + 1) * LANES)
    wide = block.astype(F32)
    out[0:rows, at] = jnp.where(lane == 0, before, pltpu.roll(wide, 1, 1)).astype(BF)
    out[rows : 2 * rows, at] = block
    out[2 * rows :, at] = jnp.where(lane == LANES - 1, after, pltpu.roll(wide, LANES - 1, 1)).astype(BF)


def lane_to(edges, source, target):
    shift = (target - source) % LANES
    return edges if shift == 0 else pltpu.roll(edges, shift, 1)


def fold_taps(product, ch, ny):
    rows = ch * ny
    lane = iota((ch, rows), 1)
    total = None
    for y in range(ny):
        block = product[y * ch : (y + 1) * ch]
        if y == 0:
            block = jnp.where(lane >= rows - ch, 0.0, block)
        if y == ny - 1:
            block = jnp.where(lane < ch, 0.0, block)
        if y != 1:
            block = pltpu.roll(block, (ch * (1 - y)) % rows, 1)
        total = block if total is None else total + block
    return total[:, :LANES]


def place_taps(columns, folded, a, c, ch):
    lane = iota(folded.shape, 1)
    for b in range(3):
        target = ch * ((a * 3 + b) * 3 + c)
        col, offset = target // LANES, target % LANES
        moved = lane_to(folded, b * ch, offset)
        columns[col] = jnp.where((lane >= offset) & (lane < offset + ch), moved, columns[col])


def bias_terms(field, ch, ny):
    nx = field.shape[1] // LANES
    wide = field.astype(F32)
    total = wide[:, 0:LANES]
    for x in range(1, nx):
        total = total + wide[:, x * LANES : (x + 1) * LANES]
    folded = total[0:ch]
    for y in range(1, ny):
        folded = folded + total[y * ch : (y + 1) * ch]
    return jnp.sum(folded, axis=1, keepdims=True)


def silu(preact):
    return (preact / (1.0 + jnp.exp(-preact))).astype(BF)


def sides(even, one, two):
    return jnp.where(even, two, one), jnp.where(even, one, two)


def edge_columns(nx, even, near_ref, one_ref, two_ref):
    n = near_ref.shape[0]
    j, k = iota((LANES, n), 0), iota((LANES, n), 1)
    s, xx = j // 16, j % 16
    column = jnp.where(s == 0, 2, jnp.where(s == 1, 3, jnp.where(s == 5, 0, jnp.where(s == 6, 1, jnp.where(s == 3, 5, jnp.where(s == 7, 4, -1))))))
    first = column * nx
    hit = lambda low, high, offset: one_hot((column >= 0) & (xx >= low) & (xx < high) & (k == first + xx - low + offset))
    before, after = sides(even, one_ref[...], two_ref[...])
    out = mm(hit(2, nx + 2, 0), near_ref[...])
    out = out + mm(hit(0, 2, nx - 2), before)
    return out + mm(hit(nx + 2, nx + 4, 0), after)


def main_kernel(
    nx, ch, ny, scale,
    t1_ref, tv_ref, f_ref, g_ref, one_ref, two_ref, near_ref, edge_one_ref, edge_two_ref, bias_ref,
    hid_ref, fs, keep_ref, give_ref,
    gs, pre,
):
    rows = ch * ny
    even = is_even("gx")
    edges = edge_columns(nx, even, near_ref, edge_one_ref, edge_two_ref).T
    for i, (src, dst, left, right) in enumerate(((f_ref, fs, 16, 80), (g_ref, gs, 48, 112))):
        above, below = sides(even, one_ref[i * rows : (i + 1) * rows], two_ref[i * rows : (i + 1) * rows])
        for x in range(nx + 2):
            if x == 0:
                block = above
            elif x == nx + 1:
                block = below
            else:
                block = src[:, (x - 1) * LANES : x * LANES]
            shifted_rows(dst, x, block, lane_to(edges, left + x + 1, 0), lane_to(edges, right + x + 1, LANES - 1), rows)

    n5 = nx * LANES
    acc = mm(t1_ref[0], fs[:, 0:n5])
    for a in range(1, 3):
        acc = acc + mm(t1_ref[a], fs[:, a * LANES : a * LANES + n5])
    preact = acc + bias_ref[...]
    pre[...] = preact
    hid_ref[...] = silu(preact)
    hidden = hid_ref[...]

    lane = iota((ch, LANES), 1)
    spare = 27 * ch % LANES
    mine = is_even("smp")
    columns = [jnp.zeros((ch, LANES), F32) for _ in range(TERMS // LANES)]
    for a in range(3):
        for c in range(3):
            left = gs[(2 - c) * rows : (3 - c) * rows, (2 - a) * LANES : (2 - a) * LANES + n5]
            place_taps(columns, fold_taps(mm_nt(left, hidden), ch, ny), a, c, ch)
    columns[-1] = jnp.where(lane == spare, bias_terms(g_ref[...], ch, ny), columns[-1])
    second = [part * scale for part in columns]

    acc = mm(tv_ref[0], gs[:, 0:n5])
    for a in range(1, 3):
        acc = acc + mm(tv_ref[a], gs[:, a * LANES : a * LANES + n5])
    preact = pre[...]
    logistic = 1.0 / (1.0 + jnp.exp(-preact))
    preact_grad = (acc * logistic * (1.0 + preact * (1.0 - logistic))).astype(BF)

    columns = [jnp.zeros((ch, LANES), F32) for _ in range(TERMS // LANES)]
    for a in range(3):
        for c in range(3):
            taps = fs[c * rows : (c + 1) * rows, a * LANES : a * LANES + n5]
            place_taps(columns, fold_taps(mm_nt(preact_grad, taps), ch, ny), a, c, ch)
    columns[-1] = jnp.where(lane == spare, bias_terms(preact_grad, ch, ny), columns[-1])
    first = [part * scale for part in columns]
    for i in range(TERMS // LANES):
        at = slice(i * LANES, (i + 1) * LANES)
        keep_ref[:, at] = jnp.where(mine, second[i], first[i])
        give_ref[:, at] = jnp.where(mine, first[i], second[i])


def main(t1, tv, field, cot, one, two, near, edge_one, edge_two, bias, ch, ny, scale):
    rows = ch * ny
    nx = field.shape[1] // LANES
    sds = jax.ShapeDtypeStruct
    return pl.pallas_call(
        functools.partial(main_kernel, nx, ch, ny, scale),
        out_shape=(
            sds((rows, nx * LANES), BF),
            sds((3 * rows, (nx + 2) * LANES), BF),
            sds((ch, TERMS), F32),
            sds((ch, TERMS), F32),
        ),
        scratch_shapes=[
            pltpu.VMEM((3 * rows, (nx + 2) * LANES), BF),
            pltpu.VMEM((rows, nx * LANES), F32),
        ],
        compiler_params=params(),
        name="main",
    )(t1, tv, field, cot, one, two, near, edge_one, edge_two, bias)


def residual_kernel(
    nx, ch, ny,
    t1_ref, t2_ref, h_ref, fs_ref, f_ref, far_one_ref, far_two_ref, near_ref, edge_one_ref, edge_two_ref, bias1_ref, bias2_ref,
    o_ref,
    ends, hs,
):
    rows = ch * ny
    even = is_even("gx")
    above, below = sides(even, far_one_ref[...], far_two_ref[...])
    middle = fs_ref[rows : 2 * rows]
    edges_t = edge_columns(nx, even, near_ref, edge_one_ref, edge_two_ref)
    j, k = iota((LANES, LANES), 0), iota((LANES, LANES), 1)
    own_end = jnp.where(j // 16 == 2, 0, jnp.where(j // 16 == 4, LANES - 1, -1))
    for x in range(nx + 4):
        block = above if x == 0 else below if x == nx + 3 else middle[:, (x - 1) * LANES : x * LANES]
        edges_t = edges_t + mm_nt(one_hot((j % 16 == x) & (k == own_end)), block)
    edges = edges_t.T
    shifted_rows(ends, 0, above, lane_to(edges, 16, 0), lane_to(edges, 80, LANES - 1), rows)
    shifted_rows(ends, 1, below, lane_to(edges, 16 + nx + 3, 0), lane_to(edges, 80 + nx + 3, LANES - 1), rows)
    acc = None
    row = lambda x: fs_ref[:, (x + 1) * LANES : (x + 2) * LANES]
    pairs = ((ends[:, 0:LANES], row(nx - 1)), (row(-1), row(nx)), (row(0), ends[:, LANES:]))
    for a in range(3):
        columns = [lane_to(edges, 16 * c + a, 0).astype(BF) for c in range(3)]
        term = mm(t1_ref[a], jnp.concatenate([*pairs[a], jnp.concatenate(columns, axis=0)], axis=1))
        acc = term if acc is None else acc + term
    hidden = silu(acc + bias1_ref[...])
    outer = hidden[:, 2 * LANES :].astype(F32)
    for x in range(nx + 2):
        if x == 0:
            block = hidden[:, 0:LANES]
        elif x == nx + 1:
            block = hidden[:, LANES : 2 * LANES]
        else:
            block = h_ref[:, (x - 1) * LANES : x * LANES]
        shifted_rows(hs, x, block, lane_to(outer, x, 0), lane_to(outer, 64 + x, LANES - 1), rows)
    n5 = nx * LANES
    acc = mm(t2_ref[0], hs[:, 0:n5])
    for a in range(1, 3):
        acc = acc + mm(t2_ref[a], hs[:, a * LANES : a * LANES + n5])
    total = (f_ref[...].astype(F32) + (acc + bias2_ref[...])).astype(BF)
    r, k = iota((rows, rows), 0), iota((rows, rows), 1)
    back = one_hot(k == (r % ny) * ch + r // ny)
    ordered = mm(back, total)
    for x in range(nx):
        o_ref[0, :, x] = ordered[:, x * LANES : (x + 1) * LANES].reshape(ch, ny, LANES).astype(BF)


def residual(t1, t2, hidden, fs, field, far_one, far_two, near, edge_one, edge_two, bias1, bias2, ch, ny):
    rows = ch * ny
    nx = field.shape[1] // LANES
    return pl.pallas_call(
        functools.partial(residual_kernel, nx, ch, ny),
        out_shape=jax.ShapeDtypeStruct((1, ch, nx, ny, LANES), BF),
        scratch_shapes=[pltpu.VMEM((3 * rows, 2 * LANES), BF), pltpu.VMEM((3 * rows, (nx + 2) * LANES), BF)],
        compiler_params=params(),
        cost_estimate=pl.CostEstimate(flops=3_000_000_000, bytes_accessed=3_000_000, transcendentals=0),
        name="residual",
    )(t1, t2, hidden, fs, field, far_one, far_two, near, edge_one, edge_two, bias1, bias2)


def moved(array, sizes, step):
    ns, nx, nz = sizes
    pairs = []
    for s in range(ns):
        for x in range(nx):
            for z in range(nz):
                t, u, v = step(s, x, z)
                pairs.append(((s * nx + x) * nz + z, (t * nx + u) * nz + v))
    return lax.ppermute(array, AXES, pairs)


def paired(array, sizes, turn, dz):
    ns, nx, nz = sizes
    return moved(array, sizes, lambda s, x, z: (s, (x + (1 if x % 2 == turn else -1)) % nx, (z + dz) % nz))


def swapped(array, sizes, bits):
    return moved(array, sizes, lambda s, x, z: (s ^ bits[0], x ^ bits[1], z ^ bits[2]))


def add_kernel(n_in, *refs):
    terms = [ref[...].astype(F32) for ref in refs[:n_in]]
    out = refs[n_in]
    while len(terms) > 1:
        terms = [terms[i] + terms[i + 1] for i in range(0, len(terms), 2)]
    total = terms[0]
    n = total.shape[1] - LANES
    out[:, :n] = total[:, :n].astype(out.dtype)
    tail = total[:, n:]
    lane = iota(tail.shape, 1)
    spare = 864 % LANES
    joined = tail + pltpu.roll(tail, LANES - 1, 1)
    if out.dtype == BF:
        low = joined - joined.astype(BF).astype(F32)
        tail = jnp.where(lane == spare + 1, pltpu.roll(low, 1, 1), tail)
    out[:, n:] = jnp.where(lane == spare, joined, tail).astype(out.dtype)


def add(terms, dtype):
    return pl.pallas_call(
        functools.partial(add_kernel, len(terms)),
        out_shape=jax.ShapeDtypeStruct(terms[0].shape, dtype),
        compiler_params=params(),
        name="add",
    )(*terms)


def exchange(sent, sizes, pair):
    steps = [(0, 0, 0)]
    for bits in pair:
        steps = steps + [tuple(p ^ q for p, q in zip(bits, step)) for step in steps]
    return [sent] + [swapped(sent, sizes, step) for step in steps[1:]]


def sum_all(keep, give, sizes, output):
    near = (1, 0, 0)
    bits = [(1 << i, 0, 0) for i in range(1, sizes[0].bit_length() - 1)]
    bits += [(0, 0, 1 << i) for i in range(sizes[2].bit_length() - 1)]
    bits += [(0, 1 << i, 0) for i in range(sizes[1].bit_length() - 1)]
    terms = [keep, swapped(give, sizes, near)]
    for i in range(0, len(bits), 2):
        terms = exchange(add(terms, BF), sizes, bits[i : i + 2])
        if i == 0:
            *terms, output = lax.optimization_barrier((*terms, output))
    mine = add(terms, F32)
    return mine, swapped(mine, sizes, near), output


def spread_kernel(ch, mine_ref, other_ref, first_ref, first_bias_ref, second_ref, second_bias_ref):
    even = is_even("smp")
    mine, other = mine_ref[...], other_ref[...]
    r, k = iota((ch, LANES), 0), iota((ch, LANES), 1)
    for terms, out, bias in (
        (jnp.where(even, other, mine), first_ref, first_bias_ref),
        (jnp.where(even, mine, other), second_ref, second_bias_ref),
    ):
        for tap in range(27):
            at = tap * ch
            block = terms[:, at // LANES * LANES : (at // LANES + 1) * LANES]
            out[tap // 9, tap // 3 % 3, tap % 3] = lane_to(block, at % LANES, 0)[:, :ch]
        tail = lane_to(terms[:, TERMS - LANES :], 27 * ch % LANES, 0)[:, 0:1]
        bias[...] = jnp.sum(jnp.where(r == k, tail, 0.0), axis=0, keepdims=True)[:, :ch]


def spread(mine, other, ch):
    sds = jax.ShapeDtypeStruct
    taps, bias = sds((3, 3, 3, ch, ch), F32), sds((1, ch), F32)
    first, first_bias, second, second_bias = pl.pallas_call(
        functools.partial(spread_kernel, ch),
        out_shape=(taps, bias, taps, bias),
        compiler_params=params(),
        name="spread",
    )(mine, other)
    laid = lambda grad: jnp.transpose(grad, (3, 0, 1, 2, 4))
    return laid(first), first_bias.reshape(ch), laid(second), second_bias.reshape(ch)


def shards(sizes, features, first_weight, first_bias, second_weight, second_bias, cotangent):
    ns, ngx, ngz = sizes
    _, ch, nx, ny, nz = features.shape
    assert features.shape[0] == 1 and nz == LANES and ngz == 2 and ngx % 2 == 0
    assert not any(n & (n - 1) for n in sizes) and ns > 1
    scale = float((ns * nx * ngx * ny * nz * ngz) ** -0.5)
    field, cot, one, two, far_one, far_two, edge = pack(features, cotangent)
    one, two = paired(one, sizes, 0, 0), paired(two, sizes, 1, 0)
    near = swapped(edge, sizes, (0, 0, 1))
    edge_one, edge_two = paired(edge, sizes, 0, 1), paired(edge, sizes, 1, 1)
    far_one, far_two = paired(far_one, sizes, 0, 0), paired(far_two, sizes, 1, 0)
    t1, tv, t2 = bands(first_weight, second_weight, ny)
    column = lambda bias: jnp.tile(bias, ny)[:, None]
    bias1, bias2 = column(first_bias), column(second_bias)
    hidden, fs, keep, give = main(t1, tv, field, cot, one, two, near, edge_one, edge_two, bias1, ch, ny, scale)
    output = residual(t1, t2, hidden, fs, field, far_one, far_two, near, edge_one, edge_two, bias1, bias2, ch, ny)
    mine, other, output = sum_all(keep, give, sizes, output)
    return output, *spread(mine, other, ch)


def solution(mesh):
    sizes = tuple(mesh.shape[axis] for axis in AXES)
    split = P("smp", None, "gx", None, "gz")
    return jax.shard_map(
        functools.partial(shards, sizes),
        mesh=mesh,
        in_specs=(split, P(), P(), P(), P(), split),
        out_specs=(split, P(), P(), P(), P()),
        check_vma=False,
    )
```

```python
import functools

import jax
import jax.numpy as jnp
from jax import lax
from jax.experimental import pallas as pl
from jax.experimental.pallas import tpu as pltpu
from jax.sharding import PartitionSpec as P

AXES = ("smp", "gx", "gz")
BF = jnp.bfloat16
F32 = jnp.float32
LANES = 128
TERMS = 896


def mm(a, b):
    return lax.dot_general(a, b, (((1,), (0,)), ((), ())), preferred_element_type=F32)


def mm_nt(a, b):
    return lax.dot_general(a, b, (((1,), (1,)), ((), ())), preferred_element_type=F32)


def iota(shape, dim):
    return lax.broadcasted_iota(jnp.int32, shape, dim)


def one_hot(hit):
    return jnp.where(hit, 1.0, 0.0).astype(BF)


def params(mib=8):
    return pltpu.CompilerParams(vmem_limit_bytes=mib * 2**20)


def in_vmem(*arrays):
    return [pltpu.with_memory_space_constraint(array, pltpu.VMEM) for array in arrays]


def in_hbm(*arrays):
    return [pltpu.with_memory_space_constraint(array, pltpu.HBM) for array in arrays]


def is_even(axis):
    return lax.axis_index(axis) % 2 == 0


def pack_kernel(
    nx, ch, ny, f_any, g_any, fo_ref, go_ref, one_ref, two_ref, far_one_ref, far_two_ref, edge_ref, held, raw, sems
):
    rows = ch * ny
    part = ch // 4
    copies = []
    for i, src in enumerate((f_any, g_any)):
        for q in range(4):
            at = pl.ds(q * part, part)
            copies.append(pltpu.make_async_copy(src.at[0, at], held.at[i, at], sems.at[i * 4 + q]))
    for copy in copies:
        copy.start()
    r, k = iota((rows, rows), 0), iota((rows, rows), 1)
    perm = one_hot(k == (r % ch) * ny + r // ch)
    for i, dst in enumerate((fo_ref, go_ref)):
        for copy in copies[i * 4 : i * 4 + 4]:
            copy.wait()
        for x in range(nx):
            block = held[i, :, x].astype(F32).reshape(rows, LANES)
            raw[:, x * LANES : (x + 1) * LANES] = block.astype(BF)
        dst[...] = mm(perm, raw[...]).astype(BF)
    even = is_even("gx")
    last = (nx - 1) * LANES
    for i, src in enumerate((fo_ref, go_ref)):
        up, down = src[:, last:], src[:, 0:LANES]
        one_ref[i * rows : (i + 1) * rows] = jnp.where(even, up, down)
        two_ref[i * rows : (i + 1) * rows] = jnp.where(even, down, up)
    up, down = fo_ref[:, last - LANES : last], fo_ref[:, LANES : 2 * LANES]
    far_one_ref[...] = jnp.where(even, up, down)
    far_two_ref[...] = jnp.where(even, down, up)
    n = edge_ref.shape[0]
    j, m = iota((n, nx * LANES), 0), iota((n, nx * LANES), 1)
    c, x = j // nx, j % nx
    zf = jnp.where(c < 2, c, LANES - 4 + c)
    pick_f = one_hot((c < 4) & (m == x * LANES + zf))
    zg = jnp.where(c == 4, 0, LANES - 1)
    pick_g = one_hot((c >= 4) & (c < 6) & (m == x * LANES + zg))
    edge_ref[...] = (mm_nt(pick_f, fo_ref[...]) + mm_nt(pick_g, go_ref[...])).astype(BF)


def pack(features, cotangent):
    _, ch, nx, ny, _ = features.shape
    rows = ch * ny
    edge_rows = -(-6 * nx // 32) * 32
    sds = pltpu.VMEM
    anywhere = pl.BlockSpec(memory_space=pl.ANY)
    return pl.pallas_call(
        functools.partial(pack_kernel, nx, ch, ny),
        out_shape=(
            sds((rows, nx * LANES), BF),
            sds((rows, nx * LANES), BF),
            sds((2 * rows, LANES), BF),
            sds((2 * rows, LANES), BF),
            sds((rows, LANES), BF),
            sds((rows, LANES), BF),
            sds((edge_rows, rows), BF),
        ),
        in_specs=[anywhere, anywhere],
        scratch_shapes=[
            pltpu.VMEM((2, ch, nx, ny, LANES), BF),
            pltpu.VMEM((rows, nx * LANES), BF),
            pltpu.SemaphoreType.DMA((8,)),
        ],
        compiler_params=params(4),
        name="pack",
    )(*in_hbm(features, cotangent))


def bands_kernel(ny, w1_any, w2_any, t1_ref, tv_ref, t2_ref, held, sems):
    copies = [pltpu.make_async_copy(src, held.at[i], sems.at[i]) for i, src in enumerate((w1_any, w2_any))]
    for copy in copies:
        copy.start()
    for copy in copies:
        copy.wait()
    w1_ref, w2_ref = held.at[0], held.at[1]
    ch = w1_ref.shape[-1]
    rows = ny * ch
    lane = iota((ch, rows), 1)
    r, k = iota((ch, ch), 0), iota((ch, ch), 1)
    turned = mm_nt(one_hot(r == k), w2_ref[...].reshape(27 * ch, ch))
    rest = jnp.zeros((ch, rows - 3 * ch), F32)

    def flipped(a, b, c):
        at = ch * ((2 - a) * 9 + (2 - b) * 3 + (2 - c))
        return turned[:, at : at + ch]

    first = lambda a, b, c: w1_ref[a, b, c].astype(F32)
    second = lambda a, b, c: w2_ref[a, b, c].astype(F32)
    for tap, out in ((first, t1_ref), (flipped, tv_ref), (second, t2_ref)):
        for a in range(3):
            for c in range(3):
                wide = jnp.concatenate([tap(a, 0, c), tap(a, 1, c), tap(a, 2, c), rest], axis=1)
                for y in range(ny):
                    block = wide if y == 1 else pltpu.roll(wide, (ch * (y - 1)) % rows, 1)
                    if y == 0:
                        block = jnp.where(lane >= rows - ch, 0.0, block)
                    if y == ny - 1:
                        block = jnp.where(lane < ch, 0.0, block)
                    out[a, y * ch : (y + 1) * ch, c * rows : (c + 1) * rows] = block.astype(BF)


def bands(first_weight, second_weight, ny):
    ch = first_weight.shape[0]
    rows = ch * ny
    laid = lambda weight: jnp.transpose(weight, (1, 2, 3, 0, 4))
    return pl.pallas_call(
        functools.partial(bands_kernel, ny),
        in_specs=[pl.BlockSpec(memory_space=pl.ANY)] * 2,
        scratch_shapes=[pltpu.VMEM((2, 3, 3, 3, ch, ch), BF), pltpu.SemaphoreType.DMA((2,))],
        out_shape=(pltpu.VMEM((3, rows, 3 * rows), BF),) * 3,
        compiler_params=params(3),
        cost_estimate=pl.CostEstimate(flops=1_000_000_000, bytes_accessed=4_000_000, transcendentals=0),
        name="bands",
    )(*in_hbm(laid(first_weight), laid(second_weight)))


def shifted_rows(out, row, block, before, after, rows):
    lane = iota(block.shape, 1)
    at = slice(row * LANES, (row + 1) * LANES)
    wide = block.astype(F32)
    out[0:rows, at] = jnp.where(lane == 0, before, pltpu.roll(wide, 1, 1)).astype(BF)
    out[rows : 2 * rows, at] = block
    out[2 * rows :, at] = jnp.where(lane == LANES - 1, after, pltpu.roll(wide, LANES - 1, 1)).astype(BF)


def lane_to(edges, source, target):
    shift = (target - source) % LANES
    return edges if shift == 0 else pltpu.roll(edges, shift, 1)


def fold_taps(product, ch, ny):
    rows = ch * ny
    lane = iota((ch, rows), 1)
    total = None
    for y in range(ny):
        block = product[y * ch : (y + 1) * ch]
        if y == 0:
            block = jnp.where(lane >= rows - ch, 0.0, block)
        if y == ny - 1:
            block = jnp.where(lane < ch, 0.0, block)
        if y != 1:
            block = pltpu.roll(block, (ch * (1 - y)) % rows, 1)
        total = block if total is None else total + block
    return total[:, :LANES]


def place_taps(columns, folded, a, c, ch):
    lane = iota(folded.shape, 1)
    for b in range(3):
        target = ch * ((a * 3 + b) * 3 + c)
        col, offset = target // LANES, target % LANES
        moved = lane_to(folded, b * ch, offset)
        columns[col] = jnp.where((lane >= offset) & (lane < offset + ch), moved, columns[col])


def bias_terms(field, ch, ny):
    nx = field.shape[1] // LANES
    wide = field.astype(F32)
    total = wide[:, 0:LANES]
    for x in range(1, nx):
        total = total + wide[:, x * LANES : (x + 1) * LANES]
    folded = total[0:ch]
    for y in range(1, ny):
        folded = folded + total[y * ch : (y + 1) * ch]
    return jnp.sum(folded, axis=1, keepdims=True)


def silu(preact):
    return (preact / (1.0 + jnp.exp(-preact))).astype(BF)


def bias_column(ref, ny):
    ch = ref.shape[1]
    r, k = iota((ch, ch), 0), iota((ch, ch), 1)
    column = jnp.sum(jnp.where(r == k, ref[...], 0.0), axis=1, keepdims=True)
    return jnp.concatenate([column] * ny, axis=0)


def sides(even, one, two):
    return jnp.where(even, two, one), jnp.where(even, one, two)


def edge_columns(nx, even, near_ref, one_ref, two_ref):
    n = near_ref.shape[0]
    j, k = iota((LANES, n), 0), iota((LANES, n), 1)
    s, xx = j // 16, j % 16
    column = jnp.where(s == 0, 2, jnp.where(s == 1, 3, jnp.where(s == 5, 0, jnp.where(s == 6, 1, jnp.where(s == 3, 5, jnp.where(s == 7, 4, -1))))))
    first = column * nx
    hit = lambda low, high, offset: one_hot((column >= 0) & (xx >= low) & (xx < high) & (k == first + xx - low + offset))
    before, after = sides(even, one_ref[...], two_ref[...])
    out = mm(hit(2, nx + 2, 0), near_ref[...])
    out = out + mm(hit(0, 2, nx - 2), before)
    return out + mm(hit(nx + 2, nx + 4, 0), after)


def main_kernel(
    nx, ch, ny, scale,
    t1_ref, tv_ref, f_ref, g_ref, one_ref, two_ref, near_ref, edge_one_ref, edge_two_ref, bias_ref,
    hid_ref, fs, keep_ref, give_ref,
    gs, pre,
):
    rows = ch * ny
    even = is_even("gx")
    edges = edge_columns(nx, even, near_ref, edge_one_ref, edge_two_ref).T
    for i, (src, dst, left, right) in enumerate(((f_ref, fs, 16, 80), (g_ref, gs, 48, 112))):
        above, below = sides(even, one_ref[i * rows : (i + 1) * rows], two_ref[i * rows : (i + 1) * rows])
        for x in range(nx + 2):
            if x == 0:
                block = above
            elif x == nx + 1:
                block = below
            else:
                block = src[:, (x - 1) * LANES : x * LANES]
            shifted_rows(dst, x, block, lane_to(edges, left + x + 1, 0), lane_to(edges, right + x + 1, LANES - 1), rows)

    n5 = nx * LANES
    acc = mm(t1_ref[0], fs[:, 0:n5])
    for a in range(1, 3):
        acc = acc + mm(t1_ref[a], fs[:, a * LANES : a * LANES + n5])
    preact = acc + bias_column(bias_ref, ny)
    pre[...] = preact
    hid_ref[...] = silu(preact)
    hidden = hid_ref[...]

    lane = iota((ch, LANES), 1)
    spare = 27 * ch % LANES
    mine = is_even("smp")
    columns = [jnp.zeros((ch, LANES), F32) for _ in range(TERMS // LANES)]
    for a in range(3):
        for c in range(3):
            left = gs[(2 - c) * rows : (3 - c) * rows, (2 - a) * LANES : (2 - a) * LANES + n5]
            place_taps(columns, fold_taps(mm_nt(left, hidden), ch, ny), a, c, ch)
    columns[-1] = jnp.where(lane == spare, bias_terms(g_ref[...], ch, ny), columns[-1])
    second = [part * scale for part in columns]

    acc = mm(tv_ref[0], gs[:, 0:n5])
    for a in range(1, 3):
        acc = acc + mm(tv_ref[a], gs[:, a * LANES : a * LANES + n5])
    preact = pre[...]
    logistic = 1.0 / (1.0 + jnp.exp(-preact))
    preact_grad = (acc * logistic * (1.0 + preact * (1.0 - logistic))).astype(BF)

    columns = [jnp.zeros((ch, LANES), F32) for _ in range(TERMS // LANES)]
    for a in range(3):
        for c in range(3):
            taps = fs[c * rows : (c + 1) * rows, a * LANES : a * LANES + n5]
            place_taps(columns, fold_taps(mm_nt(preact_grad, taps), ch, ny), a, c, ch)
    columns[-1] = jnp.where(lane == spare, bias_terms(preact_grad, ch, ny), columns[-1])
    first = [part * scale for part in columns]
    for i in range(TERMS // LANES):
        at = slice(i * LANES, (i + 1) * LANES)
        keep_ref[:, at] = jnp.where(mine, second[i], first[i])
        give_ref[:, at] = jnp.where(mine, first[i], second[i])


def main(t1, tv, field, cot, one, two, near, edge_one, edge_two, bias, ch, ny, scale):
    rows = ch * ny
    nx = field.shape[1] // LANES
    sds = pltpu.VMEM
    return pl.pallas_call(
        functools.partial(main_kernel, nx, ch, ny, scale),
        out_shape=(
            sds((rows, nx * LANES), BF),
            sds((3 * rows, (nx + 2) * LANES), BF),
            sds((ch, TERMS), F32),
            sds((ch, TERMS), F32),
        ),
        scratch_shapes=[
            pltpu.VMEM((3 * rows, (nx + 2) * LANES), BF),
            pltpu.VMEM((rows, nx * LANES), F32),
        ],
        compiler_params=params(8),
        name="main",
    )(*in_vmem(t1, tv, field, cot, one, two, near, edge_one, edge_two, bias))


def residual_kernel(
    nx, ch, ny,
    t1_ref, t2_ref, h_ref, fs_ref, f_ref, far_one_ref, far_two_ref, near_ref, edge_one_ref, edge_two_ref, bias1_ref, bias2_ref,
    o_ref,
    ends, hs,
):
    rows = ch * ny
    even = is_even("gx")
    above, below = sides(even, far_one_ref[...], far_two_ref[...])
    middle = fs_ref[rows : 2 * rows]
    edges_t = edge_columns(nx, even, near_ref, edge_one_ref, edge_two_ref)
    j, k = iota((LANES, LANES), 0), iota((LANES, LANES), 1)
    own_end = jnp.where(j // 16 == 2, 0, jnp.where(j // 16 == 4, LANES - 1, -1))
    for x in range(nx + 4):
        block = above if x == 0 else below if x == nx + 3 else middle[:, (x - 1) * LANES : x * LANES]
        edges_t = edges_t + mm_nt(one_hot((j % 16 == x) & (k == own_end)), block)
    edges = edges_t.T
    shifted_rows(ends, 0, above, lane_to(edges, 16, 0), lane_to(edges, 80, LANES - 1), rows)
    shifted_rows(ends, 1, below, lane_to(edges, 16 + nx + 3, 0), lane_to(edges, 80 + nx + 3, LANES - 1), rows)
    acc = None
    row = lambda x: fs_ref[:, (x + 1) * LANES : (x + 2) * LANES]
    pairs = ((ends[:, 0:LANES], row(nx - 1)), (row(-1), row(nx)), (row(0), ends[:, LANES:]))
    for a in range(3):
        columns = [lane_to(edges, 16 * c + a, 0).astype(BF) for c in range(3)]
        term = mm(t1_ref[a], jnp.concatenate([*pairs[a], jnp.concatenate(columns, axis=0)], axis=1))
        acc = term if acc is None else acc + term
    hidden = silu(acc + bias_column(bias1_ref, ny))
    outer = hidden[:, 2 * LANES :].astype(F32)
    for x in range(nx + 2):
        if x == 0:
            block = hidden[:, 0:LANES]
        elif x == nx + 1:
            block = hidden[:, LANES : 2 * LANES]
        else:
            block = h_ref[:, (x - 1) * LANES : x * LANES]
        shifted_rows(hs, x, block, lane_to(outer, x, 0), lane_to(outer, 64 + x, LANES - 1), rows)
    n5 = nx * LANES
    acc = mm(t2_ref[0], hs[:, 0:n5])
    for a in range(1, 3):
        acc = acc + mm(t2_ref[a], hs[:, a * LANES : a * LANES + n5])
    total = (f_ref[...].astype(F32) + (acc + bias_column(bias2_ref, ny))).astype(BF)
    r, k = iota((rows, rows), 0), iota((rows, rows), 1)
    back = one_hot(k == (r % ny) * ch + r // ny)
    ordered = mm(back, total)
    for x in range(nx):
        o_ref[0, :, x] = ordered[:, x * LANES : (x + 1) * LANES].reshape(ch, ny, LANES).astype(BF)


def residual(t1, t2, hidden, fs, field, far_one, far_two, near, edge_one, edge_two, bias1, bias2, ch, ny):
    rows = ch * ny
    nx = field.shape[1] // LANES
    return pl.pallas_call(
        functools.partial(residual_kernel, nx, ch, ny),
        out_shape=jax.ShapeDtypeStruct((1, ch, nx, ny, LANES), BF),
        scratch_shapes=[pltpu.VMEM((3 * rows, 2 * LANES), BF), pltpu.VMEM((3 * rows, (nx + 2) * LANES), BF)],
        compiler_params=params(8),
        cost_estimate=pl.CostEstimate(flops=3_000_000_000, bytes_accessed=3_000_000, transcendentals=0),
        name="residual",
    )(*in_vmem(t1, t2, hidden, fs, field, far_one, far_two, near, edge_one, edge_two, bias1, bias2))


def moved(array, sizes, step):
    ns, nx, nz = sizes
    pairs = []
    for s in range(ns):
        for x in range(nx):
            for z in range(nz):
                t, u, v = step(s, x, z)
                pairs.append(((s * nx + x) * nz + z, (t * nx + u) * nz + v))
    return lax.ppermute(array, AXES, pairs)


def paired(array, sizes, turn, dz):
    ns, nx, nz = sizes
    return moved(array, sizes, lambda s, x, z: (s, (x + (1 if x % 2 == turn else -1)) % nx, (z + dz) % nz))


def swapped(array, sizes, bits):
    return moved(array, sizes, lambda s, x, z: (s ^ bits[0], x ^ bits[1], z ^ bits[2]))


def add_kernel(n_in, *refs):
    terms = [ref[...].astype(F32) for ref in refs[:n_in]]
    out = refs[n_in]
    while len(terms) > 1:
        terms = [terms[i] + terms[i + 1] for i in range(0, len(terms), 2)]
    total = terms[0]
    n = total.shape[1] - LANES
    out[:, :n] = total[:, :n].astype(out.dtype)
    tail = total[:, n:]
    lane = iota(tail.shape, 1)
    spare = 864 % LANES
    joined = tail + pltpu.roll(tail, LANES - 1, 1)
    if out.dtype == BF:
        low = joined - joined.astype(BF).astype(F32)
        tail = jnp.where(lane == spare + 1, pltpu.roll(low, 1, 1), tail)
    out[:, n:] = jnp.where(lane == spare, joined, tail).astype(out.dtype)


def add(terms, dtype):
    return pl.pallas_call(
        functools.partial(add_kernel, len(terms)),
        out_shape=pltpu.VMEM(terms[0].shape, dtype),
        compiler_params=params(1),
        name="add",
    )(*in_vmem(*terms))


def exchange(sent, sizes, pair):
    steps = [(0, 0, 0)]
    for bits in pair:
        steps = steps + [tuple(p ^ q for p, q in zip(bits, step)) for step in steps]
    return [sent] + [swapped(sent, sizes, step) for step in steps[1:]]


def sum_all(keep, give, sizes, output):
    near = (1, 0, 0)
    bits = [(1 << i, 0, 0) for i in range(1, sizes[0].bit_length() - 1)]
    bits += [(0, 0, 1 << i) for i in range(sizes[2].bit_length() - 1)]
    bits += [(0, 1 << i, 0) for i in range(sizes[1].bit_length() - 1)]
    terms = [keep, swapped(give, sizes, near)]
    for i in range(0, len(bits), 2):
        terms = exchange(add(terms, BF), sizes, bits[i : i + 2])
        if i == 0:
            *terms, output = lax.optimization_barrier((*terms, output))
    mine = add(terms, F32)
    return mine, swapped(mine, sizes, near), output


def spread_kernel(ch, mine_ref, other_ref, first_ref, first_bias_ref, second_ref, second_bias_ref):
    even = is_even("smp")
    mine, other = mine_ref[...], other_ref[...]
    r, k = iota((ch, LANES), 0), iota((ch, LANES), 1)
    for terms, out, bias in (
        (jnp.where(even, other, mine), first_ref, first_bias_ref),
        (jnp.where(even, mine, other), second_ref, second_bias_ref),
    ):
        for tap in range(27):
            at = tap * ch
            block = terms[:, at // LANES * LANES : (at // LANES + 1) * LANES]
            out[tap // 9, tap // 3 % 3, tap % 3] = lane_to(block, at % LANES, 0)[:, :ch]
        tail = lane_to(terms[:, TERMS - LANES :], 27 * ch % LANES, 0)[:, 0:1]
        bias[...] = jnp.sum(jnp.where(r == k, tail, 0.0), axis=0, keepdims=True)[:, :ch]


def spread(mine, other, ch):
    sds = jax.ShapeDtypeStruct
    taps, bias = sds((3, 3, 3, ch, ch), F32), sds((1, ch), F32)
    first, first_bias, second, second_bias = pl.pallas_call(
        functools.partial(spread_kernel, ch),
        out_shape=(taps, bias, taps, bias),
        compiler_params=params(4),
        name="spread",
    )(*in_vmem(mine, other))
    laid = lambda grad: jnp.transpose(grad, (3, 0, 1, 2, 4))
    return laid(first), first_bias.reshape(ch), laid(second), second_bias.reshape(ch)


def shards(sizes, features, first_weight, first_bias, second_weight, second_bias, cotangent):
    ns, ngx, ngz = sizes
    _, ch, nx, ny, nz = features.shape
    assert features.shape[0] == 1 and nz == LANES and ngz == 2 and ngx % 2 == 0
    assert not any(n & (n - 1) for n in sizes) and ns > 1
    scale = float((ns * nx * ngx * ny * nz * ngz) ** -0.5)
    field, cot, one, two, far_one, far_two, edge = pack(features, cotangent)
    one, two = paired(one, sizes, 0, 0), paired(two, sizes, 1, 0)
    near = swapped(edge, sizes, (0, 0, 1))
    edge_one, edge_two = paired(edge, sizes, 0, 1), paired(edge, sizes, 1, 1)
    far_one, far_two = paired(far_one, sizes, 0, 0), paired(far_two, sizes, 1, 0)
    t1, tv, t2 = bands(first_weight, second_weight, ny)
    bias1, bias2 = first_bias.reshape(1, ch), second_bias.reshape(1, ch)
    hidden, fs, keep, give = main(t1, tv, field, cot, one, two, near, edge_one, edge_two, bias1, ch, ny, scale)
    output = residual(t1, t2, hidden, fs, field, far_one, far_two, near, edge_one, edge_two, bias1, bias2, ch, ny)
    mine, other, output = sum_all(keep, give, sizes, output)
    return output, *spread(mine, other, ch)


def solution(mesh):
    sizes = tuple(mesh.shape[axis] for axis in AXES)
    split = P("smp", None, "gx", None, "gz")
    return jax.shard_map(
        functools.partial(shards, sizes),
        mesh=mesh,
        in_specs=(split, P(), P(), P(), P(), split),
        out_specs=(split, P(), P(), P(), P()),
        check_vma=False,
    )
```

```python
import functools

import jax
import jax.numpy as jnp
from jax import lax
from jax.experimental import pallas as pl
from jax.experimental.pallas import tpu as pltpu
from jax.sharding import PartitionSpec as P

AXES = ("smp", "gx", "gz")
BF = jnp.bfloat16
F32 = jnp.float32
LANES = 128
TERMS = 896


def mm(a, b):
    return lax.dot_general(a, b, (((1,), (0,)), ((), ())), preferred_element_type=F32)


def mm_nt(a, b):
    return lax.dot_general(a, b, (((1,), (1,)), ((), ())), preferred_element_type=F32)


def iota(shape, dim):
    return lax.broadcasted_iota(jnp.int32, shape, dim)


def one_hot(hit):
    return jnp.where(hit, 1.0, 0.0).astype(BF)


def params(mib=8):
    return pltpu.CompilerParams(vmem_limit_bytes=mib * 2**20)


def in_vmem(*arrays):
    return [pltpu.with_memory_space_constraint(array, pltpu.VMEM) for array in arrays]


def in_hbm(*arrays):
    return [pltpu.with_memory_space_constraint(array, pltpu.HBM) for array in arrays]


def is_even(axis):
    return lax.axis_index(axis) % 2 == 0


def ordered(ch, ny):
    r, k = iota((ch * ny, ch * ny), 0), iota((ch * ny, ch * ny), 1)
    return one_hot(k == (r % ch) * ny + r // ch)


def faces_kernel(nx, ch, ny, f_any, g_any, w1_any, w2_any, up_ref, dn_ref, held, w1_ref, w2_ref, raw, sems):
    rows = ch * ny
    wanted = ((0, nx - 2), (0, nx - 1), (1, nx - 1), (0, 1), (0, 0), (1, 0))
    others = [(i, x) for x in range(nx) for i in range(2) if (i, x) not in wanted]
    copies = {
        (i, x): pltpu.make_async_copy((f_any, g_any)[i].at[0, :, x], held.at[i, x], sems.at[i * nx + x])
        for i, x in (*wanted, *others)
    }
    weights = [pltpu.make_async_copy(src, dst, sems.at[2 * nx + i]) for i, (src, dst) in enumerate(((w1_any, w1_ref), (w2_any, w2_ref)))]
    for copy in (*copies.values(), *weights):
        copy.start()
    for j, (i, x) in enumerate(wanted):
        copies[i, x].wait()
        raw[:, j * LANES : (j + 1) * LANES] = held[i, x].astype(F32).reshape(rows, LANES).astype(BF)
    out = mm(ordered(ch, ny), raw[...]).astype(BF)
    for j in range(3):
        at = slice(j * rows, (j + 1) * rows)
        up_ref[at] = out[:, j * LANES : (j + 1) * LANES]
        dn_ref[at] = out[:, (j + 3) * LANES : (j + 4) * LANES]
    for key in others:
        copies[key].wait()
    for copy in weights:
        copy.wait()


def faces(features, cotangent, first_weight, second_weight):
    _, ch, nx, ny, _ = features.shape
    rows = ch * ny
    sds = pltpu.VMEM
    laid = lambda weight: jnp.transpose(weight, (1, 2, 3, 0, 4))
    return pl.pallas_call(
        functools.partial(faces_kernel, nx, ch, ny),
        out_shape=(
            sds((3 * rows, LANES), BF),
            sds((3 * rows, LANES), BF),
            sds((2, nx, ch, ny, LANES), BF),
            sds((3, 3, 3, ch, ch), BF),
            sds((3, 3, 3, ch, ch), BF),
        ),
        in_specs=[pl.BlockSpec(memory_space=pl.ANY)] * 4,
        scratch_shapes=[pltpu.VMEM((rows, 6 * LANES), BF), pltpu.SemaphoreType.DMA((2 * nx + 2,))],
        compiler_params=params(4),
        name="faces",
    )(*in_hbm(features, cotangent, laid(first_weight), laid(second_weight)))


def pack_kernel(nx, ch, ny, held, fo_ref, go_ref, edge_ref, raw):
    rows = ch * ny
    perm = ordered(ch, ny)
    for i, dst in enumerate((fo_ref, go_ref)):
        for x in range(nx):
            raw[:, x * LANES : (x + 1) * LANES] = held[i, x].astype(F32).reshape(rows, LANES).astype(BF)
        dst[...] = mm(perm, raw[...]).astype(BF)
    n = edge_ref.shape[0]
    j, m = iota((n, nx * LANES), 0), iota((n, nx * LANES), 1)
    c, x = j // nx, j % nx
    zf = jnp.where(c < 2, c, LANES - 4 + c)
    pick_f = one_hot((c < 4) & (m == x * LANES + zf))
    zg = jnp.where(c == 4, 0, LANES - 1)
    pick_g = one_hot((c >= 4) & (c < 6) & (m == x * LANES + zg))
    edge_ref[...] = (mm_nt(pick_f, fo_ref[...]) + mm_nt(pick_g, go_ref[...])).astype(BF)


def pack(held):
    _, nx, ch, ny, _ = held.shape
    rows = ch * ny
    edge_rows = -(-6 * nx // 32) * 32
    sds = pltpu.VMEM
    return pl.pallas_call(
        functools.partial(pack_kernel, nx, ch, ny),
        out_shape=(sds((rows, nx * LANES), BF), sds((rows, nx * LANES), BF), sds((edge_rows, rows), BF)),
        scratch_shapes=[pltpu.VMEM((rows, nx * LANES), BF)],
        compiler_params=params(4),
        cost_estimate=pl.CostEstimate(flops=500_000_000, bytes_accessed=1_000_000, transcendentals=0),
        name="pack",
    )(*in_vmem(held))


def bands_kernel(ny, w1_ref, w2_ref, t1_ref, tv_ref, t2_ref):
    ch = w1_ref.shape[-1]
    rows = ny * ch
    lane = iota((ch, rows), 1)
    r, k = iota((ch, LANES), 0), iota((ch, LANES), 1)
    places = [one_hot(k == r + b * ch) for b in range(3)]

    def direct(ref):
        wide = None
        for b in range(3):
            part = mm(ref[:, b].reshape(9 * ch, ch), places[b])
            wide = part if wide is None else wide + part
        return [wide[i * ch : (i + 1) * ch] for i in range(9)]

    def flipped(ref):
        none = jnp.zeros((ch, ch), BF)
        stack = [ref[2 - a, 2 - b, 2 - c] if b < 3 else none for a in range(3) for c in range(3) for b in range(4)]
        wide = mm_nt(one_hot(r == k)[:, :ch], jnp.concatenate(stack, axis=0))
        return [wide[:, i * LANES : (i + 1) * LANES] for i in range(9)]

    rest = jnp.zeros((ch, rows - LANES), F32)
    for taps, out in ((direct(w1_ref), t1_ref), (flipped(w2_ref), tv_ref), (direct(w2_ref), t2_ref)):
        for i, tap in enumerate(taps):
            a, c = i // 3, i % 3
            wide = jnp.concatenate([tap, rest], axis=1)
            for y in range(ny):
                block = wide if y == 1 else pltpu.roll(wide, (ch * (y - 1)) % rows, 1)
                if y == 0:
                    block = jnp.where(lane >= rows - ch, 0.0, block)
                if y == ny - 1:
                    block = jnp.where(lane < ch, 0.0, block)
                out[a, y * ch : (y + 1) * ch, c * rows : (c + 1) * rows] = block.astype(BF)


def bands(first_weight, second_weight, ny):
    ch = first_weight.shape[-1]
    rows = ch * ny
    return pl.pallas_call(
        functools.partial(bands_kernel, ny),
        out_shape=(pltpu.VMEM((3, rows, 3 * rows), BF),) * 3,
        compiler_params=params(3),
        cost_estimate=pl.CostEstimate(flops=1_000_000_000, bytes_accessed=4_000_000, transcendentals=0),
        name="bands",
    )(*in_vmem(first_weight, second_weight))


def shifted_rows(out, row, block, before, after, rows):
    lane = iota(block.shape, 1)
    at = slice(row * LANES, (row + 1) * LANES)
    wide = block.astype(F32)
    out[0:rows, at] = jnp.where(lane == 0, before, pltpu.roll(wide, 1, 1)).astype(BF)
    out[rows : 2 * rows, at] = block
    out[2 * rows :, at] = jnp.where(lane == LANES - 1, after, pltpu.roll(wide, LANES - 1, 1)).astype(BF)


def lane_to(edges, source, target):
    shift = (target - source) % LANES
    return edges if shift == 0 else pltpu.roll(edges, shift, 1)


def fold_taps(product, ch, ny):
    rows = ch * ny
    lane = iota((ch, rows), 1)
    total = None
    for y in range(ny):
        block = product[y * ch : (y + 1) * ch]
        if y == 0:
            block = jnp.where(lane >= rows - ch, 0.0, block)
        if y == ny - 1:
            block = jnp.where(lane < ch, 0.0, block)
        if y != 1:
            block = pltpu.roll(block, (ch * (1 - y)) % rows, 1)
        total = block if total is None else total + block
    return total[:, :LANES]


def place_taps(columns, folded, a, c, ch):
    lane = iota(folded.shape, 1)
    for b in range(3):
        target = ch * ((a * 3 + b) * 3 + c)
        col, offset = target // LANES, target % LANES
        moved = lane_to(folded, b * ch, offset)
        columns[col] = jnp.where((lane >= offset) & (lane < offset + ch), moved, columns[col])


def bias_terms(field, ch, ny):
    nx = field.shape[1] // LANES
    wide = field.astype(F32)
    total = wide[:, 0:LANES]
    for x in range(1, nx):
        total = total + wide[:, x * LANES : (x + 1) * LANES]
    folded = total[0:ch]
    for y in range(1, ny):
        folded = folded + total[y * ch : (y + 1) * ch]
    return jnp.sum(folded, axis=1, keepdims=True)


def silu(preact):
    return (preact / (1.0 + jnp.exp(-preact))).astype(BF)


def bias_column(ref, ny):
    ch = ref.shape[1]
    r, k = iota((ch, ch), 0), iota((ch, ch), 1)
    column = jnp.sum(jnp.where(r == k, ref[...], 0.0), axis=1, keepdims=True)
    return jnp.concatenate([column] * ny, axis=0)


def edge_columns(nx, sources):
    n = sources[0][3].shape[0]
    j, k = iota((LANES, n), 0), iota((LANES, n), 1)
    s, xx = j // 16, j % 16
    column = jnp.where(s == 0, 2, jnp.where(s == 1, 3, jnp.where(s == 5, 0, jnp.where(s == 6, 1, jnp.where(s == 3, 5, jnp.where(s == 7, 4, -1))))))
    out = None
    for low, high, start, message in sources:
        hit = (column >= 0) & (xx >= low) & (xx < high) & (k == column * nx + xx - low + start)
        part = mm(one_hot(hit), message)
        out = part if out is None else out + part
    return out


def conv_inside(t_ref, field, out, nx):
    n, m = nx * LANES, (nx - 1) * LANES
    out[...] = mm(t_ref[1], field[:, 0:n])
    out[:, LANES:] = out[:, LANES:] + mm(t_ref[0], field[:, 0:m])
    out[:, 0:m] = out[:, 0:m] + mm(t_ref[2], field[:, LANES:n])


def gate(hidden_grad, preact):
    logistic = 1.0 / (1.0 + jnp.exp(-preact))
    return (hidden_grad * logistic * (1.0 + preact * (1.0 - logistic))).astype(BF)


def tap_terms(upstream, taps, ch, ny):
    columns = [jnp.zeros((ch, LANES), F32) for _ in range(TERMS // LANES)]
    for a in range(3):
        for c in range(3):
            product = mm_nt(*((taps(2 - a, 2 - c), upstream) if upstream is not None else taps(a, c)))
            place_taps(columns, fold_taps(product, ch, ny), a, c, ch)
    return columns


def with_bias(columns, field, ch, ny):
    lane = iota((ch, LANES), 1)
    return columns[:-1] + [jnp.where(lane == 27 * ch % LANES, bias_terms(field, ch, ny), columns[-1])]


def inner_kernel(
    nx, ch, ny,
    t1_ref, tv_ref, f_ref, g_ref, near_ref, bias_ref,
    fs, gs, pre, grad, hid_ref, second_ref, first_ref,
):
    rows = ch * ny
    edges = edge_columns(nx, ((2, nx + 2, 0, near_ref[...]),)).T
    for src, dst, left, right in ((f_ref, fs, 16, 80), (g_ref, gs, 48, 112)):
        for x in range(nx):
            block = src[:, x * LANES : (x + 1) * LANES]
            shifted_rows(dst, x, block, lane_to(edges, left + x + 2, 0), lane_to(edges, right + x + 2, LANES - 1), rows)
    conv_inside(t1_ref, fs, pre, nx)
    pre[...] = pre[...] + bias_column(bias_ref, ny)
    conv_inside(tv_ref, gs, grad, nx)
    n = (nx - 2) * LANES
    inside = slice(LANES, LANES + n)
    preact = pre[:, inside]
    hid_ref[...] = silu(preact)
    preact_grad = gate(grad[:, inside], preact)
    window = lambda ref, a, c: ref[c * rows : (c + 1) * rows, a * LANES : a * LANES + n]
    second = tap_terms(hid_ref[...], lambda a, c: window(gs, a, c), ch, ny)
    first = tap_terms(None, lambda a, c: (preact_grad, window(fs, a, c)), ch, ny)
    second = with_bias(second, g_ref[...], ch, ny)
    first = with_bias(first, preact_grad, ch, ny)
    for i in range(TERMS // LANES):
        at = slice(i * LANES, (i + 1) * LANES)
        second_ref[:, at] = second[i]
        first_ref[:, at] = first[i]


def inner(t1, tv, field, cot, near, bias, ch, ny):
    rows = ch * ny
    nx = field.shape[1] // LANES
    sds = pltpu.VMEM
    return pl.pallas_call(
        functools.partial(inner_kernel, nx, ch, ny),
        out_shape=(
            sds((3 * rows, nx * LANES), BF),
            sds((3 * rows, nx * LANES), BF),
            sds((rows, nx * LANES), F32),
            sds((rows, nx * LANES), F32),
            sds((rows, (nx - 2) * LANES), BF),
            sds((ch, TERMS), F32),
            sds((ch, TERMS), F32),
        ),
        compiler_params=params(6),
        cost_estimate=pl.CostEstimate(flops=2_000_000_000, bytes_accessed=4_000_000, transcendentals=0),
        name="inner",
    )(*in_vmem(t1, tv, field, cot, near, bias))


def outer_kernel(
    nx, ch, ny, scale,
    t1_ref, tv_ref, fs, gs, pre, grad, part_second_ref, part_first_ref, above_ref, below_ref, before_ref, after_ref,
    hid_ref, fe, keep_ref, give_ref,
    ge,
):
    rows = ch * ny
    edges = edge_columns(nx, ((0, 2, nx - 2, before_ref[...]), (nx + 2, nx + 4, 0, after_ref[...]))).T
    for i, (dst, left, right) in enumerate(((fe, 16, 80), (ge, 48, 112))):
        for j, (src, xx) in enumerate(((above_ref, 1), (below_ref, nx + 2))):
            block = src[(i + 1) * rows : (i + 2) * rows]
            shifted_rows(dst, j, block, lane_to(edges, left + xx, 0), lane_to(edges, right + xx, LANES - 1), rows)

    last = (nx - 1) * LANES
    ends = lambda ref: jnp.concatenate([ref[:, 0:LANES], ref[:, last:]], axis=1)
    both = lambda t, e: jnp.concatenate([mm(t[0], e[:, 0:LANES]), mm(t[2], e[:, LANES:])], axis=1)
    preact = ends(pre) + both(t1_ref, fe)
    hid_ref[...] = silu(preact)
    preact_grad = gate(ends(grad) + both(tv_ref, ge), preact)

    def window(own, end, a, c):
        at = slice(c * rows, (c + 1) * rows)
        head = end[at, 0:LANES] if a == 0 else own[at, (a - 1) * LANES : a * LANES]
        tail = end[at, LANES:] if a == 2 else own[at, last + (a - 1) * LANES : last + a * LANES]
        return jnp.concatenate([head, tail], axis=1)

    second = tap_terms(hid_ref[...], lambda a, c: window(gs, ge, a, c), ch, ny)
    first = tap_terms(None, lambda a, c: (preact_grad, window(fs, fe, a, c)), ch, ny)
    first = with_bias(first, preact_grad, ch, ny)
    mine = is_even("smp")
    for i in range(TERMS // LANES):
        at = slice(i * LANES, (i + 1) * LANES)
        part_second = (second[i] + part_second_ref[:, at]) * scale
        part_first = (first[i] + part_first_ref[:, at]) * scale
        keep_ref[:, at] = jnp.where(mine, part_second, part_first)
        give_ref[:, at] = jnp.where(mine, part_first, part_second)


def outer(t1, tv, fs, gs, pre, grad, second, first, above, below, before, after, ch, ny, scale):
    rows = ch * ny
    nx = fs.shape[1] // LANES
    sds = pltpu.VMEM
    return pl.pallas_call(
        functools.partial(outer_kernel, nx, ch, ny, scale),
        out_shape=(
            sds((rows, 2 * LANES), BF),
            sds((3 * rows, 2 * LANES), BF),
            sds((ch, TERMS), F32),
            sds((ch, TERMS), F32),
        ),
        scratch_shapes=[pltpu.VMEM((3 * rows, 2 * LANES), BF)],
        compiler_params=params(6),
        name="outer",
    )(*in_vmem(t1, tv, fs, gs, pre, grad, second, first, above, below, before, after))


def residual_kernel(
    nx, ch, ny,
    t1_ref, t2_ref, h_ref, h_end_ref, fs_ref, fe_ref, f_ref, above_ref, below_ref, near_ref, before_ref, after_ref, bias1_ref, bias2_ref,
    o_ref,
    ends, hs,
):
    rows = ch * ny
    above, below = above_ref[0:rows], below_ref[0:rows]
    sources = ((2, nx + 2, 0, near_ref[...]), (0, 2, nx - 2, before_ref[...]), (nx + 2, nx + 4, 0, after_ref[...]))
    edges_t = edge_columns(nx, sources)
    end = fe_ref[rows : 2 * rows]
    unshifted = [above, end[:, 0:LANES], *(f_ref[:, x * LANES : (x + 1) * LANES] for x in range(nx)), end[:, LANES:], below]
    j, k = iota((LANES, LANES), 0), iota((LANES, LANES), 1)
    own_end = jnp.where(j // 16 == 2, 0, jnp.where(j // 16 == 4, LANES - 1, -1))
    for x in range(nx + 4):
        edges_t = edges_t + mm_nt(one_hot((j % 16 == x) & (k == own_end)), unshifted[x])
    edges = edges_t.T
    shifted_rows(ends, 0, above, lane_to(edges, 16, 0), lane_to(edges, 80, LANES - 1), rows)
    shifted_rows(ends, 1, below, lane_to(edges, 16 + nx + 3, 0), lane_to(edges, 80 + nx + 3, LANES - 1), rows)
    acc = None
    row = lambda x: fs_ref[:, x * LANES : (x + 1) * LANES]
    pairs = ((ends[:, 0:LANES], row(nx - 1)), (fe_ref[:, 0:LANES], fe_ref[:, LANES:]), (row(0), ends[:, LANES:]))
    for a in range(3):
        columns = [lane_to(edges, 16 * c + a, 0).astype(BF) for c in range(3)]
        term = mm(t1_ref[a], jnp.concatenate([*pairs[a], jnp.concatenate(columns, axis=0)], axis=1))
        acc = term if acc is None else acc + term
    hidden = silu(acc + bias_column(bias1_ref, ny))
    outer = hidden[:, 2 * LANES :].astype(F32)
    for x in range(nx + 2):
        if x == 0:
            block = hidden[:, 0:LANES]
        elif x == nx + 1:
            block = hidden[:, LANES : 2 * LANES]
        elif x == 1:
            block = h_end_ref[:, 0:LANES]
        elif x == nx:
            block = h_end_ref[:, LANES:]
        else:
            block = h_ref[:, (x - 2) * LANES : (x - 1) * LANES]
        shifted_rows(hs, x, block, lane_to(outer, x, 0), lane_to(outer, 64 + x, LANES - 1), rows)
    n5 = nx * LANES
    acc = mm(t2_ref[0], hs[:, 0:n5])
    for a in range(1, 3):
        acc = acc + mm(t2_ref[a], hs[:, a * LANES : a * LANES + n5])
    total = (f_ref[...].astype(F32) + (acc + bias_column(bias2_ref, ny))).astype(BF)
    r, k = iota((rows, rows), 0), iota((rows, rows), 1)
    back = one_hot(k == (r % ny) * ch + r // ny)
    ordered = mm(back, total)
    for x in range(nx):
        o_ref[0, :, x] = ordered[:, x * LANES : (x + 1) * LANES].reshape(ch, ny, LANES).astype(BF)


def residual(t1, t2, hidden, hidden_end, fs, fe, field, above, below, near, before, after, bias1, bias2, ch, ny):
    rows = ch * ny
    nx = field.shape[1] // LANES
    return pl.pallas_call(
        functools.partial(residual_kernel, nx, ch, ny),
        out_shape=jax.ShapeDtypeStruct((1, ch, nx, ny, LANES), BF),
        scratch_shapes=[pltpu.VMEM((3 * rows, 2 * LANES), BF), pltpu.VMEM((3 * rows, (nx + 2) * LANES), BF)],
        compiler_params=params(8),
        cost_estimate=pl.CostEstimate(flops=3_000_000_000, bytes_accessed=3_000_000, transcendentals=0),
        name="residual",
    )(*in_vmem(t1, t2, hidden, hidden_end, fs, fe, field, above, below, near, before, after, bias1, bias2))


def moved(array, sizes, step):
    ns, nx, nz = sizes
    pairs = []
    for s in range(ns):
        for x in range(nx):
            for z in range(nz):
                t, u, v = step(s, x, z)
                pairs.append(((s * nx + x) * nz + z, (t * nx + u) * nz + v))
    return lax.ppermute(array, AXES, pairs)


def along(array, sizes, dx):
    ns, nx, nz = sizes
    return moved(array, sizes, lambda s, x, z: (s, (x + dx) % nx, z))


def swapped(array, sizes, bits):
    return moved(array, sizes, lambda s, x, z: (s ^ bits[0], x ^ bits[1], z ^ bits[2]))


def add_kernel(n_in, *refs):
    terms = [ref[...].astype(F32) for ref in refs[:n_in]]
    out = refs[n_in]
    while len(terms) > 1:
        terms = [terms[i] + terms[i + 1] for i in range(0, len(terms), 2)]
    total = terms[0]
    n = total.shape[1] - LANES
    out[:, :n] = total[:, :n].astype(out.dtype)
    tail = total[:, n:]
    lane = iota(tail.shape, 1)
    spare = 864 % LANES
    joined = tail + pltpu.roll(tail, LANES - 1, 1)
    if out.dtype == BF:
        low = joined - joined.astype(BF).astype(F32)
        tail = jnp.where(lane == spare + 1, pltpu.roll(low, 1, 1), tail)
    out[:, n:] = jnp.where(lane == spare, joined, tail).astype(out.dtype)


def add(terms, dtype):
    return pl.pallas_call(
        functools.partial(add_kernel, len(terms)),
        out_shape=pltpu.VMEM(terms[0].shape, dtype),
        compiler_params=params(1),
        name="add",
    )(*in_vmem(*terms))


def exchange(sent, sizes, pair):
    steps = [(0, 0, 0)]
    for bits in pair:
        steps = steps + [tuple(p ^ q for p, q in zip(bits, step)) for step in steps]
    return [sent] + [swapped(sent, sizes, step) for step in steps[1:]]


def sum_all(keep, give, sizes, output):
    near = (1, 0, 0)
    bits = [(0, 1 << i, 0) for i in range(sizes[1].bit_length() - 1)]
    bits += [(0, 0, 1 << i) for i in range(sizes[2].bit_length() - 1)]
    bits += [(1 << i, 0, 0) for i in range(1, sizes[0].bit_length() - 1)]
    terms = [keep, swapped(give, sizes, near)]
    for i in range(0, len(bits), 2):
        terms = exchange(add(terms, BF), sizes, bits[i : i + 2])
        if i == 0:
            *terms, output = lax.optimization_barrier((*terms, output))
    mine = add(terms, F32)
    return mine, swapped(mine, sizes, near), output


def spread_kernel(ch, mine_ref, other_ref, first_ref, first_bias_ref, second_ref, second_bias_ref):
    even = is_even("smp")
    mine, other = mine_ref[...], other_ref[...]
    r, k = iota((ch, LANES), 0), iota((ch, LANES), 1)
    for terms, out, bias in (
        (jnp.where(even, other, mine), first_ref, first_bias_ref),
        (jnp.where(even, mine, other), second_ref, second_bias_ref),
    ):
        for tap in range(27):
            at = tap * ch
            block = terms[:, at // LANES * LANES : (at // LANES + 1) * LANES]
            out[tap // 9, tap // 3 % 3, tap % 3] = lane_to(block, at % LANES, 0)[:, :ch]
        tail = lane_to(terms[:, TERMS - LANES :], 27 * ch % LANES, 0)[:, 0:1]
        bias[...] = jnp.sum(jnp.where(r == k, tail, 0.0), axis=0, keepdims=True)[:, :ch]


def spread(mine, other, ch):
    sds = jax.ShapeDtypeStruct
    taps, bias = sds((3, 3, 3, ch, ch), F32), sds((1, ch), F32)
    first, first_bias, second, second_bias = pl.pallas_call(
        functools.partial(spread_kernel, ch),
        out_shape=(taps, bias, taps, bias),
        compiler_params=params(4),
        name="spread",
    )(*in_vmem(mine, other))
    laid = lambda grad: jnp.transpose(grad, (3, 0, 1, 2, 4))
    return laid(first), first_bias.reshape(ch), laid(second), second_bias.reshape(ch)


def shards(sizes, features, first_weight, first_bias, second_weight, second_bias, cotangent):
    ns, ngx, ngz = sizes
    _, ch, nx, ny, nz = features.shape
    assert features.shape[0] == 1 and nz == LANES and ngz == 2
    assert not any(n & (n - 1) for n in sizes) and ns > 1
    scale = float((ns * nx * ngx * ny * nz * ngz) ** -0.5)
    up, down, held, weight1, weight2 = faces(features, cotangent, first_weight, second_weight)
    above, below = along(up, sizes, 1), along(down, sizes, -1)
    field, cot, edge = pack(held)
    near = swapped(edge, sizes, (0, 0, 1))
    before, after = along(near, sizes, 1), along(near, sizes, -1)
    t1, tv, t2 = bands(weight1, weight2, ny)
    bias1, bias2 = first_bias.reshape(1, ch), second_bias.reshape(1, ch)
    fs, gs, pre, grad, hidden, second, first = inner(t1, tv, field, cot, near, bias1, ch, ny)
    hidden_end, fe, keep, give = outer(
        t1, tv, fs, gs, pre, grad, second, first, above, below, before, after, ch, ny, scale
    )
    output = residual(t1, t2, hidden, hidden_end, fs, fe, field, above, below, near, before, after, bias1, bias2, ch, ny)
    mine, other, output = sum_all(keep, give, sizes, output)
    return output, *spread(mine, other, ch)


def solution(mesh):
    sizes = tuple(mesh.shape[axis] for axis in AXES)
    split = P("smp", None, "gx", None, "gz")
    return jax.shard_map(
        functools.partial(shards, sizes),
        mesh=mesh,
        in_specs=(split, P(), P(), P(), P(), split),
        out_specs=(split, P(), P(), P(), P()),
        check_vma=False,
    )
```

```python
import functools

import jax
import jax.numpy as jnp
from jax import lax
from jax.experimental import pallas as pl
from jax.experimental.pallas import tpu as pltpu
from jax.sharding import PartitionSpec as P

AXES = ("smp", "gx", "gz")
BF = jnp.bfloat16
F32 = jnp.float32
LANES = 128
TERMS = 896


def mm(a, b):
    return lax.dot_general(a, b, (((1,), (0,)), ((), ())), preferred_element_type=F32)


def mm_nt(a, b):
    return lax.dot_general(a, b, (((1,), (1,)), ((), ())), preferred_element_type=F32)


def iota(shape, dim):
    return lax.broadcasted_iota(jnp.int32, shape, dim)


def one_hot(hit):
    return jnp.where(hit, 1.0, 0.0).astype(BF)


def params(mib=8):
    return pltpu.CompilerParams(vmem_limit_bytes=mib * 2**20)


def in_vmem(*arrays):
    return [pltpu.with_memory_space_constraint(array, pltpu.VMEM) for array in arrays]


def in_hbm(*arrays):
    return [pltpu.with_memory_space_constraint(array, pltpu.HBM) for array in arrays]


def is_even(axis):
    return lax.axis_index(axis) % 2 == 0


def ordered(ch, ny):
    r, k = iota((ch * ny, ch * ny), 0), iota((ch * ny, ch * ny), 1)
    return one_hot(k == (r % ch) * ny + r // ch)


def faces_kernel(nx, ch, ny, f_any, g_any, w1_any, w2_any, up_ref, dn_ref, held, w1_ref, w2_ref, raw, sems):
    rows = ch * ny
    wanted = ((0, nx - 2), (0, nx - 1), (1, nx - 1), (0, 1), (0, 0), (1, 0))
    others = [(i, x) for x in range(nx) for i in range(2) if (i, x) not in wanted]
    copies = {
        (i, x): pltpu.make_async_copy((f_any, g_any)[i].at[0, :, x], held.at[i, x], sems.at[i * nx + x])
        for i, x in (*wanted, *others)
    }
    weights = [pltpu.make_async_copy(src, dst, sems.at[2 * nx + i]) for i, (src, dst) in enumerate(((w1_any, w1_ref), (w2_any, w2_ref)))]
    for copy in (*copies.values(), *weights):
        copy.start()
    for j, (i, x) in enumerate(wanted):
        copies[i, x].wait()
        raw[:, j * LANES : (j + 1) * LANES] = held[i, x].astype(F32).reshape(rows, LANES).astype(BF)
    out = mm(ordered(ch, ny), raw[...]).astype(BF)
    for j in range(3):
        at = slice(j * rows, (j + 1) * rows)
        up_ref[at] = out[:, j * LANES : (j + 1) * LANES]
        dn_ref[at] = out[:, (j + 3) * LANES : (j + 4) * LANES]
    for key in others:
        copies[key].wait()
    for copy in weights:
        copy.wait()


def faces(features, cotangent, first_weight, second_weight):
    _, ch, nx, ny, _ = features.shape
    rows = ch * ny
    sds = pltpu.VMEM
    laid = lambda weight: jnp.transpose(weight, (1, 2, 3, 0, 4))
    return pl.pallas_call(
        functools.partial(faces_kernel, nx, ch, ny),
        out_shape=(
            sds((3 * rows, LANES), BF),
            sds((3 * rows, LANES), BF),
            sds((2, nx, ch, ny, LANES), BF),
            sds((3, 3, 3, ch, ch), BF),
            sds((3, 3, 3, ch, ch), BF),
        ),
        in_specs=[pl.BlockSpec(memory_space=pl.ANY)] * 4,
        scratch_shapes=[pltpu.VMEM((rows, 6 * LANES), BF), pltpu.SemaphoreType.DMA((2 * nx + 2,))],
        compiler_params=params(4),
        name="faces",
    )(*in_hbm(features, cotangent, laid(first_weight), laid(second_weight)))


def pack_kernel(nx, ch, ny, held, fo_ref, go_ref, edge_ref, raw):
    rows = ch * ny
    perm = ordered(ch, ny)
    for i, dst in enumerate((fo_ref, go_ref)):
        for x in range(nx):
            raw[:, x * LANES : (x + 1) * LANES] = held[i, x].astype(F32).reshape(rows, LANES).astype(BF)
        dst[...] = mm(perm, raw[...]).astype(BF)
    n = edge_ref.shape[0]
    j, m = iota((n, nx * LANES), 0), iota((n, nx * LANES), 1)
    c, x = j // nx, j % nx
    zf = jnp.where(c < 2, c, LANES - 4 + c)
    pick_f = one_hot((c < 4) & (m == x * LANES + zf))
    zg = jnp.where(c == 4, 0, LANES - 1)
    pick_g = one_hot((c >= 4) & (c < 6) & (m == x * LANES + zg))
    edge_ref[...] = (mm_nt(pick_f, fo_ref[...]) + mm_nt(pick_g, go_ref[...])).astype(BF)


def pack(held):
    _, nx, ch, ny, _ = held.shape
    rows = ch * ny
    edge_rows = -(-6 * nx // 32) * 32
    sds = pltpu.VMEM
    return pl.pallas_call(
        functools.partial(pack_kernel, nx, ch, ny),
        out_shape=(sds((rows, nx * LANES), BF), sds((rows, nx * LANES), BF), sds((edge_rows, rows), BF)),
        scratch_shapes=[pltpu.VMEM((rows, nx * LANES), BF)],
        compiler_params=params(4),
        cost_estimate=pl.CostEstimate(flops=500_000_000, bytes_accessed=1_000_000, transcendentals=0),
        name="pack",
    )(*in_vmem(held))


def bands_kernel(ny, w1_ref, w2_ref, edge_ref, t1_ref, tv_ref, t2_ref, copy_ref):
    copy_ref[...] = edge_ref[...]
    ch = w1_ref.shape[-1]
    rows = ny * ch
    lane = iota((ch, rows), 1)
    r, k = iota((ch, LANES), 0), iota((ch, LANES), 1)
    places = [one_hot(k == r + b * ch) for b in range(3)]

    def direct(ref):
        wide = None
        for b in range(3):
            part = mm(ref[:, b].reshape(9 * ch, ch), places[b])
            wide = part if wide is None else wide + part
        return [wide[i * ch : (i + 1) * ch] for i in range(9)]

    def flipped(ref):
        none = jnp.zeros((ch, ch), BF)
        stack = [ref[2 - a, 2 - b, 2 - c] if b < 3 else none for a in range(3) for c in range(3) for b in range(4)]
        wide = mm_nt(one_hot(r == k)[:, :ch], jnp.concatenate(stack, axis=0))
        return [wide[:, i * LANES : (i + 1) * LANES] for i in range(9)]

    rest = jnp.zeros((ch, rows - LANES), F32)
    for taps, out in ((direct(w1_ref), t1_ref), (flipped(w2_ref), tv_ref), (direct(w2_ref), t2_ref)):
        for i, tap in enumerate(taps):
            a, c = i // 3, i % 3
            wide = jnp.concatenate([tap, rest], axis=1)
            for y in range(ny):
                block = wide if y == 1 else pltpu.roll(wide, (ch * (y - 1)) % rows, 1)
                if y == 0:
                    block = jnp.where(lane >= rows - ch, 0.0, block)
                if y == ny - 1:
                    block = jnp.where(lane < ch, 0.0, block)
                out[a, y * ch : (y + 1) * ch, c * rows : (c + 1) * rows] = block.astype(BF)


def bands(first_weight, second_weight, edge, ny):
    ch = first_weight.shape[-1]
    rows = ch * ny
    return pl.pallas_call(
        functools.partial(bands_kernel, ny),
        out_shape=(pltpu.VMEM((3, rows, 3 * rows), BF),) * 3 + (pltpu.VMEM(edge.shape, BF),),
        compiler_params=params(3),
        cost_estimate=pl.CostEstimate(flops=1_000_000_000, bytes_accessed=4_000_000, transcendentals=0),
        name="bands",
    )(*in_vmem(first_weight, second_weight, edge))


def shifted_rows(out, row, block, ends, rows):
    lane = iota(block.shape, 1)
    at = slice(row * LANES, (row + 1) * LANES)
    wide = block.astype(F32)
    out[0:rows, at] = jnp.where(lane == 0, ends, pltpu.roll(wide, 1, 1)).astype(BF)
    out[rows : 2 * rows, at] = block
    out[2 * rows :, at] = jnp.where(lane == LANES - 1, ends, pltpu.roll(wide, LANES - 1, 1)).astype(BF)


def lane_to(edges, source, target):
    shift = (target - source) % LANES
    return edges if shift == 0 else pltpu.roll(edges, shift, 1)


def fold_taps(product, ch, ny):
    rows = ch * ny
    lane = iota((ch, LANES), 1)
    total = None
    for y in range(ny):
        low = max(ch * (y - 1), 0)
        high = min(ch * (y + 2), rows)
        band = product[y * ch : (y + 1) * ch]
        col = low // LANES
        turn = ch * (y - 1) % LANES
        part = lane_to(band[:, col * LANES : (col + 1) * LANES], turn, 0)
        if (high - 1) // LANES > col:
            rest = lane_to(band[:, (col + 1) * LANES : (col + 2) * LANES], turn, 0)
            part = jnp.where(lane < LANES - turn, part, rest)
        if y == 0:
            part = jnp.where(lane < ch, 0.0, part)
        if y == ny - 1:
            part = jnp.where(lane < 2 * ch, part, 0.0)
        total = part if total is None else total + part
    return total


def place_taps(columns, folded, a, c, ch):
    lane = iota(folded.shape, 1)
    for b in range(3):
        target = ch * ((a * 3 + b) * 3 + c)
        col, offset = target // LANES, target % LANES
        moved = lane_to(folded, b * ch, offset)
        columns[col] = jnp.where((lane >= offset) & (lane < offset + ch), moved, columns[col])


def bias_terms(field, ch, ny):
    nx = field.shape[1] // LANES
    wide = field.astype(F32)
    total = wide[:, 0:LANES]
    for x in range(1, nx):
        total = total + wide[:, x * LANES : (x + 1) * LANES]
    folded = total[0:ch]
    for y in range(1, ny):
        folded = folded + total[y * ch : (y + 1) * ch]
    return jnp.sum(folded, axis=1, keepdims=True)


def logistic(preact):
    return 1.0 / (1.0 + jnp.exp(-preact))


def bias_column(ref, ny):
    ch = ref.shape[1]
    r, k = iota((ch, ch), 0), iota((ch, ch), 1)
    column = jnp.sum(jnp.where(r == k, ref[...], 0.0), axis=1, keepdims=True)
    return jnp.concatenate([column] * ny, axis=0)


def end_columns(nx, sources):
    n = sources[0][3].shape[0]
    j, k = iota((LANES, n), 0), iota((LANES, n), 1)
    row, side = j % 64 // 2, j % 2
    column = jnp.where(j < 64, jnp.where(side == 0, 0, 3), jnp.where(side == 0, 4, 5))
    out = None
    for x, start, count, message in sources:
        hit = (row >= x) & (row < x + count) & (k == column * nx + row - x + start)
        part = mm(one_hot(hit), message)
        out = part if out is None else out + part
    return out


def edge_columns(nx, sources):
    n = sources[0][3].shape[0]
    j, k = iota((LANES, n), 0), iota((LANES, n), 1)
    s, xx = j // 16, j % 16
    column = jnp.where(s == 0, 2, jnp.where(s == 1, 3, jnp.where(s == 5, 0, jnp.where(s == 6, 1, jnp.where(s == 3, 5, jnp.where(s == 7, 4, -1))))))
    out = None
    for low, high, start, message in sources:
        hit = (column >= 0) & (xx >= low) & (xx < high) & (k == column * nx + xx - low + start)
        part = mm(one_hot(hit), message)
        out = part if out is None else out + part
    return out


def conv_inside(t_ref, field, out, nx):
    n, m = nx * LANES, (nx - 1) * LANES
    out[...] = mm(t_ref[1], field[:, 0:n])
    out[:, LANES:] = out[:, LANES:] + mm(t_ref[0], field[:, 0:m])
    out[:, 0:m] = out[:, 0:m] + mm(t_ref[2], field[:, LANES:n])


def gate(hidden_grad, preact, q):
    return (hidden_grad * q * (1.0 + preact * (1.0 - q))).astype(BF)


def tap_terms(upstream, taps, ch, ny):
    columns = [jnp.zeros((ch, LANES), F32) for _ in range(TERMS // LANES)]
    for a in range(3):
        for c in range(3):
            product = mm_nt(*((taps(2 - a, 2 - c), upstream) if upstream is not None else taps(a, c)))
            place_taps(columns, fold_taps(product, ch, ny), a, c, ch)
    return columns


def with_bias(columns, field, ch, ny):
    lane = iota((ch, LANES), 1)
    return columns[:-1] + [jnp.where(lane == 27 * ch % LANES, bias_terms(field, ch, ny), columns[-1])]


def inner_kernel(
    nx, ch, ny,
    t1_ref, tv_ref, f_ref, g_ref, near_ref, bias_ref,
    fs, gs, pre, grad, hid_ref, second_ref, first_ref,
):
    rows = ch * ny
    ends = end_columns(nx, ((0, 0, nx, near_ref[...]),)).T
    for src, dst, first in ((f_ref, fs, 0), (g_ref, gs, 64)):
        for x in range(nx):
            block = src[:, x * LANES : (x + 1) * LANES]
            shifted_rows(dst, x, block, lane_to(ends, first + 2 * x + 1, 0), rows)
    conv_inside(t1_ref, fs, pre, nx)
    pre[...] = pre[...] + bias_column(bias_ref, ny)
    conv_inside(tv_ref, gs, grad, nx)
    n = (nx - 2) * LANES
    inside = slice(LANES, LANES + n)
    preact = pre[:, inside]
    q = logistic(preact)
    hid_ref[...] = (preact * q).astype(BF)
    preact_grad = gate(grad[:, inside], preact, q)
    window = lambda ref, a, c: ref[c * rows : (c + 1) * rows, a * LANES : a * LANES + n]
    second = tap_terms(hid_ref[...], lambda a, c: window(gs, a, c), ch, ny)
    first = tap_terms(None, lambda a, c: (preact_grad, window(fs, a, c)), ch, ny)
    second = with_bias(second, g_ref[...], ch, ny)
    first = with_bias(first, preact_grad, ch, ny)
    for i in range(TERMS // LANES):
        at = slice(i * LANES, (i + 1) * LANES)
        second_ref[:, at] = second[i]
        first_ref[:, at] = first[i]


def inner(t1, tv, field, cot, near, bias, ch, ny):
    rows = ch * ny
    nx = field.shape[1] // LANES
    sds = pltpu.VMEM
    return pl.pallas_call(
        functools.partial(inner_kernel, nx, ch, ny),
        out_shape=(
            sds((3 * rows, nx * LANES), BF),
            sds((3 * rows, nx * LANES), BF),
            sds((rows, nx * LANES), F32),
            sds((rows, nx * LANES), F32),
            sds((rows, (nx - 2) * LANES), BF),
            sds((ch, TERMS), F32),
            sds((ch, TERMS), F32),
        ),
        compiler_params=params(6),
        cost_estimate=pl.CostEstimate(flops=2_000_000_000, bytes_accessed=4_000_000, transcendentals=0),
        name="inner",
    )(*in_vmem(t1, tv, field, cot, near, bias))


def outer_kernel(
    nx, ch, ny, scale,
    t1_ref, tv_ref, fs, gs, pre, grad, part_second_ref, part_first_ref, above_ref, below_ref, before_ref, after_ref,
    hid_ref, fe, keep_ref, give_ref,
    ge,
):
    rows = ch * ny
    columns = end_columns(nx, ((0, nx - 1, 1, before_ref[...]), (1, 0, 1, after_ref[...]))).T
    for i, dst in enumerate((fe, ge)):
        for j, src in enumerate((above_ref, below_ref)):
            block = src[(i + 1) * rows : (i + 2) * rows]
            shifted_rows(dst, j, block, lane_to(columns, 64 * i + 2 * j + 1, 0), rows)

    last = (nx - 1) * LANES
    ends = lambda ref: jnp.concatenate([ref[:, 0:LANES], ref[:, last:]], axis=1)
    both = lambda t, e: jnp.concatenate([mm(t[0], e[:, 0:LANES]), mm(t[2], e[:, LANES:])], axis=1)
    preact = ends(pre) + both(t1_ref, fe)
    q = logistic(preact)
    hid_ref[...] = (preact * q).astype(BF)
    preact_grad = gate(ends(grad) + both(tv_ref, ge), preact, q)

    def window(own, end, a, c):
        at = slice(c * rows, (c + 1) * rows)
        head = end[at, 0:LANES] if a == 0 else own[at, (a - 1) * LANES : a * LANES]
        tail = end[at, LANES:] if a == 2 else own[at, last + (a - 1) * LANES : last + a * LANES]
        return jnp.concatenate([head, tail], axis=1)

    second = tap_terms(hid_ref[...], lambda a, c: window(gs, ge, a, c), ch, ny)
    first = tap_terms(None, lambda a, c: (preact_grad, window(fs, fe, a, c)), ch, ny)
    first = with_bias(first, preact_grad, ch, ny)
    mine = is_even("smp")
    for i in range(TERMS // LANES):
        at = slice(i * LANES, (i + 1) * LANES)
        part_second = (second[i] + part_second_ref[:, at]) * scale
        part_first = (first[i] + part_first_ref[:, at]) * scale
        keep_ref[:, at] = jnp.where(mine, part_second, part_first)
        give_ref[:, at] = jnp.where(mine, part_first, part_second)


def outer(t1, tv, fs, gs, pre, grad, second, first, above, below, before, after, ch, ny, scale):
    rows = ch * ny
    nx = fs.shape[1] // LANES
    sds = pltpu.VMEM
    return pl.pallas_call(
        functools.partial(outer_kernel, nx, ch, ny, scale),
        out_shape=(
            sds((rows, 2 * LANES), BF),
            sds((3 * rows, 2 * LANES), BF),
            sds((ch, TERMS), F32),
            sds((ch, TERMS), F32),
        ),
        scratch_shapes=[pltpu.VMEM((3 * rows, 2 * LANES), BF)],
        compiler_params=params(6),
        name="outer",
    )(*in_vmem(t1, tv, fs, gs, pre, grad, second, first, above, below, before, after))


def rim_kernel(
    nx, ch, ny,
    t1_ref, h_ref, h_end_ref, fs_ref, fe_ref, f_ref, above_ref, below_ref, near_ref, before_ref, after_ref, bias_ref,
    hs,
    ends,
):
    rows = ch * ny
    above, below = above_ref[0:rows], below_ref[0:rows]
    sources = ((2, nx + 2, 0, near_ref[...]), (0, 2, nx - 2, before_ref[...]), (nx + 2, nx + 4, 0, after_ref[...]))
    edges_t = edge_columns(nx, sources)
    end = fe_ref[rows : 2 * rows]
    unshifted = [above, end[:, 0:LANES], *(f_ref[:, x * LANES : (x + 1) * LANES] for x in range(nx)), end[:, LANES:], below]
    j, k = iota((LANES, LANES), 0), iota((LANES, LANES), 1)
    own_end = jnp.where(j // 16 == 2, 0, jnp.where(j // 16 == 4, LANES - 1, -1))
    for x in range(nx + 4):
        edges_t = edges_t + mm_nt(one_hot((j % 16 == x) & (k == own_end)), unshifted[x])
    edges = edges_t.T
    lane = iota((rows, LANES), 1)
    both = lambda left, right: jnp.where(lane == 0, lane_to(edges, left, 0), lane_to(edges, right, LANES - 1))
    shifted_rows(ends, 0, above, both(16, 80), rows)
    shifted_rows(ends, 1, below, both(16 + nx + 3, 80 + nx + 3), rows)
    acc = None
    row = lambda x: fs_ref[:, x * LANES : (x + 1) * LANES]
    pairs = ((ends[:, 0:LANES], row(nx - 1)), (fe_ref[:, 0:LANES], fe_ref[:, LANES:]), (row(0), ends[:, LANES:]))
    for a in range(3):
        columns = [lane_to(edges, 16 * c + a, 0).astype(BF) for c in range(3)]
        term = mm(t1_ref[a], jnp.concatenate([*pairs[a], jnp.concatenate(columns, axis=0)], axis=1))
        acc = term if acc is None else acc + term
    preact = acc + bias_column(bias_ref, ny)
    hidden = (preact * logistic(preact)).astype(BF)
    outer = hidden[:, 2 * LANES :].astype(F32)
    for x in range(nx + 2):
        if x == 0:
            block = hidden[:, 0:LANES]
        elif x == nx + 1:
            block = hidden[:, LANES : 2 * LANES]
        elif x == 1:
            block = h_end_ref[:, 0:LANES]
        elif x == nx:
            block = h_end_ref[:, LANES:]
        else:
            block = h_ref[:, (x - 2) * LANES : (x - 1) * LANES]
        shifted_rows(hs, x, block, jnp.where(lane == 0, lane_to(outer, x, 0), lane_to(outer, 64 + x, LANES - 1)), rows)


def rim(t1, hidden, hidden_end, fs, fe, field, above, below, near, before, after, bias, ch, ny):
    rows = ch * ny
    nx = field.shape[1] // LANES
    return pl.pallas_call(
        functools.partial(rim_kernel, nx, ch, ny),
        out_shape=pltpu.VMEM((3 * rows, (nx + 2) * LANES), BF),
        scratch_shapes=[pltpu.VMEM((3 * rows, 2 * LANES), BF)],
        compiler_params=params(6),
        cost_estimate=pl.CostEstimate(flops=1_000_000_000, bytes_accessed=3_000_000, transcendentals=0),
        name="rim",
    )(*in_vmem(t1, hidden, hidden_end, fs, fe, field, above, below, near, before, after, bias))


def residual_kernel(nx, ch, ny, t2_ref, hs, f_ref, bias_ref, o_ref):
    rows = ch * ny
    n = nx * LANES
    acc = mm(t2_ref[0], hs[:, 0:n])
    for a in range(1, 3):
        acc = acc + mm(t2_ref[a], hs[:, a * LANES : a * LANES + n])
    total = (f_ref[...].astype(F32) + (acc + bias_column(bias_ref, ny))).astype(BF)
    r, k = iota((rows, rows), 0), iota((rows, rows), 1)
    back = one_hot(k == (r % ny) * ch + r // ny)
    ordered = mm(back, total)
    for x in range(nx):
        o_ref[0, :, x] = ordered[:, x * LANES : (x + 1) * LANES].reshape(ch, ny, LANES).astype(BF)


def residual(t2, hs, field, bias, ch, ny):
    nx = field.shape[1] // LANES
    return pl.pallas_call(
        functools.partial(residual_kernel, nx, ch, ny),
        out_shape=jax.ShapeDtypeStruct((1, ch, nx, ny, LANES), BF),
        compiler_params=params(6),
        cost_estimate=pl.CostEstimate(flops=3_000_000_000, bytes_accessed=3_000_000, transcendentals=0),
        name="residual",
    )(*in_vmem(t2, hs, field, bias))


def moved(array, sizes, step):
    ns, nx, nz = sizes
    pairs = []
    for s in range(ns):
        for x in range(nx):
            for z in range(nz):
                t, u, v = step(s, x, z)
                pairs.append(((s * nx + x) * nz + z, (t * nx + u) * nz + v))
    return lax.ppermute(array, AXES, pairs)


def along(array, sizes, dx, dz=0):
    ns, nx, nz = sizes
    return moved(array, sizes, lambda s, x, z: (s, (x + dx) % nx, (z + dz) % nz))


def swapped(array, sizes, bits):
    return moved(array, sizes, lambda s, x, z: (s ^ bits[0], x ^ bits[1], z ^ bits[2]))


def add_kernel(n_in, *refs):
    terms = [ref[...].astype(F32) for ref in refs[:n_in]]
    out = refs[n_in]
    while len(terms) > 1:
        terms = [terms[i] + terms[i + 1] for i in range(0, len(terms), 2)]
    total = terms[0]
    n = total.shape[1] - LANES
    out[:, :n] = total[:, :n].astype(out.dtype)
    tail = total[:, n:]
    lane = iota(tail.shape, 1)
    spare = 864 % LANES
    joined = tail + pltpu.roll(tail, LANES - 1, 1)
    if out.dtype == BF:
        low = joined - joined.astype(BF).astype(F32)
        tail = jnp.where(lane == spare + 1, pltpu.roll(low, 1, 1), tail)
    out[:, n:] = jnp.where(lane == spare, joined, tail).astype(out.dtype)


def add(terms, dtype):
    return pl.pallas_call(
        functools.partial(add_kernel, len(terms)),
        out_shape=pltpu.VMEM(terms[0].shape, dtype),
        compiler_params=params(1),
        name="add",
    )(*in_vmem(*terms))


def exchange(sent, sizes, pair):
    steps = [(0, 0, 0)]
    for bits in pair:
        steps = steps + [tuple(p ^ q for p, q in zip(bits, step)) for step in steps]
    return [sent] + [swapped(sent, sizes, step) for step in steps[1:]]


def sum_all(keep, give, sizes, hs, finish):
    near = (1, 0, 0)
    bits = [(0, 1 << i, 0) for i in range(sizes[1].bit_length() - 1)]
    flat = [(0, 0, 1 << i) for i in range(sizes[2].bit_length() - 1)]
    flat += [(1 << i, 0, 0) for i in range(1, sizes[0].bit_length() - 1)]
    groups = [flat[i : i + 2] for i in range(0, len(flat), 2)] + [bits[i : i + 2] for i in range(0, len(bits), 2)]
    terms = [keep, swapped(give, sizes, near)]
    output = None
    for i, group in enumerate(groups):
        terms = exchange(add(terms, BF), sizes, group)
        if i == 0:
            *terms, hs = lax.optimization_barrier((*terms, hs))
            output = finish(hs)
        elif i == 1:
            *terms, output = lax.optimization_barrier((*terms, output))
    mine = add(terms, F32)
    return mine, swapped(mine, sizes, near), output


def spread_kernel(ch, mine_ref, other_ref, first_ref, first_bias_ref, second_ref, second_bias_ref):
    even = is_even("smp")
    mine, other = mine_ref[...], other_ref[...]
    r, k = iota((ch, LANES), 0), iota((ch, LANES), 1)
    for terms, out, bias in (
        (jnp.where(even, other, mine), first_ref, first_bias_ref),
        (jnp.where(even, mine, other), second_ref, second_bias_ref),
    ):
        for tap in range(27):
            at = tap * ch
            block = terms[:, at // LANES * LANES : (at // LANES + 1) * LANES]
            out[tap // 9, tap // 3 % 3, tap % 3] = lane_to(block, at % LANES, 0)[:, :ch]
        tail = lane_to(terms[:, TERMS - LANES :], 27 * ch % LANES, 0)[:, 0:1]
        bias[...] = jnp.sum(jnp.where(r == k, tail, 0.0), axis=0, keepdims=True)[:, :ch]


def spread(mine, other, ch):
    sds = jax.ShapeDtypeStruct
    taps, bias = sds((3, 3, 3, ch, ch), F32), sds((1, ch), F32)
    first, first_bias, second, second_bias = pl.pallas_call(
        functools.partial(spread_kernel, ch),
        out_shape=(taps, bias, taps, bias),
        compiler_params=params(4),
        name="spread",
    )(*in_vmem(mine, other))
    laid = lambda grad: jnp.transpose(grad, (3, 0, 1, 2, 4))
    return laid(first), first_bias.reshape(ch), laid(second), second_bias.reshape(ch)


def shards(sizes, features, first_weight, first_bias, second_weight, second_bias, cotangent):
    ns, ngx, ngz = sizes
    _, ch, nx, ny, nz = features.shape
    assert features.shape[0] == 1 and nz == LANES and ngz == 2
    assert not any(n & (n - 1) for n in sizes) and ns > 1
    scale = float((ns * nx * ngx * ny * nz * ngz) ** -0.5)
    up, down, held, weight1, weight2 = faces(features, cotangent, first_weight, second_weight)
    above, below = along(up, sizes, 1), along(down, sizes, -1)
    field, cot, edge = pack(held)
    near = swapped(edge, sizes, (0, 0, 1))
    t1, tv, t2, edge = bands(weight1, weight2, edge, ny)
    before, after = along(edge, sizes, 1, 1), along(edge, sizes, -1, 1)
    bias1, bias2 = first_bias.reshape(1, ch), second_bias.reshape(1, ch)
    fs, gs, pre, grad, hidden, second, first = inner(t1, tv, field, cot, near, bias1, ch, ny)
    hidden_end, fe, keep, give = outer(
        t1, tv, fs, gs, pre, grad, second, first, above, below, before, after, ch, ny, scale
    )
    hs = rim(t1, hidden, hidden_end, fs, fe, field, above, below, near, before, after, bias1, ch, ny)
    mine, other, output = sum_all(keep, give, sizes, hs, lambda hs: residual(t2, hs, field, bias2, ch, ny))
    return output, *spread(mine, other, ch)


def solution(mesh):
    sizes = tuple(mesh.shape[axis] for axis in AXES)
    split = P("smp", None, "gx", None, "gz")
    return jax.shard_map(
        functools.partial(shards, sizes),
        mesh=mesh,
        in_specs=(split, P(), P(), P(), P(), split),
        out_specs=(split, P(), P(), P(), P()),
        check_vma=False,
    )
```

```python
import functools

import jax
import jax.numpy as jnp
from jax import lax
from jax.experimental import pallas as pl
from jax.experimental.pallas import tpu as pltpu
from jax.sharding import PartitionSpec as P

AXES = ("smp", "gx", "gz")
BF = jnp.bfloat16
F32 = jnp.float32
LANES = 128
TERMS = 896


def mm(a, b):
    return lax.dot_general(a, b, (((1,), (0,)), ((), ())), preferred_element_type=F32)


def mm_nt(a, b):
    return lax.dot_general(a, b, (((1,), (1,)), ((), ())), preferred_element_type=F32)


def iota(shape, dim):
    return lax.broadcasted_iota(jnp.int32, shape, dim)


def one_hot(hit):
    return jnp.where(hit, 1.0, 0.0).astype(BF)


def params(mib=8):
    return pltpu.CompilerParams(vmem_limit_bytes=mib * 2**20)


def in_vmem(*arrays):
    return [pltpu.with_memory_space_constraint(array, pltpu.VMEM) for array in arrays]


def in_hbm(*arrays):
    return [pltpu.with_memory_space_constraint(array, pltpu.HBM) for array in arrays]


def is_even(axis):
    return lax.axis_index(axis) % 2 == 0


def ordered(ch, ny):
    r, k = iota((ch * ny, ch * ny), 0), iota((ch * ny, ch * ny), 1)
    return one_hot(k == (r % ch) * ny + r // ch)


def faces_kernel(nx, ch, ny, f_any, g_any, w1_any, w2_any, up_ref, dn_ref, held, w1_ref, w2_ref, raw, sems):
    rows = ch * ny
    wanted = ((0, nx - 2), (0, nx - 1), (1, nx - 1), (0, 1), (0, 0), (1, 0))
    others = [(i, x) for x in range(nx) for i in range(2) if (i, x) not in wanted]
    copies = {
        (i, x): pltpu.make_async_copy((f_any, g_any)[i].at[0, :, x], held.at[i, x], sems.at[i * nx + x])
        for i, x in (*wanted, *others)
    }
    weights = [pltpu.make_async_copy(src, dst, sems.at[2 * nx + i]) for i, (src, dst) in enumerate(((w1_any, w1_ref), (w2_any, w2_ref)))]
    for copy in (*copies.values(), *weights):
        copy.start()
    for j, (i, x) in enumerate(wanted):
        copies[i, x].wait()
        raw[:, j * LANES : (j + 1) * LANES] = held[i, x].astype(F32).reshape(rows, LANES).astype(BF)
    out = mm(ordered(ch, ny), raw[...]).astype(BF)
    for j in range(3):
        at = slice(j * rows, (j + 1) * rows)
        up_ref[at] = out[:, j * LANES : (j + 1) * LANES]
        dn_ref[at] = out[:, (j + 3) * LANES : (j + 4) * LANES]
    for key in others:
        copies[key].wait()
    for copy in weights:
        copy.wait()


def faces(features, cotangent, first_weight, second_weight):
    _, ch, nx, ny, _ = features.shape
    rows = ch * ny
    sds = pltpu.VMEM
    laid = lambda weight: jnp.transpose(weight, (1, 2, 3, 0, 4))
    return pl.pallas_call(
        functools.partial(faces_kernel, nx, ch, ny),
        out_shape=(
            sds((3 * rows, LANES), BF),
            sds((3 * rows, LANES), BF),
            sds((2, nx, ch, ny, LANES), BF),
            sds((3, 3, 3, ch, ch), BF),
            sds((3, 3, 3, ch, ch), BF),
        ),
        in_specs=[pl.BlockSpec(memory_space=pl.ANY)] * 4,
        scratch_shapes=[pltpu.VMEM((rows, 6 * LANES), BF), pltpu.SemaphoreType.DMA((2 * nx + 2,))],
        compiler_params=params(4),
        name="faces",
    )(*in_hbm(features, cotangent, laid(first_weight), laid(second_weight)))


def pack_kernel(nx, ch, ny, held, fo_ref, go_ref, edge_ref, raw):
    rows = ch * ny
    perm = ordered(ch, ny)
    for i, dst in enumerate((fo_ref, go_ref)):
        for x in range(nx):
            raw[:, x * LANES : (x + 1) * LANES] = held[i, x].astype(F32).reshape(rows, LANES).astype(BF)
        dst[...] = mm(perm, raw[...]).astype(BF)
    n = edge_ref.shape[0]
    j, m = iota((n, nx * LANES), 0), iota((n, nx * LANES), 1)
    c, x = j // nx, j % nx
    zf = jnp.where(c < 2, c, LANES - 4 + c)
    pick_f = one_hot((c < 4) & (m == x * LANES + zf))
    zg = jnp.where(c == 4, 0, LANES - 1)
    pick_g = one_hot((c >= 4) & (c < 6) & (m == x * LANES + zg))
    edge_ref[...] = (mm_nt(pick_f, fo_ref[...]) + mm_nt(pick_g, go_ref[...])).astype(BF)


def pack(held):
    _, nx, ch, ny, _ = held.shape
    rows = ch * ny
    edge_rows = -(-6 * nx // 32) * 32
    sds = pltpu.VMEM
    return pl.pallas_call(
        functools.partial(pack_kernel, nx, ch, ny),
        out_shape=(sds((rows, nx * LANES), BF), sds((rows, nx * LANES), BF), sds((edge_rows, rows), BF)),
        scratch_shapes=[pltpu.VMEM((rows, nx * LANES), BF)],
        compiler_params=params(4),
        cost_estimate=pl.CostEstimate(flops=500_000_000, bytes_accessed=1_000_000, transcendentals=0),
        name="pack",
    )(*in_vmem(held))


def bands_kernel(ny, w1_ref, w2_ref, edge_ref, t1_ref, tv_ref, t2_ref, copy_ref):
    copy_ref[...] = edge_ref[...]
    ch = w1_ref.shape[-1]
    rows = ny * ch
    lane = iota((ch, rows), 1)
    r, k = iota((ch, LANES), 0), iota((ch, LANES), 1)
    places = [one_hot(k == r + b * ch) for b in range(3)]

    def direct(ref):
        wide = None
        for b in range(3):
            part = mm(ref[:, b].reshape(9 * ch, ch), places[b])
            wide = part if wide is None else wide + part
        return [wide[i * ch : (i + 1) * ch] for i in range(9)]

    def flipped(ref):
        none = jnp.zeros((ch, ch), BF)
        stack = [ref[2 - a, 2 - b, 2 - c] if b < 3 else none for a in range(3) for c in range(3) for b in range(4)]
        wide = mm_nt(one_hot(r == k)[:, :ch], jnp.concatenate(stack, axis=0))
        return [wide[:, i * LANES : (i + 1) * LANES] for i in range(9)]

    rest = jnp.zeros((ch, rows - LANES), F32)
    for taps, out in ((direct(w1_ref), t1_ref), (flipped(w2_ref), tv_ref), (direct(w2_ref), t2_ref)):
        for i, tap in enumerate(taps):
            a, c = i // 3, i % 3
            wide = jnp.concatenate([tap, rest], axis=1)
            for y in range(ny):
                block = wide if y == 1 else pltpu.roll(wide, (ch * (y - 1)) % rows, 1)
                if y == 0:
                    block = jnp.where(lane >= rows - ch, 0.0, block)
                if y == ny - 1:
                    block = jnp.where(lane < ch, 0.0, block)
                out[a, y * ch : (y + 1) * ch, c * rows : (c + 1) * rows] = block.astype(BF)


def bands(first_weight, second_weight, edge, ny):
    ch = first_weight.shape[-1]
    rows = ch * ny
    return pl.pallas_call(
        functools.partial(bands_kernel, ny),
        out_shape=(pltpu.VMEM((3, rows, 3 * rows), BF),) * 3 + (pltpu.VMEM(edge.shape, BF),),
        compiler_params=params(3),
        cost_estimate=pl.CostEstimate(flops=1_000_000_000, bytes_accessed=4_000_000, transcendentals=0),
        name="bands",
    )(*in_vmem(first_weight, second_weight, edge))


def shifted_rows(out, row, block, ends, rows):
    lane = iota(block.shape, 1)
    at = slice(row * LANES, (row + 1) * LANES)
    wide = block.astype(F32)
    out[0:rows, at] = jnp.where(lane == 0, ends, pltpu.roll(wide, 1, 1)).astype(BF)
    out[rows : 2 * rows, at] = block
    out[2 * rows :, at] = jnp.where(lane == LANES - 1, ends, pltpu.roll(wide, LANES - 1, 1)).astype(BF)


def lane_to(edges, source, target):
    shift = (target - source) % LANES
    return edges if shift == 0 else pltpu.roll(edges, shift, 1)


def fold_taps(product, ch, ny):
    rows = ch * ny
    lane = iota((ch, LANES), 1)
    total = None
    for y in range(ny):
        low = max(ch * (y - 1), 0)
        high = min(ch * (y + 2), rows)
        band = product[y * ch : (y + 1) * ch]
        col = low // LANES
        turn = ch * (y - 1) % LANES
        part = lane_to(band[:, col * LANES : (col + 1) * LANES], turn, 0)
        if (high - 1) // LANES > col:
            rest = lane_to(band[:, (col + 1) * LANES : (col + 2) * LANES], turn, 0)
            part = jnp.where(lane < LANES - turn, part, rest)
        if y == 0:
            part = jnp.where(lane < ch, 0.0, part)
        if y == ny - 1:
            part = jnp.where(lane < 2 * ch, part, 0.0)
        total = part if total is None else total + part
    return total


def place_taps(columns, folded, a, c, ch):
    lane = iota(folded.shape, 1)
    for b in range(3):
        target = ch * ((a * 3 + b) * 3 + c)
        col, offset = target // LANES, target % LANES
        moved = lane_to(folded, b * ch, offset)
        columns[col] = jnp.where((lane >= offset) & (lane < offset + ch), moved, columns[col])


def bias_terms(field, ch, ny):
    nx = field.shape[1] // LANES
    wide = field.astype(F32)
    total = wide[:, 0:LANES]
    for x in range(1, nx):
        total = total + wide[:, x * LANES : (x + 1) * LANES]
    folded = total[0:ch]
    for y in range(1, ny):
        folded = folded + total[y * ch : (y + 1) * ch]
    return jnp.sum(folded, axis=1, keepdims=True)


def logistic(preact):
    return 1.0 / (1.0 + jnp.exp(-preact))


def bias_column(ref, ny):
    ch = ref.shape[1]
    r, k = iota((ch, ch), 0), iota((ch, ch), 1)
    column = jnp.sum(jnp.where(r == k, ref[...], 0.0), axis=1, keepdims=True)
    return jnp.concatenate([column] * ny, axis=0)


def sides(one, two):
    even = is_even("gx")
    return jnp.where(even, two, one), jnp.where(even, one, two)


def end_columns(nx, sources):
    n = sources[0][3].shape[0]
    j, k = iota((LANES, n), 0), iota((LANES, n), 1)
    row, side = j % 64 // 2, j % 2
    column = jnp.where(j < 64, jnp.where(side == 0, 0, 3), jnp.where(side == 0, 4, 5))
    out = None
    for x, start, count, message in sources:
        hit = (row >= x) & (row < x + count) & (k == column * nx + row - x + start)
        part = mm(one_hot(hit), message)
        out = part if out is None else out + part
    return out


def edge_columns(nx, sources):
    n = sources[0][3].shape[0]
    j, k = iota((LANES, n), 0), iota((LANES, n), 1)
    s, xx = j // 16, j % 16
    column = jnp.where(s == 0, 2, jnp.where(s == 1, 3, jnp.where(s == 5, 0, jnp.where(s == 6, 1, jnp.where(s == 3, 5, jnp.where(s == 7, 4, -1))))))
    out = None
    for low, high, start, message in sources:
        hit = (column >= 0) & (xx >= low) & (xx < high) & (k == column * nx + xx - low + start)
        part = mm(one_hot(hit), message)
        out = part if out is None else out + part
    return out


def conv_inside(t_ref, field, out, nx):
    n, m = nx * LANES, (nx - 1) * LANES
    out[...] = mm(t_ref[1], field[:, 0:n])
    out[:, LANES:] = out[:, LANES:] + mm(t_ref[0], field[:, 0:m])
    out[:, 0:m] = out[:, 0:m] + mm(t_ref[2], field[:, LANES:n])


def gate(hidden_grad, preact, q):
    return (hidden_grad * q * (1.0 + preact * (1.0 - q))).astype(BF)


def tap_terms(upstream, taps, ch, ny):
    columns = [jnp.zeros((ch, LANES), F32) for _ in range(TERMS // LANES)]
    for a in range(3):
        for c in range(3):
            product = mm_nt(*((taps(2 - a, 2 - c), upstream) if upstream is not None else taps(a, c)))
            place_taps(columns, fold_taps(product, ch, ny), a, c, ch)
    return columns


def with_bias(columns, field, ch, ny):
    lane = iota((ch, LANES), 1)
    return columns[:-1] + [jnp.where(lane == 27 * ch % LANES, bias_terms(field, ch, ny), columns[-1])]


def inner_kernel(
    nx, ch, ny,
    t1_ref, tv_ref, f_ref, g_ref, near_ref, bias_ref,
    fs, gs, pre, grad, hid_ref, second_ref, first_ref,
):
    rows = ch * ny
    ends = end_columns(nx, ((0, 0, nx, near_ref[...]),)).T
    for src, dst, first in ((f_ref, fs, 0), (g_ref, gs, 64)):
        for x in range(nx):
            block = src[:, x * LANES : (x + 1) * LANES]
            shifted_rows(dst, x, block, lane_to(ends, first + 2 * x + 1, 0), rows)
    conv_inside(t1_ref, fs, pre, nx)
    pre[...] = pre[...] + bias_column(bias_ref, ny)
    conv_inside(tv_ref, gs, grad, nx)
    n = (nx - 2) * LANES
    inside = slice(LANES, LANES + n)
    preact = pre[:, inside]
    q = logistic(preact)
    hid_ref[...] = (preact * q).astype(BF)
    preact_grad = gate(grad[:, inside], preact, q)
    window = lambda ref, a, c: ref[c * rows : (c + 1) * rows, a * LANES : a * LANES + n]
    second = tap_terms(hid_ref[...], lambda a, c: window(gs, a, c), ch, ny)
    first = tap_terms(None, lambda a, c: (preact_grad, window(fs, a, c)), ch, ny)
    second = with_bias(second, g_ref[...], ch, ny)
    first = with_bias(first, preact_grad, ch, ny)
    for i in range(TERMS // LANES):
        at = slice(i * LANES, (i + 1) * LANES)
        second_ref[:, at] = second[i]
        first_ref[:, at] = first[i]


def inner(t1, tv, field, cot, near, bias, ch, ny):
    rows = ch * ny
    nx = field.shape[1] // LANES
    sds = pltpu.VMEM
    return pl.pallas_call(
        functools.partial(inner_kernel, nx, ch, ny),
        out_shape=(
            sds((3 * rows, nx * LANES), BF),
            sds((3 * rows, nx * LANES), BF),
            sds((rows, nx * LANES), F32),
            sds((rows, nx * LANES), F32),
            sds((rows, (nx - 2) * LANES), BF),
            sds((ch, TERMS), F32),
            sds((ch, TERMS), F32),
        ),
        compiler_params=params(6),
        cost_estimate=pl.CostEstimate(flops=1000, bytes_accessed=1000, transcendentals=0),
        name="inner",
    )(*in_vmem(t1, tv, field, cot, near, bias))


def corners_kernel(nx, one_ref, two_ref, columns_ref):
    before, after = sides(one_ref[...], two_ref[...])
    columns_ref[...] = end_columns(nx, ((0, nx - 1, 1, before), (1, 0, 1, after))).T


def corners(one, two, nx):
    return pl.pallas_call(
        functools.partial(corners_kernel, nx),
        out_shape=pltpu.VMEM((one.shape[1], LANES), F32),
        compiler_params=params(1),
        name="corners",
    )(*in_vmem(one, two))


def outer_kernel(
    nx, ch, ny, scale,
    t1_ref, tv_ref, fs, gs, pre, grad, part_second_ref, part_first_ref, above_ref, below_ref, columns_ref,
    hid_ref, fe, keep_ref, give_ref,
    ge,
):
    rows = ch * ny
    columns = columns_ref[...]
    for i, dst in enumerate((fe, ge)):
        for j, src in enumerate((above_ref, below_ref)):
            block = src[(i + 1) * rows : (i + 2) * rows]
            shifted_rows(dst, j, block, lane_to(columns, 64 * i + 2 * j + 1, 0), rows)

    last = (nx - 1) * LANES
    ends = lambda ref: jnp.concatenate([ref[:, 0:LANES], ref[:, last:]], axis=1)
    both = lambda t, e: jnp.concatenate([mm(t[0], e[:, 0:LANES]), mm(t[2], e[:, LANES:])], axis=1)
    preact = ends(pre) + both(t1_ref, fe)
    q = logistic(preact)
    hid_ref[...] = (preact * q).astype(BF)
    preact_grad = gate(ends(grad) + both(tv_ref, ge), preact, q)

    def window(own, end, a, c):
        at = slice(c * rows, (c + 1) * rows)
        head = end[at, 0:LANES] if a == 0 else own[at, (a - 1) * LANES : a * LANES]
        tail = end[at, LANES:] if a == 2 else own[at, last + (a - 1) * LANES : last + a * LANES]
        return jnp.concatenate([head, tail], axis=1)

    second = tap_terms(hid_ref[...], lambda a, c: window(gs, ge, a, c), ch, ny)
    first = tap_terms(None, lambda a, c: (preact_grad, window(fs, fe, a, c)), ch, ny)
    first = with_bias(first, preact_grad, ch, ny)
    mine = is_even("smp")
    for i in range(TERMS // LANES):
        at = slice(i * LANES, (i + 1) * LANES)
        part_second = (second[i] + part_second_ref[:, at]) * scale
        part_first = (first[i] + part_first_ref[:, at]) * scale
        keep_ref[:, at] = jnp.where(mine, part_second, part_first)
        give_ref[:, at] = jnp.where(mine, part_first, part_second)


def outer(t1, tv, fs, gs, pre, grad, second, first, above, below, columns, ch, ny, scale):
    rows = ch * ny
    nx = fs.shape[1] // LANES
    sds = pltpu.VMEM
    return pl.pallas_call(
        functools.partial(outer_kernel, nx, ch, ny, scale),
        out_shape=(
            sds((rows, 2 * LANES), BF),
            sds((3 * rows, 2 * LANES), BF),
            sds((ch, TERMS), F32),
            sds((ch, TERMS), F32),
        ),
        scratch_shapes=[pltpu.VMEM((3 * rows, 2 * LANES), BF)],
        compiler_params=params(6),
        name="outer",
    )(*in_vmem(t1, tv, fs, gs, pre, grad, second, first, above, below, columns))


def rim_kernel(
    nx, ch, ny,
    t1_ref, h_ref, h_end_ref, fs_ref, fe_ref, f_ref, above_ref, below_ref, near_ref, corner_one_ref, corner_two_ref, bias_ref,
    hs,
    ends,
):
    rows = ch * ny
    above, below = above_ref[0:rows], below_ref[0:rows]
    before, after = sides(corner_one_ref[...], corner_two_ref[...])
    sources = ((2, nx + 2, 0, near_ref[...]), (0, 2, nx - 2, before), (nx + 2, nx + 4, 0, after))
    edges_t = edge_columns(nx, sources)
    end = fe_ref[rows : 2 * rows]
    unshifted = [above, end[:, 0:LANES], *(f_ref[:, x * LANES : (x + 1) * LANES] for x in range(nx)), end[:, LANES:], below]
    j, k = iota((LANES, LANES), 0), iota((LANES, LANES), 1)
    own_end = jnp.where(j // 16 == 2, 0, jnp.where(j // 16 == 4, LANES - 1, -1))
    for x in range(nx + 4):
        edges_t = edges_t + mm_nt(one_hot((j % 16 == x) & (k == own_end)), unshifted[x])
    edges = edges_t.T
    lane = iota((rows, LANES), 1)
    both = lambda left, right: jnp.where(lane == 0, lane_to(edges, left, 0), lane_to(edges, right, LANES - 1))
    shifted_rows(ends, 0, above, both(16, 80), rows)
    shifted_rows(ends, 1, below, both(16 + nx + 3, 80 + nx + 3), rows)
    acc = None
    row = lambda x: fs_ref[:, x * LANES : (x + 1) * LANES]
    pairs = ((ends[:, 0:LANES], row(nx - 1)), (fe_ref[:, 0:LANES], fe_ref[:, LANES:]), (row(0), ends[:, LANES:]))
    for a in range(3):
        columns = [lane_to(edges, 16 * c + a, 0).astype(BF) for c in range(3)]
        term = mm(t1_ref[a], jnp.concatenate([*pairs[a], jnp.concatenate(columns, axis=0)], axis=1))
        acc = term if acc is None else acc + term
    preact = acc + bias_column(bias_ref, ny)
    hidden = (preact * logistic(preact)).astype(BF)
    outer = hidden[:, 2 * LANES :].astype(F32)
    for x in range(nx + 2):
        if x == 0:
            block = hidden[:, 0:LANES]
        elif x == nx + 1:
            block = hidden[:, LANES : 2 * LANES]
        elif x == 1:
            block = h_end_ref[:, 0:LANES]
        elif x == nx:
            block = h_end_ref[:, LANES:]
        else:
            block = h_ref[:, (x - 2) * LANES : (x - 1) * LANES]
        shifted_rows(hs, x, block, jnp.where(lane == 0, lane_to(outer, x, 0), lane_to(outer, 64 + x, LANES - 1)), rows)


def rim(t1, hidden, hidden_end, fs, fe, field, above, below, near, corner_one, corner_two, bias, ch, ny):
    rows = ch * ny
    nx = field.shape[1] // LANES
    return pl.pallas_call(
        functools.partial(rim_kernel, nx, ch, ny),
        out_shape=pltpu.VMEM((3 * rows, (nx + 2) * LANES), BF),
        scratch_shapes=[pltpu.VMEM((3 * rows, 2 * LANES), BF)],
        compiler_params=params(6),
        cost_estimate=pl.CostEstimate(flops=1_000_000_000, bytes_accessed=3_000_000, transcendentals=0),
        name="rim",
    )(*in_vmem(t1, hidden, hidden_end, fs, fe, field, above, below, near, corner_one, corner_two, bias))


def residual_kernel(nx, ch, ny, t2_ref, hs, f_ref, bias_ref, o_ref):
    rows = ch * ny
    n = nx * LANES
    acc = mm(t2_ref[0], hs[:, 0:n])
    for a in range(1, 3):
        acc = acc + mm(t2_ref[a], hs[:, a * LANES : a * LANES + n])
    total = (f_ref[...].astype(F32) + (acc + bias_column(bias_ref, ny))).astype(BF)
    r, k = iota((rows, rows), 0), iota((rows, rows), 1)
    back = one_hot(k == (r % ny) * ch + r // ny)
    ordered = mm(back, total)
    for x in range(nx):
        o_ref[0, :, x] = ordered[:, x * LANES : (x + 1) * LANES].reshape(ch, ny, LANES).astype(BF)


def residual(t2, hs, field, bias, ch, ny):
    nx = field.shape[1] // LANES
    return pl.pallas_call(
        functools.partial(residual_kernel, nx, ch, ny),
        out_shape=jax.ShapeDtypeStruct((1, ch, nx, ny, LANES), BF),
        compiler_params=params(6),
        cost_estimate=pl.CostEstimate(flops=3_000_000_000, bytes_accessed=3_000_000, transcendentals=0),
        name="residual",
    )(*in_vmem(t2, hs, field, bias))


def moved(array, sizes, step):
    ns, nx, nz = sizes
    pairs = []
    for s in range(ns):
        for x in range(nx):
            for z in range(nz):
                t, u, v = step(s, x, z)
                pairs.append(((s * nx + x) * nz + z, (t * nx + u) * nz + v))
    return lax.ppermute(array, AXES, pairs)


def diagonal(array, sizes, turn):
    ns, nx, nz = sizes
    return moved(array, sizes, lambda s, x, z: (s, (x + (1 if x % 2 == turn else -1)) % nx, (z + 1) % nz))


def along(array, sizes, dx, dz=0):
    ns, nx, nz = sizes
    return moved(array, sizes, lambda s, x, z: (s, (x + dx) % nx, (z + dz) % nz))


def swapped(array, sizes, bits):
    return moved(array, sizes, lambda s, x, z: (s ^ bits[0], x ^ bits[1], z ^ bits[2]))


def add_kernel(n_in, *refs):
    terms = [ref[...].astype(F32) for ref in refs[:n_in]]
    out = refs[n_in]
    while len(terms) > 1:
        terms = [terms[i] + terms[i + 1] for i in range(0, len(terms), 2)]
    total = terms[0]
    n = total.shape[1] - LANES
    out[:, :n] = total[:, :n].astype(out.dtype)
    tail = total[:, n:]
    lane = iota(tail.shape, 1)
    spare = 864 % LANES
    joined = tail + pltpu.roll(tail, LANES - 1, 1)
    if out.dtype == BF:
        low = joined - joined.astype(BF).astype(F32)
        tail = jnp.where(lane == spare + 1, pltpu.roll(low, 1, 1), tail)
    out[:, n:] = jnp.where(lane == spare, joined, tail).astype(out.dtype)


def add(terms, dtype):
    return pl.pallas_call(
        functools.partial(add_kernel, len(terms)),
        out_shape=pltpu.VMEM(terms[0].shape, dtype),
        compiler_params=params(1),
        name="add",
    )(*in_vmem(*terms))


def exchange(sent, sizes, pair):
    steps = [(0, 0, 0)]
    for bits in pair:
        steps = steps + [tuple(p ^ q for p, q in zip(bits, step)) for step in steps]
    return [sent] + [swapped(sent, sizes, step) for step in steps[1:]]


def sum_all(keep, give, sizes, hs, finish):
    near = (1, 0, 0)
    bits = [(0, 1 << i, 0) for i in range(sizes[1].bit_length() - 1)]
    flat = [(0, 0, 1 << i) for i in range(sizes[2].bit_length() - 1)]
    flat += [(1 << i, 0, 0) for i in range(1, sizes[0].bit_length() - 1)]
    groups = [flat[i : i + 2] for i in range(0, len(flat), 2)] + [bits[i : i + 2] for i in range(0, len(bits), 2)]
    terms = [keep, swapped(give, sizes, near)]
    output = None
    for i, group in enumerate(groups):
        terms = exchange(add(terms, BF), sizes, group)
        if i == 0:
            *terms, hs = lax.optimization_barrier((*terms, hs))
            output = finish(hs)
        elif i == 1:
            *terms, output = lax.optimization_barrier((*terms, output))
    mine = add(terms, F32)
    return mine, swapped(mine, sizes, near), output


def spread_kernel(ch, mine_ref, other_ref, first_ref, first_bias_ref, second_ref, second_bias_ref):
    even = is_even("smp")
    mine, other = mine_ref[...], other_ref[...]
    r, k = iota((ch, LANES), 0), iota((ch, LANES), 1)
    for terms, out, bias in (
        (jnp.where(even, other, mine), first_ref, first_bias_ref),
        (jnp.where(even, mine, other), second_ref, second_bias_ref),
    ):
        for tap in range(27):
            at = tap * ch
            block = terms[:, at // LANES * LANES : (at // LANES + 1) * LANES]
            out[tap // 9, tap // 3 % 3, tap % 3] = lane_to(block, at % LANES, 0)[:, :ch]
        tail = lane_to(terms[:, TERMS - LANES :], 27 * ch % LANES, 0)[:, 0:1]
        bias[...] = jnp.sum(jnp.where(r == k, tail, 0.0), axis=0, keepdims=True)[:, :ch]


def spread(mine, other, ch):
    sds = jax.ShapeDtypeStruct
    taps, bias = sds((3, 3, 3, ch, ch), F32), sds((1, ch), F32)
    first, first_bias, second, second_bias = pl.pallas_call(
        functools.partial(spread_kernel, ch),
        out_shape=(taps, bias, taps, bias),
        compiler_params=params(4),
        name="spread",
    )(*in_vmem(mine, other))
    laid = lambda grad: jnp.transpose(grad, (3, 0, 1, 2, 4))
    return laid(first), first_bias.reshape(ch), laid(second), second_bias.reshape(ch)


def shards(sizes, features, first_weight, first_bias, second_weight, second_bias, cotangent):
    ns, ngx, ngz = sizes
    _, ch, nx, ny, nz = features.shape
    assert features.shape[0] == 1 and nz == LANES and ngz == 2 and ngx % 2 == 0
    assert not any(n & (n - 1) for n in sizes) and ns > 1
    scale = float((ns * nx * ngx * ny * nz * ngz) ** -0.5)
    up, down, held, weight1, weight2 = faces(features, cotangent, first_weight, second_weight)
    above, below = along(up, sizes, 1), along(down, sizes, -1)
    field, cot, edge = pack(held)
    near = swapped(edge, sizes, (0, 0, 1))
    t1, tv, t2, edge = bands(weight1, weight2, edge, ny)
    corner_two, corner_one = diagonal(edge, sizes, 1), diagonal(edge, sizes, 0)
    bias1, bias2 = first_bias.reshape(1, ch), second_bias.reshape(1, ch)
    fs, gs, pre, grad, hidden, second, first = inner(t1, tv, field, cot, near, bias1, ch, ny)
    columns = corners(corner_one, corner_two, nx)
    hidden_end, fe, keep, give = outer(
        t1, tv, fs, gs, pre, grad, second, first, above, below, columns, ch, ny, scale
    )
    hs = rim(t1, hidden, hidden_end, fs, fe, field, above, below, near, corner_one, corner_two, bias1, ch, ny)
    mine, other, output = sum_all(keep, give, sizes, hs, lambda hs: residual(t2, hs, field, bias2, ch, ny))
    return output, *spread(mine, other, ch)


def solution(mesh):
    sizes = tuple(mesh.shape[axis] for axis in AXES)
    split = P("smp", None, "gx", None, "gz")
    return jax.shard_map(
        functools.partial(shards, sizes),
        mesh=mesh,
        in_specs=(split, P(), P(), P(), P(), split),
        out_specs=(split, P(), P(), P(), P()),
        check_vma=False,
    )
```

```python
import functools

import jax
import jax.numpy as jnp
from jax import lax
from jax.experimental import pallas as pl
from jax.experimental.pallas import tpu as pltpu
from jax.sharding import PartitionSpec as P

AXES = ("smp", "gx", "gz")
BF = jnp.bfloat16
F32 = jnp.float32
LANES = 128
TERMS = 896


def mm(a, b):
    return lax.dot_general(a, b, (((1,), (0,)), ((), ())), preferred_element_type=F32)


def mm_nt(a, b):
    return lax.dot_general(a, b, (((1,), (1,)), ((), ())), preferred_element_type=F32)


def iota(shape, dim):
    return lax.broadcasted_iota(jnp.int32, shape, dim)


def one_hot(hit):
    return jnp.where(hit, 1.0, 0.0).astype(BF)


def params(mib=8):
    return pltpu.CompilerParams(vmem_limit_bytes=mib * 2**20)


def in_vmem(*arrays):
    return [pltpu.with_memory_space_constraint(array, pltpu.VMEM) for array in arrays]


def in_hbm(*arrays):
    return [pltpu.with_memory_space_constraint(array, pltpu.HBM) for array in arrays]


def is_even(axis):
    return lax.axis_index(axis) % 2 == 0


def ordered(ch, ny):
    r, k = iota((ch * ny, ch * ny), 0), iota((ch * ny, ch * ny), 1)
    return one_hot(k == (r % ch) * ny + r // ch)


def faces_kernel(nx, ch, ny, f_any, g_any, w1_any, w2_any, up_ref, dn_ref, held, w1_ref, w2_ref, raw, sems):
    rows = ch * ny
    wanted = ((0, nx - 2), (0, nx - 1), (1, nx - 1), (0, 1), (0, 0), (1, 0))
    others = [(i, x) for x in range(nx) for i in range(2) if (i, x) not in wanted]
    copies = {
        (i, x): pltpu.make_async_copy((f_any, g_any)[i].at[0, :, x], held.at[i, x], sems.at[i * nx + x])
        for i, x in (*wanted, *others)
    }
    weights = [pltpu.make_async_copy(src, dst, sems.at[2 * nx + i]) for i, (src, dst) in enumerate(((w1_any, w1_ref), (w2_any, w2_ref)))]
    for copy in (*copies.values(), *weights):
        copy.start()
    for j, (i, x) in enumerate(wanted):
        copies[i, x].wait()
        raw[:, j * LANES : (j + 1) * LANES] = held[i, x].astype(F32).reshape(rows, LANES).astype(BF)
    out = mm(ordered(ch, ny), raw[...]).astype(BF)
    for j in range(3):
        at = slice(j * rows, (j + 1) * rows)
        up_ref[at] = out[:, j * LANES : (j + 1) * LANES]
        dn_ref[at] = out[:, (j + 3) * LANES : (j + 4) * LANES]
    for key in others:
        copies[key].wait()
    for copy in weights:
        copy.wait()


def faces(features, cotangent, first_weight, second_weight):
    _, ch, nx, ny, _ = features.shape
    rows = ch * ny
    sds = pltpu.VMEM
    laid = lambda weight: jnp.transpose(weight, (1, 2, 3, 0, 4))
    return pl.pallas_call(
        functools.partial(faces_kernel, nx, ch, ny),
        out_shape=(
            sds((3 * rows, LANES), BF),
            sds((3 * rows, LANES), BF),
            sds((2, nx, ch, ny, LANES), BF),
            sds((3, 3, 3, ch, ch), BF),
            sds((3, 3, 3, ch, ch), BF),
        ),
        in_specs=[pl.BlockSpec(memory_space=pl.ANY)] * 4,
        scratch_shapes=[pltpu.VMEM((rows, 6 * LANES), BF), pltpu.SemaphoreType.DMA((2 * nx + 2,))],
        compiler_params=params(4),
        name="faces",
    )(*in_hbm(features, cotangent, laid(first_weight), laid(second_weight)))


def pack_kernel(nx, ch, ny, held, fo_ref, go_ref, edge_ref, raw):
    rows = ch * ny
    perm = ordered(ch, ny)
    for i, dst in enumerate((fo_ref, go_ref)):
        for x in range(nx):
            raw[:, x * LANES : (x + 1) * LANES] = held[i, x].astype(F32).reshape(rows, LANES).astype(BF)
        dst[...] = mm(perm, raw[...]).astype(BF)
    n = edge_ref.shape[0]
    j, m = iota((n, nx * LANES), 0), iota((n, nx * LANES), 1)
    c, x = j // nx, j % nx
    zf = jnp.where(c < 2, c, LANES - 4 + c)
    pick_f = one_hot((c < 4) & (m == x * LANES + zf))
    zg = jnp.where(c == 4, 0, LANES - 1)
    pick_g = one_hot((c >= 4) & (c < 6) & (m == x * LANES + zg))
    edge_ref[...] = (mm_nt(pick_f, fo_ref[...]) + mm_nt(pick_g, go_ref[...])).astype(BF)


def pack(held):
    _, nx, ch, ny, _ = held.shape
    rows = ch * ny
    edge_rows = -(-6 * nx // 32) * 32
    sds = pltpu.VMEM
    return pl.pallas_call(
        functools.partial(pack_kernel, nx, ch, ny),
        out_shape=(sds((rows, nx * LANES), BF), sds((rows, nx * LANES), BF), sds((edge_rows, rows), BF)),
        scratch_shapes=[pltpu.VMEM((rows, nx * LANES), BF)],
        compiler_params=params(4),
        cost_estimate=pl.CostEstimate(flops=500_000_000, bytes_accessed=1_000_000, transcendentals=0),
        name="pack",
    )(*in_vmem(held))


def bands_kernel(ny, w1_ref, w2_ref, edge_ref, t1_ref, tv_ref, t2_ref, copy_ref):
    copy_ref[...] = edge_ref[...]
    ch = w1_ref.shape[-1]
    rows = ny * ch
    lane = iota((ch, rows), 1)
    r, k = iota((ch, LANES), 0), iota((ch, LANES), 1)
    places = [one_hot(k == r + b * ch) for b in range(3)]

    def direct(ref):
        wide = None
        for b in range(3):
            part = mm(ref[:, b].reshape(9 * ch, ch), places[b])
            wide = part if wide is None else wide + part
        return [wide[i * ch : (i + 1) * ch] for i in range(9)]

    def flipped(ref):
        none = jnp.zeros((ch, ch), BF)
        stack = [ref[2 - a, 2 - b, 2 - c] if b < 3 else none for a in range(3) for c in range(3) for b in range(4)]
        wide = mm_nt(one_hot(r == k)[:, :ch], jnp.concatenate(stack, axis=0))
        return [wide[:, i * LANES : (i + 1) * LANES] for i in range(9)]

    rest = jnp.zeros((ch, rows - LANES), F32)
    for taps, out in ((direct(w1_ref), t1_ref), (flipped(w2_ref), tv_ref), (direct(w2_ref), t2_ref)):
        for i, tap in enumerate(taps):
            a, c = i // 3, i % 3
            wide = jnp.concatenate([tap, rest], axis=1)
            for y in range(ny):
                block = wide if y == 1 else pltpu.roll(wide, (ch * (y - 1)) % rows, 1)
                if y == 0:
                    block = jnp.where(lane >= rows - ch, 0.0, block)
                if y == ny - 1:
                    block = jnp.where(lane < ch, 0.0, block)
                out[a, y * ch : (y + 1) * ch, c * rows : (c + 1) * rows] = block.astype(BF)


def bands(first_weight, second_weight, edge, ny):
    ch = first_weight.shape[-1]
    rows = ch * ny
    return pl.pallas_call(
        functools.partial(bands_kernel, ny),
        out_shape=(pltpu.VMEM((3, rows, 3 * rows), BF),) * 3 + (pltpu.VMEM(edge.shape, BF),),
        compiler_params=params(3),
        cost_estimate=pl.CostEstimate(flops=1_000_000_000, bytes_accessed=4_000_000, transcendentals=0),
        name="bands",
    )(*in_vmem(first_weight, second_weight, edge))


def shifted_rows(out, row, block, ends, rows):
    lane = iota(block.shape, 1)
    at = slice(row * LANES, (row + 1) * LANES)
    wide = block.astype(F32)
    out[0:rows, at] = jnp.where(lane == 0, ends, pltpu.roll(wide, 1, 1)).astype(BF)
    out[rows : 2 * rows, at] = block
    out[2 * rows :, at] = jnp.where(lane == LANES - 1, ends, pltpu.roll(wide, LANES - 1, 1)).astype(BF)


def lane_to(edges, source, target):
    shift = (target - source) % LANES
    return edges if shift == 0 else pltpu.roll(edges, shift, 1)


def fold_taps(product, ch, ny):
    rows = ch * ny
    lane = iota((ch, LANES), 1)
    total = None
    for y in range(ny):
        low = max(ch * (y - 1), 0)
        high = min(ch * (y + 2), rows)
        band = product[y * ch : (y + 1) * ch]
        col = low // LANES
        turn = ch * (y - 1) % LANES
        part = lane_to(band[:, col * LANES : (col + 1) * LANES], turn, 0)
        if (high - 1) // LANES > col:
            rest = lane_to(band[:, (col + 1) * LANES : (col + 2) * LANES], turn, 0)
            part = jnp.where(lane < LANES - turn, part, rest)
        if y == 0:
            part = jnp.where(lane < ch, 0.0, part)
        if y == ny - 1:
            part = jnp.where(lane < 2 * ch, part, 0.0)
        total = part if total is None else total + part
    return total


def place_taps(columns, folded, a, c, ch):
    lane = iota(folded.shape, 1)
    for b in range(3):
        target = ch * ((a * 3 + b) * 3 + c)
        col, offset = target // LANES, target % LANES
        moved = lane_to(folded, b * ch, offset)
        columns[col] = jnp.where((lane >= offset) & (lane < offset + ch), moved, columns[col])


def bias_terms(field, ch, ny):
    nx = field.shape[1] // LANES
    wide = field.astype(F32)
    total = wide[:, 0:LANES]
    for x in range(1, nx):
        total = total + wide[:, x * LANES : (x + 1) * LANES]
    folded = total[0:ch]
    for y in range(1, ny):
        folded = folded + total[y * ch : (y + 1) * ch]
    return jnp.sum(folded, axis=1, keepdims=True)


def logistic(preact):
    return 1.0 / (1.0 + jnp.exp(-preact))


def bias_column(ref, ny):
    ch = ref.shape[1]
    r, k = iota((ch, ch), 0), iota((ch, ch), 1)
    column = jnp.sum(jnp.where(r == k, ref[...], 0.0), axis=1, keepdims=True)
    return jnp.concatenate([column] * ny, axis=0)


def sides(one, two):
    even = is_even("gx")
    return jnp.where(even, two, one), jnp.where(even, one, two)


def end_columns(nx, sources):
    n = sources[0][3].shape[0]
    j, k = iota((LANES, n), 0), iota((LANES, n), 1)
    row, side = j % 64 // 2, j % 2
    column = jnp.where(j < 64, jnp.where(side == 0, 0, 3), jnp.where(side == 0, 4, 5))
    out = None
    for x, start, count, message in sources:
        hit = (row >= x) & (row < x + count) & (k == column * nx + row - x + start)
        part = mm(one_hot(hit), message)
        out = part if out is None else out + part
    return out


def edge_columns(nx, sources):
    n = sources[0][3].shape[0]
    j, k = iota((LANES, n), 0), iota((LANES, n), 1)
    s, xx = j // 16, j % 16
    column = jnp.where(s == 0, 2, jnp.where(s == 1, 3, jnp.where(s == 5, 0, jnp.where(s == 6, 1, jnp.where(s == 3, 5, jnp.where(s == 7, 4, -1))))))
    out = None
    for low, high, start, message in sources:
        hit = (column >= 0) & (xx >= low) & (xx < high) & (k == column * nx + xx - low + start)
        part = mm(one_hot(hit), message)
        out = part if out is None else out + part
    return out


def conv_inside(t_ref, field, out, nx):
    n, m = nx * LANES, (nx - 1) * LANES
    out[...] = mm(t_ref[1], field[:, 0:n])
    out[:, LANES:] = out[:, LANES:] + mm(t_ref[0], field[:, 0:m])
    out[:, 0:m] = out[:, 0:m] + mm(t_ref[2], field[:, LANES:n])


def gate(hidden_grad, preact, q):
    return (hidden_grad * q * (1.0 + preact * (1.0 - q))).astype(BF)


def tap_terms(upstream, taps, ch, ny):
    columns = [jnp.zeros((ch, LANES), F32) for _ in range(TERMS // LANES)]
    for a in range(3):
        for c in range(3):
            product = mm_nt(*((taps(2 - a, 2 - c), upstream) if upstream is not None else taps(a, c)))
            place_taps(columns, fold_taps(product, ch, ny), a, c, ch)
    return columns


def with_bias(columns, field, ch, ny):
    lane = iota((ch, LANES), 1)
    return columns[:-1] + [jnp.where(lane == 27 * ch % LANES, bias_terms(field, ch, ny), columns[-1])]


def inner_kernel(
    nx, ch, ny,
    t1_ref, tv_ref, f_ref, g_ref, near_ref, bias_ref,
    fs, gs, pre, grad, hid_ref, second_ref, first_ref,
):
    rows = ch * ny
    ends = end_columns(nx, ((0, 0, nx, near_ref[...]),)).T
    for src, dst, first in ((f_ref, fs, 0), (g_ref, gs, 64)):
        for x in range(nx):
            block = src[:, x * LANES : (x + 1) * LANES]
            shifted_rows(dst, x, block, lane_to(ends, first + 2 * x + 1, 0), rows)
    conv_inside(t1_ref, fs, pre, nx)
    pre[...] = pre[...] + bias_column(bias_ref, ny)
    conv_inside(tv_ref, gs, grad, nx)
    n = (nx - 2) * LANES
    inside = slice(LANES, LANES + n)
    preact = pre[:, inside]
    q = logistic(preact)
    hid_ref[...] = (preact * q).astype(BF)
    preact_grad = gate(grad[:, inside], preact, q)
    window = lambda ref, a, c: ref[c * rows : (c + 1) * rows, a * LANES : a * LANES + n]
    second = tap_terms(hid_ref[...], lambda a, c: window(gs, a, c), ch, ny)
    first = tap_terms(None, lambda a, c: (preact_grad, window(fs, a, c)), ch, ny)
    second = with_bias(second, g_ref[...], ch, ny)
    first = with_bias(first, preact_grad, ch, ny)
    for i in range(TERMS // LANES):
        at = slice(i * LANES, (i + 1) * LANES)
        second_ref[:, at] = second[i]
        first_ref[:, at] = first[i]


def inner(t1, tv, field, cot, near, bias, ch, ny):
    rows = ch * ny
    nx = field.shape[1] // LANES
    sds = pltpu.VMEM
    return pl.pallas_call(
        functools.partial(inner_kernel, nx, ch, ny),
        out_shape=(
            sds((3 * rows, nx * LANES), BF),
            sds((3 * rows, nx * LANES), BF),
            sds((rows, nx * LANES), F32),
            sds((rows, nx * LANES), F32),
            sds((rows, (nx - 2) * LANES), BF),
            sds((ch, TERMS), F32),
            sds((ch, TERMS), F32),
        ),
        compiler_params=params(6),
        cost_estimate=pl.CostEstimate(flops=1000, bytes_accessed=1000, transcendentals=0),
        name="inner",
    )(*in_vmem(t1, tv, field, cot, near, bias))


def corners_kernel(nx, one_ref, two_ref, columns_ref):
    before, after = sides(one_ref[...], two_ref[...])
    columns_ref[...] = end_columns(nx, ((0, nx - 1, 1, before), (1, 0, 1, after))).T


def corners(one, two, nx):
    return pl.pallas_call(
        functools.partial(corners_kernel, nx),
        out_shape=pltpu.VMEM((one.shape[1], LANES), F32),
        compiler_params=params(1),
        name="corners",
    )(*in_vmem(one, two))


def outer_kernel(
    nx, ch, ny, scale,
    t1_ref, tv_ref, fs, gs, pre, grad, part_second_ref, part_first_ref, above_ref, below_ref, columns_ref,
    hid_ref, fe, keep_ref, give_ref,
    ge,
):
    rows = ch * ny
    columns = columns_ref[...]
    for i, dst in enumerate((fe, ge)):
        for j, src in enumerate((above_ref, below_ref)):
            block = src[(i + 1) * rows : (i + 2) * rows]
            shifted_rows(dst, j, block, lane_to(columns, 64 * i + 2 * j + 1, 0), rows)

    last = (nx - 1) * LANES
    ends = lambda ref: jnp.concatenate([ref[:, 0:LANES], ref[:, last:]], axis=1)
    both = lambda t, e: jnp.concatenate([mm(t[0], e[:, 0:LANES]), mm(t[2], e[:, LANES:])], axis=1)
    preact = ends(pre) + both(t1_ref, fe)
    q = logistic(preact)
    hid_ref[...] = (preact * q).astype(BF)
    preact_grad = gate(ends(grad) + both(tv_ref, ge), preact, q)

    def window(own, end, a, c):
        at = slice(c * rows, (c + 1) * rows)
        head = end[at, 0:LANES] if a == 0 else own[at, (a - 1) * LANES : a * LANES]
        tail = end[at, LANES:] if a == 2 else own[at, last + (a - 1) * LANES : last + a * LANES]
        return jnp.concatenate([head, tail], axis=1)

    second = tap_terms(hid_ref[...], lambda a, c: window(gs, ge, a, c), ch, ny)
    first = tap_terms(None, lambda a, c: (preact_grad, window(fs, fe, a, c)), ch, ny)
    first = with_bias(first, preact_grad, ch, ny)
    mine = is_even("smp")
    for i in range(TERMS // LANES):
        at = slice(i * LANES, (i + 1) * LANES)
        part_second = (second[i] + part_second_ref[:, at]) * scale
        part_first = (first[i] + part_first_ref[:, at]) * scale
        keep_ref[:, at] = jnp.where(mine, part_second, part_first)
        give_ref[:, at] = jnp.where(mine, part_first, part_second)


def outer(t1, tv, fs, gs, pre, grad, second, first, above, below, columns, ch, ny, scale):
    rows = ch * ny
    nx = fs.shape[1] // LANES
    sds = pltpu.VMEM
    return pl.pallas_call(
        functools.partial(outer_kernel, nx, ch, ny, scale),
        out_shape=(
            sds((rows, 2 * LANES), BF),
            sds((3 * rows, 2 * LANES), BF),
            sds((ch, TERMS), F32),
            sds((ch, TERMS), F32),
        ),
        scratch_shapes=[pltpu.VMEM((3 * rows, 2 * LANES), BF)],
        compiler_params=params(6),
        name="outer",
    )(*in_vmem(t1, tv, fs, gs, pre, grad, second, first, above, below, columns))


def rim_kernel(
    nx, ch, ny,
    t1_ref, h_ref, h_end_ref, fs_ref, fe_ref, f_ref, above_ref, below_ref, near_ref, corner_one_ref, corner_two_ref, bias_ref,
    hs,
    ends,
):
    rows = ch * ny
    above, below = above_ref[0:rows], below_ref[0:rows]
    before, after = sides(corner_one_ref[...], corner_two_ref[...])
    sources = ((2, nx + 2, 0, near_ref[...]), (0, 2, nx - 2, before), (nx + 2, nx + 4, 0, after))
    edges_t = edge_columns(nx, sources)
    end = fe_ref[rows : 2 * rows]
    unshifted = [above, end[:, 0:LANES], *(f_ref[:, x * LANES : (x + 1) * LANES] for x in range(nx)), end[:, LANES:], below]
    j, k = iota((LANES, LANES), 0), iota((LANES, LANES), 1)
    own_end = jnp.where(j // 16 == 2, 0, jnp.where(j // 16 == 4, LANES - 1, -1))
    for x in range(nx + 4):
        edges_t = edges_t + mm_nt(one_hot((j % 16 == x) & (k == own_end)), unshifted[x])
    edges = edges_t.T
    lane = iota((rows, LANES), 1)
    both = lambda left, right: jnp.where(lane == 0, lane_to(edges, left, 0), lane_to(edges, right, LANES - 1))
    shifted_rows(ends, 0, above, both(16, 80), rows)
    shifted_rows(ends, 1, below, both(16 + nx + 3, 80 + nx + 3), rows)
    acc = None
    row = lambda x: fs_ref[:, x * LANES : (x + 1) * LANES]
    pairs = ((ends[:, 0:LANES], row(nx - 1)), (fe_ref[:, 0:LANES], fe_ref[:, LANES:]), (row(0), ends[:, LANES:]))
    for a in range(3):
        columns = [lane_to(edges, 16 * c + a, 0).astype(BF) for c in range(3)]
        term = mm(t1_ref[a], jnp.concatenate([*pairs[a], jnp.concatenate(columns, axis=0)], axis=1))
        acc = term if acc is None else acc + term
    preact = acc + bias_column(bias_ref, ny)
    hidden = (preact * logistic(preact)).astype(BF)
    outer = hidden[:, 2 * LANES :].astype(F32)
    for x in range(nx + 2):
        if x == 0:
            block = hidden[:, 0:LANES]
        elif x == nx + 1:
            block = hidden[:, LANES : 2 * LANES]
        elif x == 1:
            block = h_end_ref[:, 0:LANES]
        elif x == nx:
            block = h_end_ref[:, LANES:]
        else:
            block = h_ref[:, (x - 2) * LANES : (x - 1) * LANES]
        shifted_rows(hs, x, block, jnp.where(lane == 0, lane_to(outer, x, 0), lane_to(outer, 64 + x, LANES - 1)), rows)


def rim(t1, hidden, hidden_end, fs, fe, field, above, below, near, corner_one, corner_two, bias, ch, ny):
    rows = ch * ny
    nx = field.shape[1] // LANES
    return pl.pallas_call(
        functools.partial(rim_kernel, nx, ch, ny),
        out_shape=pltpu.VMEM((3 * rows, (nx + 2) * LANES), BF),
        scratch_shapes=[pltpu.VMEM((3 * rows, 2 * LANES), BF)],
        compiler_params=params(6),
        cost_estimate=pl.CostEstimate(flops=1_000_000_000, bytes_accessed=3_000_000, transcendentals=0),
        name="rim",
    )(*in_vmem(t1, hidden, hidden_end, fs, fe, field, above, below, near, corner_one, corner_two, bias))


def residual_kernel(nx, ch, ny, t2_ref, hs, f_ref, bias_ref, o_ref):
    rows = ch * ny
    n = nx * LANES
    acc = mm(t2_ref[0], hs[:, 0:n])
    for a in range(1, 3):
        acc = acc + mm(t2_ref[a], hs[:, a * LANES : a * LANES + n])
    total = (f_ref[...].astype(F32) + (acc + bias_column(bias_ref, ny))).astype(BF)
    r, k = iota((rows, rows), 0), iota((rows, rows), 1)
    back = one_hot(k == (r % ny) * ch + r // ny)
    ordered = mm(back, total)
    for x in range(nx):
        o_ref[0, :, x] = ordered[:, x * LANES : (x + 1) * LANES].reshape(ch, ny, LANES).astype(BF)


def residual(t2, hs, field, bias, ch, ny):
    nx = field.shape[1] // LANES
    return pl.pallas_call(
        functools.partial(residual_kernel, nx, ch, ny),
        out_shape=jax.ShapeDtypeStruct((1, ch, nx, ny, LANES), BF),
        compiler_params=params(6),
        cost_estimate=pl.CostEstimate(flops=3_000_000_000, bytes_accessed=3_000_000, transcendentals=0),
        name="residual",
    )(*in_vmem(t2, hs, field, bias))


def moved(array, sizes, step):
    ns, nx, nz = sizes
    pairs = []
    for s in range(ns):
        for x in range(nx):
            for z in range(nz):
                t, u, v = step(s, x, z)
                pairs.append(((s * nx + x) * nz + z, (t * nx + u) * nz + v))
    return lax.ppermute(array, AXES, pairs)


def diagonal(array, sizes, turn):
    ns, nx, nz = sizes
    return moved(array, sizes, lambda s, x, z: (s, (x + (1 if x % 2 == turn else -1)) % nx, (z + 1) % nz))


def along(array, sizes, dx, dz=0):
    ns, nx, nz = sizes
    return moved(array, sizes, lambda s, x, z: (s, (x + dx) % nx, (z + dz) % nz))


def swapped(array, sizes, bits):
    return moved(array, sizes, lambda s, x, z: (s ^ bits[0], x ^ bits[1], z ^ bits[2]))


def add_kernel(n_in, *refs):
    terms = [ref[...].astype(F32) for ref in refs[:n_in]]
    out = refs[n_in]
    while len(terms) > 1:
        terms = [terms[i] + terms[i + 1] for i in range(0, len(terms), 2)]
    total = terms[0]
    n = total.shape[1] - LANES
    out[:, :n] = total[:, :n].astype(out.dtype)
    tail = total[:, n:]
    lane = iota(tail.shape, 1)
    spare = 864 % LANES
    joined = tail + pltpu.roll(tail, LANES - 1, 1)
    if out.dtype == BF:
        low = joined - joined.astype(BF).astype(F32)
        tail = jnp.where(lane == spare + 1, pltpu.roll(low, 1, 1), tail)
    out[:, n:] = jnp.where(lane == spare, joined, tail).astype(out.dtype)


def add(terms, dtype):
    return pl.pallas_call(
        functools.partial(add_kernel, len(terms)),
        out_shape=pltpu.VMEM(terms[0].shape, dtype),
        compiler_params=params(1),
        name="add",
    )(*in_vmem(*terms))


def exchange(sent, sizes, pair):
    steps = [(0, 0, 0)]
    for bits in pair:
        steps = steps + [tuple(p ^ q for p, q in zip(bits, step)) for step in steps]
    return [sent] + [swapped(sent, sizes, step) for step in steps[1:]]


def sum_all(keep, give, sizes, hs, finish):
    near = (1, 0, 0)
    bits = [(0, 1 << i, 0) for i in range(sizes[1].bit_length() - 1)]
    flat = [(0, 0, 1 << i) for i in range(sizes[2].bit_length() - 1)]
    flat += [(1 << i, 0, 0) for i in range(1, sizes[0].bit_length() - 1)]
    groups = [flat[i : i + 2] for i in range(0, len(flat), 2)] + [bits[i : i + 2] for i in range(0, len(bits), 2)]
    terms = [keep, swapped(give, sizes, near)]
    output = None
    for i, group in enumerate(groups):
        terms = exchange(add(terms, BF), sizes, group)
        if i == 0:
            *terms, hs = lax.optimization_barrier((*terms, hs))
            output = finish(hs)
        elif i == 1:
            *terms, output = lax.optimization_barrier((*terms, output))
    mine = add(terms, F32)
    return mine, swapped(mine, sizes, near), output


def spread_kernel(ch, own, terms_ref, *refs):
    first, first_bias, second, second_bias, taps, bias, sems = refs[-7:]
    for tap in range(27):
        at = tap * ch
        block = terms_ref[:, at // LANES * LANES : (at // LANES + 1) * LANES]
        taps[tap // 9, tap // 3 % 3, tap % 3] = lane_to(block, at % LANES, 0)[:, :ch]
    tail = lane_to(terms_ref[:, TERMS - LANES :], 27 * ch % LANES, 0)[:, 0:1]
    r, k = iota((ch, LANES), 0), iota((ch, LANES), 1)
    bias[...] = jnp.sum(jnp.where(r == k, tail, 0.0), axis=0, keepdims=True)[:, :ch]

    def write(out, bias_out):
        copies = [pltpu.make_async_copy(taps, out, sems.at[0]), pltpu.make_async_copy(bias, bias_out, sems.at[1])]
        for copy in copies:
            copy.start()
        for copy in copies:
            copy.wait()

    to_second = is_even("smp") if own else ~is_even("smp")
    pl.when(to_second)(lambda: write(second, second_bias))
    pl.when(~to_second)(lambda: write(first, first_bias))


def spread(terms, ch, written=()):
    taps, bias = pltpu.HBM((3, 3, 3, ch, ch), F32), pltpu.HBM((1, ch), F32)
    anywhere = pl.BlockSpec(memory_space=pl.ANY)
    return pl.pallas_call(
        functools.partial(spread_kernel, ch, not written),
        out_shape=(taps, bias, taps, bias),
        in_specs=[pl.BlockSpec(memory_space=pltpu.VMEM)] + [anywhere] * len(written),
        out_specs=(anywhere,) * 4,
        input_output_aliases={1 + i: i for i in range(len(written))},
        scratch_shapes=[
            pltpu.VMEM((3, 3, 3, ch, ch), F32),
            pltpu.VMEM((1, ch), F32),
            pltpu.SemaphoreType.DMA((2,)),
        ],
        compiler_params=params(3),
        cost_estimate=pl.CostEstimate(flops=1_000_000_000, bytes_accessed=2_000_000, transcendentals=0),
        name="spread",
    )(*in_vmem(terms), *written)


def shards(sizes, features, first_weight, first_bias, second_weight, second_bias, cotangent):
    ns, ngx, ngz = sizes
    _, ch, nx, ny, nz = features.shape
    assert features.shape[0] == 1 and nz == LANES and ngz == 2 and ngx % 2 == 0
    assert not any(n & (n - 1) for n in sizes) and ns > 1
    scale = float((ns * nx * ngx * ny * nz * ngz) ** -0.5)
    up, down, held, weight1, weight2 = faces(features, cotangent, first_weight, second_weight)
    above, below = along(up, sizes, 1), along(down, sizes, -1)
    field, cot, edge = pack(held)
    near = swapped(edge, sizes, (0, 0, 1))
    t1, tv, t2, edge = bands(weight1, weight2, edge, ny)
    corner_two, corner_one = diagonal(edge, sizes, 1), diagonal(edge, sizes, 0)
    bias1, bias2 = first_bias.reshape(1, ch), second_bias.reshape(1, ch)
    fs, gs, pre, grad, hidden, second, first = inner(t1, tv, field, cot, near, bias1, ch, ny)
    columns = corners(corner_one, corner_two, nx)
    hidden_end, fe, keep, give = outer(
        t1, tv, fs, gs, pre, grad, second, first, above, below, columns, ch, ny, scale
    )
    hs = rim(t1, hidden, hidden_end, fs, fe, field, above, below, near, corner_one, corner_two, bias1, ch, ny)
    mine, other, output = sum_all(keep, give, sizes, hs, lambda hs: residual(t2, hs, field, bias2, ch, ny))
    first, first_bias, second, second_bias = spread(other, ch, spread(mine, ch))
    laid = lambda grad: jnp.transpose(grad, (3, 0, 1, 2, 4))
    return output, laid(first), first_bias.reshape(ch), laid(second), second_bias.reshape(ch)


def solution(mesh):
    sizes = tuple(mesh.shape[axis] for axis in AXES)
    split = P("smp", None, "gx", None, "gz")
    return jax.shard_map(
        functools.partial(shards, sizes),
        mesh=mesh,
        in_specs=(split, P(), P(), P(), P(), split),
        out_specs=(split, P(), P(), P(), P()),
        check_vma=False,
    )
```

```python
import functools

import jax
import jax.numpy as jnp
from jax import lax
from jax.experimental import pallas as pl
from jax.experimental.pallas import tpu as pltpu
from jax.sharding import PartitionSpec as P

AXES = ("smp", "gx", "gz")
BF = jnp.bfloat16
F32 = jnp.float32
LANES = 128
TERMS = 896


def mm(a, b):
    return lax.dot_general(a, b, (((1,), (0,)), ((), ())), preferred_element_type=F32)


def mm_nt(a, b):
    return lax.dot_general(a, b, (((1,), (1,)), ((), ())), preferred_element_type=F32)


def iota(shape, dim):
    return lax.broadcasted_iota(jnp.int32, shape, dim)


def one_hot(hit):
    return jnp.where(hit, 1.0, 0.0).astype(BF)


def params(mib=8):
    return pltpu.CompilerParams(vmem_limit_bytes=mib * 2**20)


def in_vmem(*arrays):
    return [pltpu.with_memory_space_constraint(array, pltpu.VMEM) for array in arrays]


def in_hbm(*arrays):
    return [pltpu.with_memory_space_constraint(array, pltpu.HBM) for array in arrays]


def is_even(axis):
    return lax.axis_index(axis) % 2 == 0


def ordered(ch, ny):
    r, k = iota((ch * ny, ch * ny), 0), iota((ch * ny, ch * ny), 1)
    return one_hot(k == (r % ch) * ny + r // ch)


def faces_kernel(nx, ch, ny, f_any, g_any, w1_any, w2_any, up_ref, dn_ref, held, w1_ref, w2_ref, raw, sems):
    rows = ch * ny
    wanted = ((0, nx - 2), (0, nx - 1), (1, nx - 1), (0, 1), (0, 0), (1, 0))
    others = [(i, x) for x in range(nx) for i in range(2) if (i, x) not in wanted]
    copies = {
        (i, x): pltpu.make_async_copy((f_any, g_any)[i].at[0, :, x], held.at[i, x], sems.at[i * nx + x])
        for i, x in (*wanted, *others)
    }
    weights = [pltpu.make_async_copy(src, dst, sems.at[2 * nx + i]) for i, (src, dst) in enumerate(((w1_any, w1_ref), (w2_any, w2_ref)))]
    for copy in (*copies.values(), *weights):
        copy.start()
    for j, (i, x) in enumerate(wanted):
        copies[i, x].wait()
        raw[:, j * LANES : (j + 1) * LANES] = held[i, x].astype(F32).reshape(rows, LANES).astype(BF)
    out = mm(ordered(ch, ny), raw[...]).astype(BF)
    for j in range(3):
        at = slice(j * rows, (j + 1) * rows)
        up_ref[at] = out[:, j * LANES : (j + 1) * LANES]
        dn_ref[at] = out[:, (j + 3) * LANES : (j + 4) * LANES]
    for key in others:
        copies[key].wait()
    for copy in weights:
        copy.wait()


def faces(features, cotangent, first_weight, second_weight):
    _, ch, nx, ny, _ = features.shape
    rows = ch * ny
    sds = pltpu.VMEM
    laid = lambda weight: jnp.transpose(weight, (1, 2, 3, 0, 4))
    return pl.pallas_call(
        functools.partial(faces_kernel, nx, ch, ny),
        out_shape=(
            sds((3 * rows, LANES), BF),
            sds((3 * rows, LANES), BF),
            sds((2, nx, ch, ny, LANES), BF),
            sds((3, 3, 3, ch, ch), BF),
            sds((3, 3, 3, ch, ch), BF),
        ),
        in_specs=[pl.BlockSpec(memory_space=pl.ANY)] * 4,
        scratch_shapes=[pltpu.VMEM((rows, 6 * LANES), BF), pltpu.SemaphoreType.DMA((2 * nx + 2,))],
        compiler_params=params(4),
        name="faces",
    )(*in_hbm(features, cotangent, laid(first_weight), laid(second_weight)))


def pack_kernel(nx, ch, ny, held, fo_ref, go_ref, edge_ref, raw):
    rows = ch * ny
    perm = ordered(ch, ny)
    for i, dst in enumerate((fo_ref, go_ref)):
        for x in range(nx):
            raw[:, x * LANES : (x + 1) * LANES] = held[i, x].astype(F32).reshape(rows, LANES).astype(BF)
        dst[...] = mm(perm, raw[...]).astype(BF)
    n = edge_ref.shape[0]
    j, m = iota((n, nx * LANES), 0), iota((n, nx * LANES), 1)
    c, x = j // nx, j % nx
    zf = jnp.where(c < 2, c, LANES - 4 + c)
    pick_f = one_hot((c < 4) & (m == x * LANES + zf))
    zg = jnp.where(c == 4, 0, LANES - 1)
    pick_g = one_hot((c >= 4) & (c < 6) & (m == x * LANES + zg))
    edge_ref[...] = (mm_nt(pick_f, fo_ref[...]) + mm_nt(pick_g, go_ref[...])).astype(BF)


def pack(held):
    _, nx, ch, ny, _ = held.shape
    rows = ch * ny
    edge_rows = -(-6 * nx // 32) * 32
    sds = pltpu.VMEM
    return pl.pallas_call(
        functools.partial(pack_kernel, nx, ch, ny),
        out_shape=(sds((rows, nx * LANES), BF), sds((rows, nx * LANES), BF), sds((edge_rows, rows), BF)),
        scratch_shapes=[pltpu.VMEM((rows, nx * LANES), BF)],
        compiler_params=params(4),
        cost_estimate=pl.CostEstimate(flops=500_000_000, bytes_accessed=1_000_000, transcendentals=0),
        name="pack",
    )(*in_vmem(held))


def bands_kernel(ny, w1_ref, w2_ref, edge_ref, t1_ref, tv_ref, t2_ref, copy_ref):
    copy_ref[...] = edge_ref[...]
    ch = w1_ref.shape[-1]
    rows = ny * ch
    lane = iota((ch, rows), 1)
    r, k = iota((ch, LANES), 0), iota((ch, LANES), 1)
    places = [one_hot(k == r + b * ch) for b in range(3)]

    def direct(ref):
        wide = None
        for b in range(3):
            part = mm(ref[:, b].reshape(9 * ch, ch), places[b])
            wide = part if wide is None else wide + part
        return [wide[i * ch : (i + 1) * ch] for i in range(9)]

    def flipped(ref):
        none = jnp.zeros((ch, ch), BF)
        stack = [ref[2 - a, 2 - b, 2 - c] if b < 3 else none for a in range(3) for c in range(3) for b in range(4)]
        wide = mm_nt(one_hot(r == k)[:, :ch], jnp.concatenate(stack, axis=0))
        return [wide[:, i * LANES : (i + 1) * LANES] for i in range(9)]

    rest = jnp.zeros((ch, rows - LANES), F32)
    for taps, out in ((direct(w1_ref), t1_ref), (flipped(w2_ref), tv_ref), (direct(w2_ref), t2_ref)):
        for i, tap in enumerate(taps):
            a, c = i // 3, i % 3
            wide = jnp.concatenate([tap, rest], axis=1)
            for y in range(ny):
                block = wide if y == 1 else pltpu.roll(wide, (ch * (y - 1)) % rows, 1)
                if y == 0:
                    block = jnp.where(lane >= rows - ch, 0.0, block)
                if y == ny - 1:
                    block = jnp.where(lane < ch, 0.0, block)
                out[a, y * ch : (y + 1) * ch, c * rows : (c + 1) * rows] = block.astype(BF)


def bands(first_weight, second_weight, edge, ny):
    ch = first_weight.shape[-1]
    rows = ch * ny
    return pl.pallas_call(
        functools.partial(bands_kernel, ny),
        out_shape=(pltpu.VMEM((3, rows, 3 * rows), BF),) * 3 + (pltpu.VMEM(edge.shape, BF),),
        compiler_params=params(3),
        cost_estimate=pl.CostEstimate(flops=1_000_000_000, bytes_accessed=4_000_000, transcendentals=0),
        name="bands",
    )(*in_vmem(first_weight, second_weight, edge))


def shifted_rows(out, row, block, ends, rows):
    lane = iota(block.shape, 1)
    at = slice(row * LANES, (row + 1) * LANES)
    wide = block.astype(F32)
    out[0:rows, at] = jnp.where(lane == 0, ends, pltpu.roll(wide, 1, 1)).astype(BF)
    out[rows : 2 * rows, at] = block
    out[2 * rows :, at] = jnp.where(lane == LANES - 1, ends, pltpu.roll(wide, LANES - 1, 1)).astype(BF)


def lane_to(edges, source, target):
    shift = (target - source) % LANES
    return edges if shift == 0 else pltpu.roll(edges, shift, 1)


def fold_taps(product, ch, ny):
    rows = ch * ny
    lane = iota((ch, LANES), 1)
    total = None
    for y in range(ny):
        low = max(ch * (y - 1), 0)
        high = min(ch * (y + 2), rows)
        band = product[y * ch : (y + 1) * ch]
        col = low // LANES
        turn = ch * (y - 1) % LANES
        part = lane_to(band[:, col * LANES : (col + 1) * LANES], turn, 0)
        if (high - 1) // LANES > col:
            rest = lane_to(band[:, (col + 1) * LANES : (col + 2) * LANES], turn, 0)
            part = jnp.where(lane < LANES - turn, part, rest)
        if y == 0:
            part = jnp.where(lane < ch, 0.0, part)
        if y == ny - 1:
            part = jnp.where(lane < 2 * ch, part, 0.0)
        total = part if total is None else total + part
    return total


def place_taps(columns, folded, a, c, ch):
    lane = iota(folded.shape, 1)
    for b in range(3):
        target = ch * ((a * 3 + b) * 3 + c)
        col, offset = target // LANES, target % LANES
        moved = lane_to(folded, b * ch, offset)
        columns[col] = jnp.where((lane >= offset) & (lane < offset + ch), moved, columns[col])


def bias_terms(field, ch, ny):
    nx = field.shape[1] // LANES
    wide = field.astype(F32)
    total = wide[:, 0:LANES]
    for x in range(1, nx):
        total = total + wide[:, x * LANES : (x + 1) * LANES]
    folded = total[0:ch]
    for y in range(1, ny):
        folded = folded + total[y * ch : (y + 1) * ch]
    return jnp.sum(folded, axis=1, keepdims=True)


def logistic(preact):
    return 1.0 / (1.0 + jnp.exp(-preact))


def bias_column(ref, ny):
    ch = ref.shape[1]
    r, k = iota((ch, ch), 0), iota((ch, ch), 1)
    column = jnp.sum(jnp.where(r == k, ref[...], 0.0), axis=1, keepdims=True)
    return jnp.concatenate([column] * ny, axis=0)


def sides(one, two):
    even = is_even("gx")
    return jnp.where(even, two, one), jnp.where(even, one, two)


def end_columns(nx, sources):
    n = sources[0][3].shape[0]
    j, k = iota((LANES, n), 0), iota((LANES, n), 1)
    row, side = j % 64 // 2, j % 2
    column = jnp.where(j < 64, jnp.where(side == 0, 0, 3), jnp.where(side == 0, 4, 5))
    out = None
    for x, start, count, message in sources:
        hit = (row >= x) & (row < x + count) & (k == column * nx + row - x + start)
        part = mm(one_hot(hit), message)
        out = part if out is None else out + part
    return out


def edge_columns(nx, sources):
    n = sources[0][3].shape[0]
    j, k = iota((LANES, n), 0), iota((LANES, n), 1)
    s, xx = j // 16, j % 16
    column = jnp.where(s == 0, 2, jnp.where(s == 1, 3, jnp.where(s == 5, 0, jnp.where(s == 6, 1, jnp.where(s == 3, 5, jnp.where(s == 7, 4, -1))))))
    out = None
    for low, high, start, message in sources:
        hit = (column >= 0) & (xx >= low) & (xx < high) & (k == column * nx + xx - low + start)
        part = mm(one_hot(hit), message)
        out = part if out is None else out + part
    return out


def conv_inside(t_ref, field, out, nx):
    n, m = nx * LANES, (nx - 1) * LANES
    out[...] = mm(t_ref[1], field[:, 0:n])
    out[:, LANES:] = out[:, LANES:] + mm(t_ref[0], field[:, 0:m])
    out[:, 0:m] = out[:, 0:m] + mm(t_ref[2], field[:, LANES:n])


def gate(hidden_grad, preact, q):
    return (hidden_grad * q * (1.0 + preact * (1.0 - q))).astype(BF)


def tap_terms(upstream, taps, ch, ny):
    columns = [jnp.zeros((ch, LANES), F32) for _ in range(TERMS // LANES)]
    for a in range(3):
        for c in range(3):
            product = mm_nt(*((taps(2 - a, 2 - c), upstream) if upstream is not None else taps(a, c)))
            place_taps(columns, fold_taps(product, ch, ny), a, c, ch)
    return columns


def with_bias(columns, field, ch, ny):
    lane = iota((ch, LANES), 1)
    return columns[:-1] + [jnp.where(lane == 27 * ch % LANES, bias_terms(field, ch, ny), columns[-1])]


def inner_kernel(
    nx, ch, ny,
    t1_ref, tv_ref, f_ref, g_ref, near_ref, bias_ref,
    fs, gs, pre, grad, hid_ref, second_ref, first_ref,
):
    rows = ch * ny
    ends = end_columns(nx, ((0, 0, nx, near_ref[...]),)).T
    for src, dst, first in ((f_ref, fs, 0), (g_ref, gs, 64)):
        for x in range(nx):
            block = src[:, x * LANES : (x + 1) * LANES]
            shifted_rows(dst, x, block, lane_to(ends, first + 2 * x + 1, 0), rows)
    conv_inside(t1_ref, fs, pre, nx)
    pre[...] = pre[...] + bias_column(bias_ref, ny)
    conv_inside(tv_ref, gs, grad, nx)
    n = (nx - 2) * LANES
    inside = slice(LANES, LANES + n)
    preact = pre[:, inside]
    q = logistic(preact)
    hid_ref[...] = (preact * q).astype(BF)
    preact_grad = gate(grad[:, inside], preact, q)
    window = lambda ref, a, c: ref[c * rows : (c + 1) * rows, a * LANES : a * LANES + n]
    second = tap_terms(hid_ref[...], lambda a, c: window(gs, a, c), ch, ny)
    first = tap_terms(None, lambda a, c: (preact_grad, window(fs, a, c)), ch, ny)
    second = with_bias(second, g_ref[...], ch, ny)
    first = with_bias(first, preact_grad, ch, ny)
    for i in range(TERMS // LANES):
        at = slice(i * LANES, (i + 1) * LANES)
        second_ref[:, at] = second[i]
        first_ref[:, at] = first[i]


def inner(t1, tv, field, cot, near, bias, ch, ny):
    rows = ch * ny
    nx = field.shape[1] // LANES
    sds = pltpu.VMEM
    return pl.pallas_call(
        functools.partial(inner_kernel, nx, ch, ny),
        out_shape=(
            sds((3 * rows, nx * LANES), BF),
            sds((3 * rows, nx * LANES), BF),
            sds((rows, nx * LANES), F32),
            sds((rows, nx * LANES), F32),
            sds((rows, (nx - 2) * LANES), BF),
            sds((ch, TERMS), F32),
            sds((ch, TERMS), F32),
        ),
        compiler_params=params(6),
        cost_estimate=pl.CostEstimate(flops=1000, bytes_accessed=1000, transcendentals=0),
        name="inner",
    )(*in_vmem(t1, tv, field, cot, near, bias))


def corners_kernel(nx, one_ref, two_ref, after_ref, columns_ref):
    before, after = sides(one_ref[...], two_ref[...])
    columns_ref[...] = end_columns(nx, ((0, nx - 1, 1, before), (1, 0, 1, after))).T


def corners(one, two, after, nx):
    return pl.pallas_call(
        functools.partial(corners_kernel, nx),
        out_shape=pltpu.VMEM((one.shape[1], LANES), F32),
        compiler_params=params(1),
        name="corners",
    )(*in_vmem(one, two, after))


def ahead_kernel(nx, t1_ref, tv_ref, pre, grad, above_ref, below_ref, pre_end, grad_end, fe, ge):
    rows = above_ref.shape[0] // 3
    last = (nx - 1) * LANES
    none = jnp.zeros((rows, LANES), F32)
    for i, (t, own, out, end) in enumerate(((t1_ref, pre, pre_end, fe), (tv_ref, grad, grad_end, ge))):
        for j, (src, at) in enumerate(((above_ref, 0), (below_ref, last))):
            shifted_rows(end, j, src[(i + 1) * rows : (i + 2) * rows], none, rows)
            block = slice(j * LANES, (j + 1) * LANES)
            out[:, block] = own[:, at : at + LANES] + mm(t[2 * j], end[:, block])


def ahead(t1, tv, pre, grad, above, below):
    rows = above.shape[0] // 3
    nx = pre.shape[1] // LANES
    sds = pltpu.VMEM
    sums, windows = sds((rows, 2 * LANES), F32), sds((3 * rows, 2 * LANES), BF)
    return pl.pallas_call(
        functools.partial(ahead_kernel, nx),
        out_shape=(sums, sums, windows, windows),
        compiler_params=params(2),
        cost_estimate=pl.CostEstimate(flops=1000, bytes_accessed=1000, transcendentals=0),
        name="ahead",
    )(*in_vmem(t1, tv, pre, grad, above, below))


def outer_kernel(
    nx, ch, ny, scale,
    t1_ref, tv_ref, fs, gs, pre_end, grad_end, fe_in, ge_in, part_second_ref, part_first_ref, columns_ref,
    hid_ref, fe, keep_ref, give_ref,
    ge,
):
    rows = ch * ny
    last = (nx - 1) * LANES
    columns = columns_ref[...]
    lane = iota((rows, LANES), 1)
    sums = []
    for i, (t, own, old, new) in enumerate(((t1_ref, pre_end, fe_in, fe), (tv_ref, grad_end, ge_in, ge))):
        parts = []
        for j in range(2):
            block = slice(j * LANES, (j + 1) * LANES)
            corner = lane_to(columns, 64 * i + 2 * j + 1, 0)
            part = own[:, block]
            for c, hit in ((0, lane == 0), (2, lane == LANES - 1)):
                at = slice(c * rows, (c + 1) * rows)
                window = old[at, block].astype(F32)
                new[at, block] = jnp.where(hit, corner, window).astype(BF)
                part = part + mm(t[2 * j, :, at], jnp.where(hit, corner, 0.0).astype(BF))
            new[rows : 2 * rows, block] = old[rows : 2 * rows, block]
            parts.append(part)
        sums.append(jnp.concatenate(parts, axis=1))
    preact, hidden_grad = sums
    q = logistic(preact)
    hid_ref[...] = (preact * q).astype(BF)
    preact_grad = gate(hidden_grad, preact, q)

    def window(own, end, a, c):
        at = slice(c * rows, (c + 1) * rows)
        head = end[at, 0:LANES] if a == 0 else own[at, (a - 1) * LANES : a * LANES]
        tail = end[at, LANES:] if a == 2 else own[at, last + (a - 1) * LANES : last + a * LANES]
        return jnp.concatenate([head, tail], axis=1)

    second = tap_terms(hid_ref[...], lambda a, c: window(gs, ge, a, c), ch, ny)
    first = tap_terms(None, lambda a, c: (preact_grad, window(fs, fe, a, c)), ch, ny)
    first = with_bias(first, preact_grad, ch, ny)
    mine = is_even("smp")
    for i in range(TERMS // LANES):
        at = slice(i * LANES, (i + 1) * LANES)
        part_second = (second[i] + part_second_ref[:, at]) * scale
        part_first = (first[i] + part_first_ref[:, at]) * scale
        keep_ref[:, at] = jnp.where(mine, part_second, part_first)
        give_ref[:, at] = jnp.where(mine, part_first, part_second)


def outer(t1, tv, fs, gs, pre_end, grad_end, fe, ge, second, first, columns, ch, ny, scale):
    rows = ch * ny
    nx = fs.shape[1] // LANES
    sds = pltpu.VMEM
    return pl.pallas_call(
        functools.partial(outer_kernel, nx, ch, ny, scale),
        out_shape=(
            sds((rows, 2 * LANES), BF),
            sds((3 * rows, 2 * LANES), BF),
            sds((ch, TERMS), F32),
            sds((ch, TERMS), F32),
        ),
        scratch_shapes=[pltpu.VMEM((3 * rows, 2 * LANES), BF)],
        compiler_params=params(6),
        name="outer",
    )(*in_vmem(t1, tv, fs, gs, pre_end, grad_end, fe, ge, second, first, columns))


def rim_kernel(
    nx, ch, ny,
    t1_ref, h_ref, h_end_ref, fs_ref, fe_ref, f_ref, above_ref, below_ref, near_ref, corner_one_ref, corner_two_ref, bias_ref,
    hs,
    ends,
):
    rows = ch * ny
    above, below = above_ref[0:rows], below_ref[0:rows]
    before, after = sides(corner_one_ref[...], corner_two_ref[...])
    sources = ((2, nx + 2, 0, near_ref[...]), (0, 2, nx - 2, before), (nx + 2, nx + 4, 0, after))
    edges_t = edge_columns(nx, sources)
    end = fe_ref[rows : 2 * rows]
    unshifted = [above, end[:, 0:LANES], *(f_ref[:, x * LANES : (x + 1) * LANES] for x in range(nx)), end[:, LANES:], below]
    j, k = iota((LANES, LANES), 0), iota((LANES, LANES), 1)
    own_end = jnp.where(j // 16 == 2, 0, jnp.where(j // 16 == 4, LANES - 1, -1))
    for x in range(nx + 4):
        edges_t = edges_t + mm_nt(one_hot((j % 16 == x) & (k == own_end)), unshifted[x])
    edges = edges_t.T
    lane = iota((rows, LANES), 1)
    both = lambda left, right: jnp.where(lane == 0, lane_to(edges, left, 0), lane_to(edges, right, LANES - 1))
    shifted_rows(ends, 0, above, both(16, 80), rows)
    shifted_rows(ends, 1, below, both(16 + nx + 3, 80 + nx + 3), rows)
    acc = None
    row = lambda x: fs_ref[:, x * LANES : (x + 1) * LANES]
    pairs = ((ends[:, 0:LANES], row(nx - 1)), (fe_ref[:, 0:LANES], fe_ref[:, LANES:]), (row(0), ends[:, LANES:]))
    for a in range(3):
        columns = [lane_to(edges, 16 * c + a, 0).astype(BF) for c in range(3)]
        term = mm(t1_ref[a], jnp.concatenate([*pairs[a], jnp.concatenate(columns, axis=0)], axis=1))
        acc = term if acc is None else acc + term
    preact = acc + bias_column(bias_ref, ny)
    hidden = (preact * logistic(preact)).astype(BF)
    outer = hidden[:, 2 * LANES :].astype(F32)
    for x in range(nx + 2):
        if x == 0:
            block = hidden[:, 0:LANES]
        elif x == nx + 1:
            block = hidden[:, LANES : 2 * LANES]
        elif x == 1:
            block = h_end_ref[:, 0:LANES]
        elif x == nx:
            block = h_end_ref[:, LANES:]
        else:
            block = h_ref[:, (x - 2) * LANES : (x - 1) * LANES]
        shifted_rows(hs, x, block, jnp.where(lane == 0, lane_to(outer, x, 0), lane_to(outer, 64 + x, LANES - 1)), rows)


def rim(t1, hidden, hidden_end, fs, fe, field, above, below, near, corner_one, corner_two, bias, ch, ny):
    rows = ch * ny
    nx = field.shape[1] // LANES
    return pl.pallas_call(
        functools.partial(rim_kernel, nx, ch, ny),
        out_shape=pltpu.VMEM((3 * rows, (nx + 2) * LANES), BF),
        scratch_shapes=[pltpu.VMEM((3 * rows, 2 * LANES), BF)],
        compiler_params=params(6),
        cost_estimate=pl.CostEstimate(flops=1_000_000_000, bytes_accessed=3_000_000, transcendentals=0),
        name="rim",
    )(*in_vmem(t1, hidden, hidden_end, fs, fe, field, above, below, near, corner_one, corner_two, bias))


def residual_kernel(nx, ch, ny, t2_ref, hs, f_ref, bias_ref, o_ref):
    rows = ch * ny
    n = nx * LANES
    acc = mm(t2_ref[0], hs[:, 0:n])
    for a in range(1, 3):
        acc = acc + mm(t2_ref[a], hs[:, a * LANES : a * LANES + n])
    total = (f_ref[...].astype(F32) + (acc + bias_column(bias_ref, ny))).astype(BF)
    r, k = iota((rows, rows), 0), iota((rows, rows), 1)
    back = one_hot(k == (r % ny) * ch + r // ny)
    ordered = mm(back, total)
    for x in range(nx):
        o_ref[0, :, x] = ordered[:, x * LANES : (x + 1) * LANES].reshape(ch, ny, LANES).astype(BF)


def residual(t2, hs, field, bias, ch, ny):
    nx = field.shape[1] // LANES
    return pl.pallas_call(
        functools.partial(residual_kernel, nx, ch, ny),
        out_shape=jax.ShapeDtypeStruct((1, ch, nx, ny, LANES), BF),
        compiler_params=params(6),
        cost_estimate=pl.CostEstimate(flops=3_000_000_000, bytes_accessed=3_000_000, transcendentals=0),
        name="residual",
    )(*in_vmem(t2, hs, field, bias))


def moved(array, sizes, step):
    ns, nx, nz = sizes
    pairs = []
    for s in range(ns):
        for x in range(nx):
            for z in range(nz):
                t, u, v = step(s, x, z)
                pairs.append(((s * nx + x) * nz + z, (t * nx + u) * nz + v))
    return lax.ppermute(array, AXES, pairs)


def diagonal(array, sizes, turn):
    ns, nx, nz = sizes
    return moved(array, sizes, lambda s, x, z: (s, (x + (1 if x % 2 == turn else -1)) % nx, (z + 1) % nz))


def along(array, sizes, dx, dz=0):
    ns, nx, nz = sizes
    return moved(array, sizes, lambda s, x, z: (s, (x + dx) % nx, (z + dz) % nz))


def swapped(array, sizes, bits):
    return moved(array, sizes, lambda s, x, z: (s ^ bits[0], x ^ bits[1], z ^ bits[2]))


def add_kernel(n_in, *refs):
    terms = [ref[...].astype(F32) for ref in refs[:n_in]]
    out = refs[n_in]
    while len(terms) > 1:
        terms = [terms[i] + terms[i + 1] for i in range(0, len(terms), 2)]
    total = terms[0]
    n = total.shape[1] - LANES
    out[:, :n] = total[:, :n].astype(out.dtype)
    tail = total[:, n:]
    lane = iota(tail.shape, 1)
    spare = 864 % LANES
    joined = tail + pltpu.roll(tail, LANES - 1, 1)
    if out.dtype == BF:
        low = joined - joined.astype(BF).astype(F32)
        tail = jnp.where(lane == spare + 1, pltpu.roll(low, 1, 1), tail)
    out[:, n:] = jnp.where(lane == spare, joined, tail).astype(out.dtype)


def add(terms, dtype):
    return pl.pallas_call(
        functools.partial(add_kernel, len(terms)),
        out_shape=pltpu.VMEM(terms[0].shape, dtype),
        compiler_params=params(1),
        name="add",
    )(*in_vmem(*terms))


def exchange(sent, sizes, pair, far_first):
    steps = [(0, 0, 0)]
    for bits in pair:
        steps = steps + [tuple(p ^ q for p, q in zip(bits, step)) for step in steps]
    order = steps[:0:-1] if far_first else steps[2:] + steps[1:2]
    return [sent] + [swapped(sent, sizes, step) for step in order]


def sum_all(keep, give, sizes, hs, finish):
    near = (1, 0, 0)
    bits = [(0, 1 << i, 0) for i in range(sizes[1].bit_length() - 1)]
    flat = [(0, 0, 1 << i) for i in range(sizes[2].bit_length() - 1)]
    flat += [(1 << i, 0, 0) for i in range(1, sizes[0].bit_length() - 1)]
    groups = [flat[i : i + 2] for i in range(0, len(flat), 2)] + [bits[i : i + 2] for i in range(0, len(bits), 2)]
    terms = [keep, swapped(give, sizes, near)]
    output = None
    for i, group in enumerate(groups):
        terms = exchange(add(terms, BF), sizes, group, i == 0)
        if i == 0:
            *terms, hs = lax.optimization_barrier((*terms, hs))
            output = finish(hs)
        elif i == 1:
            *terms, output = lax.optimization_barrier((*terms, output))
    mine = add(terms, F32)
    return mine, swapped(mine, sizes, near), output


def spread_kernel(ch, own, terms_ref, *refs):
    first, first_bias, second, second_bias, taps, bias, sems = refs[-7:]
    for tap in range(27):
        at = tap * ch
        block = terms_ref[:, at // LANES * LANES : (at // LANES + 1) * LANES]
        taps[tap // 9, tap // 3 % 3, tap % 3] = lane_to(block, at % LANES, 0)[:, :ch]
    tail = lane_to(terms_ref[:, TERMS - LANES :], 27 * ch % LANES, 0)[:, 0:1]
    r, k = iota((ch, LANES), 0), iota((ch, LANES), 1)
    bias[...] = jnp.sum(jnp.where(r == k, tail, 0.0), axis=0, keepdims=True)[:, :ch]

    def write(out, bias_out):
        copies = [pltpu.make_async_copy(taps, out, sems.at[0]), pltpu.make_async_copy(bias, bias_out, sems.at[1])]
        for copy in copies:
            copy.start()
        for copy in copies:
            copy.wait()

    to_second = is_even("smp") if own else ~is_even("smp")
    pl.when(to_second)(lambda: write(second, second_bias))
    pl.when(~to_second)(lambda: write(first, first_bias))


def spread(terms, ch, written=()):
    taps, bias = pltpu.HBM((3, 3, 3, ch, ch), F32), pltpu.HBM((1, ch), F32)
    anywhere = pl.BlockSpec(memory_space=pl.ANY)
    return pl.pallas_call(
        functools.partial(spread_kernel, ch, not written),
        out_shape=(taps, bias, taps, bias),
        in_specs=[pl.BlockSpec(memory_space=pltpu.VMEM)] + [anywhere] * len(written),
        out_specs=(anywhere,) * 4,
        input_output_aliases={1 + i: i for i in range(len(written))},
        scratch_shapes=[
            pltpu.VMEM((3, 3, 3, ch, ch), F32),
            pltpu.VMEM((1, ch), F32),
            pltpu.SemaphoreType.DMA((2,)),
        ],
        compiler_params=params(3),
        cost_estimate=pl.CostEstimate(flops=1_000_000_000, bytes_accessed=2_000_000, transcendentals=0),
        name="spread",
    )(*in_vmem(terms), *written)


def shards(sizes, features, first_weight, first_bias, second_weight, second_bias, cotangent):
    ns, ngx, ngz = sizes
    _, ch, nx, ny, nz = features.shape
    assert features.shape[0] == 1 and nz == LANES and ngz == 2 and ngx % 2 == 0
    assert not any(n & (n - 1) for n in sizes) and ns > 1
    scale = float((ns * nx * ngx * ny * nz * ngz) ** -0.5)
    up, down, held, weight1, weight2 = faces(features, cotangent, first_weight, second_weight)
    above, below = along(up, sizes, 1), along(down, sizes, -1)
    field, cot, edge = pack(held)
    near = swapped(edge, sizes, (0, 0, 1))
    t1, tv, t2, edge = bands(weight1, weight2, edge, ny)
    corner_two, corner_one = diagonal(edge, sizes, 1), diagonal(edge, sizes, 0)
    bias1, bias2 = first_bias.reshape(1, ch), second_bias.reshape(1, ch)
    fs, gs, pre, grad, hidden, second, first = inner(t1, tv, field, cot, near, bias1, ch, ny)
    pre_end, grad_end, fe, ge = ahead(t1, tv, pre, grad, above, below)
    columns = corners(corner_one, corner_two, pre_end, nx)
    hidden_end, fe, keep, give = outer(
        t1, tv, fs, gs, pre_end, grad_end, fe, ge, second, first, columns, ch, ny, scale
    )
    hs = rim(t1, hidden, hidden_end, fs, fe, field, above, below, near, corner_one, corner_two, bias1, ch, ny)
    mine, other, output = sum_all(keep, give, sizes, hs, lambda hs: residual(t2, hs, field, bias2, ch, ny))
    first, first_bias, second, second_bias = spread(other, ch, spread(mine, ch))
    laid = lambda grad: jnp.transpose(grad, (3, 0, 1, 2, 4))
    return output, laid(first), first_bias.reshape(ch), laid(second), second_bias.reshape(ch)


def solution(mesh):
    sizes = tuple(mesh.shape[axis] for axis in AXES)
    split = P("smp", None, "gx", None, "gz")
    return jax.shard_map(
        functools.partial(shards, sizes),
        mesh=mesh,
        in_specs=(split, P(), P(), P(), P(), split),
        out_specs=(split, P(), P(), P(), P()),
        check_vma=False,
    )
```
